32 devices in a mesh: cell: 4 (over y, x), snap: 8 (over z, core).
Axes of the slice: x: 2, y: 2, z: 4, core: 2. Of those that a mesh axis runs over, the one named last changes fastest.
Arguments:
- snapshots: float32 [4096, 2048], P('cell', 'snap'), as said below
- sketch: float32 [2048, 256], P('snap'), may hold values from -6 to 6
Outputs:
- q_basis: float32 [4096, 256], P(('cell', 'snap'))
- z_sketch: float32 [2048, 256], P('snap')
- column_scales: float32 [5, 256], replicated
The draws below stay inside these ranges and needn't reach their ends.
Inputs may be any that keep to these rules, and one draw needn't show every extreme that they name: `snapshots`: finite values with row and column scales of varying size.
All inputs are finite; a program needn't handle non-finite values.
Results may differ from the reference program's by a relative error of at most 0.0003.
Values sent between devices are 32-bit elements; how exact they have to be, the bound alone decides.
No kernel may reach another device: no remote copies, remote signals or barrier semaphores. Data moves between devices by JAX's collectives and lax.ppermute only.
A program may use at most 64 MiB of HBM per device.

```python
import math
import jax
import jax.numpy as jnp
from jax import lax

K = 256
ITERS = 2
CELLS = 4096
SNAPS = 2048


def draw_snapshots(key, part):
    key = jax.random.fold_in(key, 1)
    key_rows, key_cols, key_base = jax.random.split(key, 3)
    ramp_rows = jnp.exp(jnp.arange(CELLS, dtype=jnp.float32) / CELLS * math.log(3.0))
    ramp_cols = jnp.exp(jnp.arange(SNAPS, dtype=jnp.float32) / SNAPS * math.log(3.0))
    row_scale = jnp.exp(jax.random.uniform(key_rows, (CELLS,), jnp.float32) * math.log(10.0)) * ramp_rows
    col_scale = jnp.exp(jax.random.uniform(key_cols, (SNAPS,), jnp.float32) * math.log(10.0)) * ramp_cols
    base = jax.random.normal(key_base, (CELLS, SNAPS), jnp.float32)
    return base * row_scale[:, None] * col_scale[None, :] / math.sqrt(SNAPS)


def shard_levels(own_key, dims, pieces, least, top_value):
    def one(dim, parts):
        heights = jax.random.uniform(jax.random.fold_in(jax.random.fold_in(own_key, 6), dim), (parts,), jnp.float32, least / len(pieces), top_value / len(pieces))
        return jnp.repeat(jnp.exp(heights), dims[dim] // parts).reshape((-1,) + (1,) * (len(dims) - dim - 1))

    factor_of = one(*pieces[0])
    for cut in pieces[1:]:
        factor_of = factor_of * one(*cut)
    return factor_of


def noise(rng, extent, scale, bound, shards=(), kind=jnp.bfloat16):
    array = jax.random.normal(rng, extent, jnp.float32) * scale
    if len(shards) > 0:
        array = shard_levels(rng, extent, shards, -0.22, 0.18) * array
    return jnp.clip(array, min=-bound, max=bound).astype(kind)


def setup_inputs(seed: int = 0) -> dict:
    streams_of = jax.random.split(jax.random.key(seed), 3)
    return {
        "snapshots": draw_snapshots(jax.random.fold_in(streams_of[2], 71), 0),
        "sketch": noise(streams_of[1], (SNAPS, K), 1.0, 6.0, ((0, 8),), jnp.float32),
    }


def column_scale(matrix, count):
    return jnp.sqrt(lax.optimization_barrier(jnp.sum(matrix * matrix, axis=0)) / count + 1e-05)

def reference(snapshots, sketch):
    cells = snapshots.shape[0]
    snaps = snapshots.shape[1]
    high = lax.Precision.HIGHEST
    y_full = jnp.dot(snapshots, sketch, precision=high, preferred_element_type=jnp.float32)
    scale_y = column_scale(y_full, cells)
    q_full = y_full / scale_y
    scales = [scale_y]
    z_full = jnp.zeros((snaps, sketch.shape[1]), jnp.float32)
    for section_index in range(ITERS):
        z_part = jnp.dot(snapshots.T, q_full, precision=high, preferred_element_type=jnp.float32)
        scale_z = column_scale(z_part, snaps)
        z_full = z_part / scale_z
        y_full = jnp.dot(snapshots, z_full, precision=high, preferred_element_type=jnp.float32)
        scale_y = column_scale(y_full, cells)
        q_full = y_full / scale_y
        scales.append(scale_z)
        scales.append(scale_y)
    return (q_full, z_full, jnp.stack(scales))
```

```python
import jax
import jax.numpy as jnp
from jax import lax
from jax.sharding import PartitionSpec as P

ITERS = 2
EPS = 1e-05
TILE = 8
DIRECT = 8


def local(snapshots, sketch):
    groups = lax.axis_size("cell")
    places = lax.axis_size("snap")
    chips = places // 2
    rows, width = snapshots.shape
    rank = sketch.shape[1]
    half = rank // 2
    chunk = rows // chips
    all_cells = rows * groups
    all_snaps = width * places
    place = lax.axis_index("snap")
    core = place % 2
    chip = place // 2
    same_core = [[2 * z + k for z in range(chips)] for k in range(2)]
    swap = [(i, i ^ 1) for i in range(places)]

    def swap_core(x):
        return lax.ppermute(x, "snap", swap)

    def exchange_z(x):
        return lax.all_to_all(x, "snap", 0, 0, axis_index_groups=same_core, tiled=True)

    def exchange_cell(x):
        return lax.all_to_all(x, "cell", 0, 0, tiled=True)

    def scatter_sum(y, extra):
        if chips > DIRECT:
            mine = lax.psum_scatter(y, "snap", scatter_dimension=0, axis_index_groups=same_core, tiled=True)
            return mine, lax.psum(extra, "snap", axis_index_groups=same_core)
        pieces = y.reshape(chips, chunk, half)
        extras = jnp.broadcast_to(extra, (chips,) + extra.shape)
        got = exchange_z(jnp.concatenate([pieces, extras], axis=1))
        total = jnp.sum(got, axis=0)
        return total[:chunk], total[chunk:]

    def gather_rows(part, extra):
        if chips > DIRECT:
            full = lax.all_gather(part, "snap", axis=0, axis_index_groups=same_core, tiled=True)
            return full, lax.psum(extra, "snap", axis_index_groups=same_core)
        sent = jnp.concatenate([part, extra], axis=0)
        got = exchange_z(jnp.broadcast_to(sent, (chips,) + sent.shape))
        return got[:, :chunk].reshape(rows, half), jnp.sum(got[:, chunk:], axis=0)

    def cell_sum(z, extra):
        if groups != 4:
            return lax.psum(z, "cell"), lax.psum(extra, "cell")
        part = z.shape[0] // groups
        pieces = z.reshape(groups, part, half)
        extras = jnp.broadcast_to(extra, (groups,) + extra.shape)
        mine = jnp.sum(exchange_cell(jnp.concatenate([pieces, extras], axis=1)), axis=0)
        got = exchange_cell(jnp.broadcast_to(mine[:part], (groups, part, half)))
        return got.reshape(z.shape), mine[part:]

    def dot(a, b, contract):
        return lax.dot_general(
            a, b, (((contract,), (0,)), ((), ())), precision=lax.Precision.HIGH, preferred_element_type=jnp.float32
        )

    def squares(x):
        return jnp.broadcast_to(jnp.sum(x * x, axis=0, keepdims=True), (TILE, half))

    def rms(total, count):
        return jnp.sqrt(total[0:1] / count + EPS)

    other = swap_core(snapshots)
    split = sketch.reshape(width, 2, half)
    z_own = lax.dynamic_index_in_dim(split, core, 1, keepdims=False)
    z_other = swap_core(lax.dynamic_index_in_dim(split, 1 - core, 1, keepdims=False))
    z_extra = jnp.zeros((TILE, half), jnp.float32)

    scales = []
    for section in range(ITERS + 1):
        partial = dot(snapshots, z_own, 1) + dot(other, z_other, 1)
        y, z_total = scatter_sum(partial, z_extra)
        if section > 0:
            scale_z = rms(z_total, all_snaps)
            scales.append(scale_z)
            y = y / scale_z
            z_own, z_other = z_own / scale_z, z_other / scale_z
        if section == ITERS:
            break
        y_all, y_total = gather_rows(y, squares(y))
        z = jnp.concatenate([dot(snapshots, y_all, 0), dot(other, y_all, 0)], axis=0)
        z, y_total = cell_sum(z, y_total)
        scale_y = rms(y_total, all_cells)
        scales.append(scale_y)
        z_own, z_other = z[:width] / scale_y, z[width:] / scale_y
        z_extra = squares(z_own) + squares(z_other)

    def join(own, got):
        pair = jnp.where(core == 0, jnp.stack([own, got]), jnp.stack([got, own]))
        return jnp.moveaxis(pair, 0, 1).reshape(own.shape[0], rank)

    z_out = join(z_own, swap_core(z_other))
    y_split = y.reshape(2, chunk // 2, half)
    y_own = lax.dynamic_index_in_dim(y_split, core, 0, keepdims=False)
    y_send = lax.dynamic_index_in_dim(y_split, 1 - core, 0, keepdims=False)
    known = jnp.concatenate(scales + [squares(y)[: TILE - len(scales)]], axis=0)
    sent = jnp.concatenate([y_send, known], axis=0)
    got = swap_core(sent)
    y_join = join(y_own, got[: chunk // 2])
    known = join(known, got[chunk // 2 :])
    if chips > DIRECT or groups != 4:
        tail = lax.psum(known, ("cell", "snap")) / 2
    else:
        tail = jnp.sum(exchange_z(jnp.broadcast_to(known, (chips,) + known.shape)), axis=0)
        tail = jnp.sum(exchange_cell(jnp.broadcast_to(tail, (groups,) + tail.shape)), axis=0)
    scale_y = rms(tail[TILE - 1 :], all_cells)
    q_out = y_join / scale_y
    return q_out, z_out, jnp.concatenate([known[: len(scales)], scale_y], axis=0)


def solution(mesh):
    return jax.shard_map(
        local,
        mesh=mesh,
        in_specs=(P("cell", "snap"), P("snap", None)),
        out_specs=(P(("cell", "snap"), None), P("snap", None), P()),
        check_vma=False,
    )
```

```python
import functools

import jax
import jax.numpy as jnp
from jax import lax
from jax.experimental import pallas as pl
from jax.experimental.pallas import tpu as pltpu
from jax.sharding import PartitionSpec as P

ITERS = 2
EPS = 1e-05
LANES = 128
TILE = 8
PARTS = 4


def split(x):
    high = x.astype(jnp.bfloat16)
    return high, (x - high.astype(jnp.float32)).astype(jnp.bfloat16)


def product(high, low, a_high, a_low, contract):
    dims = (((1,), (contract,)), ((), ()))
    both = lax.dot_general(
        jnp.concatenate([high, low], axis=0), a_high, dims, preferred_element_type=jnp.float32
    )
    cross = lax.dot_general(high, a_low, dims, preferred_element_type=jnp.float32)
    cols = high.shape[0]
    return both[:cols] + both[cols:] + cross


def eye(cols):
    shape = (cols, LANES)
    return lax.broadcasted_iota(jnp.int32, shape, 0) == lax.broadcasted_iota(jnp.int32, shape, 1)


def to_column(row, cols):
    return jnp.sum(jnp.where(eye(cols), row, 0.0), axis=1, keepdims=True)


def to_row(column):
    return jnp.sum(jnp.where(eye(column.shape[0]), column, 0.0), axis=0, keepdims=True)


def squares_row(x):
    return to_row(jnp.sum(x * x, axis=1, keepdims=True))


def rms(total, count):
    return jnp.sqrt(total / count + EPS)


def wide(ref, cols, count):
    return jnp.concatenate([ref[j * cols : (j + 1) * cols, :] for j in range(count)], axis=1)


def store_blocks(ref, start, x):
    cols = x.shape[0]
    for j in range(x.shape[1] // LANES):
        ref[start + j * cols : start + (j + 1) * cols, :] = x[:, j * LANES : (j + 1) * LANES]


def first_kernel(near_ref, far_ref, own_ref, core_ref, side_ref, diagonal_ref, y_ref, high_ref, low_ref):
    width = own_ref.shape[1]
    for b, ref in enumerate((own_ref, core_ref, side_ref, diagonal_ref)):
        high, low = split(ref[...])
        high_ref[:, b * width : (b + 1) * width] = high
        low_ref[:, b * width : (b + 1) * width] = low
    high, low = split(jnp.concatenate([near_ref[...], far_ref[...]], axis=1))
    store_blocks(y_ref, 0, product(high, low, high_ref[...], low_ref[...], 1))


def send_z(y, high_refs, low_refs, z_ref):
    high, low = split(y)
    part = high_refs[0].shape[0]
    z = None
    for i, (high_ref, low_ref) in enumerate(zip(high_refs, low_refs)):
        cut = slice(i * part, (i + 1) * part)
        term = product(high[:, cut], low[:, cut], high_ref[...], low_ref[...], 0)
        z = term if z is None else z + term
    store_blocks(z_ref, 0, z)
    z_ref[-TILE:, :] = jnp.broadcast_to(squares_row(y), (TILE, LANES))


def first_z_kernel(*refs):
    own, got, high, low = (refs[i * PARTS : (i + 1) * PARTS] for i in range(4))
    cols = own[0].shape[0] * LANES // high[0].shape[0]
    blocks = own[0].shape[0] // cols
    y = jnp.concatenate([wide(a, cols, blocks) + wide(b, cols, blocks) for a, b in zip(own, got)], axis=1)
    send_z(y, high, low, refs[-1])


def z_kernel(count, *refs):
    own_ref, got_ref = refs[:2]
    high, low = refs[2 : 2 + PARTS], refs[2 + PARTS : 2 + 2 * PARTS]
    z_ref, scale_ref = refs[-2:]
    blocks = high[0].shape[0] * PARTS // LANES
    cols = (own_ref.shape[0] - TILE) // blocks
    scale = rms(own_ref[-TILE:, :] + got_ref[-TILE:, :], count)
    scale_ref[...] = scale
    y = (wide(own_ref, cols, blocks) + wide(got_ref, cols, blocks)) / to_column(scale[:1], cols)
    send_z(y, high, low, z_ref)


def y_kernel(count, *refs):
    own_ref, got_ref = refs[:2]
    high_refs, low_refs = refs[2 : 2 + PARTS], refs[2 + PARTS : 2 + 2 * PARTS]
    y_ref, scale_ref, z_ref = refs[-3:]
    blocks = high_refs[0].shape[1] // LANES
    cols = (own_ref.shape[0] - TILE) // blocks
    scale = rms(own_ref[-TILE:, :] + got_ref[-TILE:, :], count)
    scale_ref[...] = scale
    z = (wide(own_ref, cols, blocks) + wide(got_ref, cols, blocks)) / to_column(scale[:1], cols)
    store_blocks(z_ref, 0, z)
    high, low = split(z)
    step = cols * high_refs[0].shape[0] // LANES
    for i, (high_ref, low_ref) in enumerate(zip(high_refs, low_refs)):
        store_blocks(y_ref, i * step, product(high, low, high_ref[...], low_ref[...], 1))
    y_ref[-TILE:, :] = jnp.broadcast_to(squares_row(z), (TILE, LANES))


def prepare_kernel(place_ref, near_ref, got_ref, mine_ref, theirs_ref):
    cols = mine_ref.shape[0]
    width = near_ref.shape[0]
    for b, ref in enumerate((near_ref, got_ref)):
        flipped = ref[...].T
        for ours, out in ((0, mine_ref), (1, theirs_ref)):
            first = place_ref[1] == ours
            out[:, b * width : (b + 1) * width] = jnp.where(first, flipped[:cols], flipped[cols:])


def call(kernel, outs, *args, scalars=0):
    specs = [pl.BlockSpec(memory_space=pltpu.SMEM)] * scalars
    specs += [pl.BlockSpec(memory_space=pltpu.VMEM)] * (len(args) - scalars)
    return pl.pallas_call(
        kernel,
        out_shape=[jax.ShapeDtypeStruct(shape, dtype) for shape, dtype in outs],
        in_specs=specs,
        out_specs=[pl.BlockSpec(memory_space=pltpu.VMEM)] * len(outs),
        compiler_params=pltpu.CompilerParams(vmem_limit_bytes=24 * 1024 * 1024),
    )(*args)


def local(snapshots, sketch):
    f32 = jnp.float32
    groups = lax.axis_size("cell")
    places = lax.axis_size("snap")
    pairs = places // 4
    rows, width = snapshots.shape
    rank = sketch.shape[1]
    half = rank // 2
    cols = rank // 4
    all_cells = rows * groups
    all_snaps = width * places
    place = lax.axis_index("snap")
    core = place % 2
    side = (place // 2) % 2
    pair = place // 4
    where = jnp.stack([core, side, pair]).astype(jnp.int32)
    same_seat = [[4 * p + s for p in range(pairs)] for s in range(4)]

    def swap_core(x):
        return lax.ppermute(x, "snap", [(i, i ^ 1) for i in range(places)])

    def swap_side(x):
        return lax.ppermute(x, "snap", [(i, i ^ 2) for i in range(places)])

    def swap_pair(x):
        if pairs == 2:
            return lax.ppermute(x, "snap", [(i, i ^ 4) for i in range(places)])
        return lax.psum(x, "snap", axis_index_groups=same_seat) - x

    def swap_cell(x, step):
        def target(cell, seat):
            return cell ^ (1 if seat % 2 == step else 2)

        perm = [(c * places + i, target(c, i) * places + i) for c in range(groups) for i in range(places)]
        return lax.ppermute(x, ("cell", "snap"), perm)

    def cell_sum(x):
        if groups != 4:
            return lax.psum(x, "cell"), jnp.zeros_like(x)
        x = x + swap_cell(x, 0)
        return x, swap_cell(x, 1)

    def pick(x, index, count, axis):
        size = x.shape[axis] // count
        return lax.dynamic_slice_in_dim(x, index * size, size, axis)

    def order(flag, own, got, axis):
        first = jnp.where(flag == 0, own, got)
        second = jnp.where(flag == 0, got, own)
        return jnp.concatenate([first, second], axis=axis)

    def unpack(x):
        return jnp.moveaxis(x.reshape(-1, cols, LANES), 0, 1).reshape(cols, -1)

    part = rows // PARTS
    chunks = [snapshots[i * part : (i + 1) * part] for i in range(PARTS)]
    side_chunks = [swap_side(chunks[0])]
    got = swap_core(pick(sketch, 1 - core, 2, 1))
    mine, theirs = call(
        prepare_kernel, [((cols, 2 * width), f32)] * 2, where, pick(sketch, core, 2, 1), got, scalars=1
    )
    far = swap_side(theirs)
    core_block = swap_core(snapshots)
    side_chunks += [swap_side(c) for c in chunks[1:]]
    diagonal_chunks = [swap_core(c) for c in side_chunks]

    high, low, own = [], [], []
    for i in range(PARTS):
        y, a_high, a_low = call(
            first_kernel,
            [((cols * part // LANES, LANES), f32)] + [((part, 4 * width), jnp.bfloat16)] * 2,
            mine, far, chunks[i], core_block[i * part : (i + 1) * part], side_chunks[i], diagonal_chunks[i],
        )
        high.append(a_high)
        low.append(a_low)
        own.append(y)
    got = [swap_pair(y) for y in own]

    sent_shape = ((cols * 4 * width // LANES + TILE, LANES), f32)
    y_shape = ((cols * rows // LANES + TILE, LANES), f32)
    scale_shape = ((TILE, LANES), f32)
    z_shape = ((cols * 4 * width // LANES, LANES), f32)
    (sent,) = call(first_z_kernel, [sent_shape], *own, *got, *high, *low)
    scales = []
    for section in range(ITERS):
        a, b = cell_sum(sent)
        y, scale, z = call(
            functools.partial(y_kernel, all_cells), [y_shape, scale_shape, z_shape], a, b, *high, *low
        )
        scales.append(scale)
        if section == ITERS - 1:
            break
        sent, scale = call(
            functools.partial(z_kernel, all_snaps), [sent_shape, scale_shape], y, swap_pair(y), *high, *low
        )
        scales.append(scale)

    near, far = z[: z.shape[0] // 2], z[z.shape[0] // 2 :]
    z = order(side, unpack(near), unpack(swap_side(far)), 0)
    z = order(core, z[:, :width], swap_core(z[:, width:]), 0)

    tail = y[-TILE:]
    y = y[:-TILE]
    if pairs == 2:
        got = swap_pair(jnp.concatenate([pick(y, 1 - pair, 2, 0), tail], axis=0))
        y, tail = unpack(pick(y, pair, 2, 0) + got[:-TILE]), tail + got[-TILE:]
    else:
        y = lax.psum(unpack(y), "snap", axis_index_groups=same_seat)
        y = pick(y, pair, pairs, 1)
        tail = lax.psum(tail, "snap", axis_index_groups=same_seat)
    scales.append(rms(tail, all_snaps))
    known = jnp.concatenate([s[:1, :cols] for s in scales], axis=0).T
    y = y / known[:, -1:]
    known = jnp.concatenate([known, jnp.sum(y * y, axis=1, keepdims=True)], axis=1)
    known = jnp.pad(known, ((0, 0), (0, LANES - known.shape[1])))
    got = swap_side(jnp.concatenate([pick(y, 1 - side, 2, 1), known], axis=1))
    y = order(side, jnp.concatenate([pick(y, side, 2, 1), known], axis=1), got, 0)
    y, known = y[:, :-LANES], y[:, -LANES:]
    got = swap_core(jnp.concatenate([pick(y, 1 - core, 2, 1), known], axis=1))
    y = order(core, jnp.concatenate([pick(y, core, 2, 1), known], axis=1), got, 0)
    y, known = y[:, :-LANES], y[:, -LANES:].T[: 2 * ITERS + 1]
    total = known + swap_pair(known)
    a, b = cell_sum(total)
    scale_y = rms((a + b)[2 * ITERS :], all_cells)
    q_out = y.T / scale_y
    z_out = z.T / known[2 * ITERS - 1 : 2 * ITERS]
    return q_out, z_out, jnp.concatenate([known[: 2 * ITERS], scale_y], axis=0)


def solution(mesh):
    return jax.shard_map(
        local,
        mesh=mesh,
        in_specs=(P("cell", "snap"), P("snap", None)),
        out_specs=(P(("cell", "snap"), None), P("snap", None), P()),
        check_vma=False,
    )
```

```python
import functools

import jax
import jax.numpy as jnp
from jax import lax
from jax.experimental import pallas as pl
from jax.experimental.pallas import tpu as pltpu
from jax.sharding import PartitionSpec as P

ITERS = 2
EPS = 1e-05
LANES = 128
TILE = 8
PARTS = (2, 2, 2, 1, 1)
BF16 = jnp.bfloat16
F32 = jnp.float32


def split(x):
    high = x.astype(BF16).astype(F32)
    return high, x - high


def dot(a, b):
    return lax.dot_general(a, b, (((1,), (0,)), ((), ())), preferred_element_type=F32)


def eye(cols):
    shape = (cols, LANES)
    return lax.broadcasted_iota(jnp.int32, shape, 0) == lax.broadcasted_iota(jnp.int32, shape, 1)


def to_column(row, cols):
    return jnp.sum(jnp.where(eye(cols), row, 0.0), axis=1, keepdims=True)


def to_row(column):
    return jnp.sum(jnp.where(eye(column.shape[0]), column, 0.0), axis=0, keepdims=True)


def squares_row(x):
    return to_row(jnp.sum(x * x, axis=1, keepdims=True))


def rms(total, count):
    return jnp.sqrt(total / count + EPS)


def wide(x, cols):
    return jnp.concatenate([x[j * cols : (j + 1) * cols] for j in range(x.shape[0] // cols)], axis=1)


def store_blocks(ref, start, x):
    cols = x.shape[0]
    for j in range(x.shape[1] // LANES):
        ref[start + j * cols : start + (j + 1) * cols, :] = x[:, j * LANES : (j + 1) * LANES]


def turn(x, cols):
    return pltpu.roll(x, cols, 1)


def left(shape, cols):
    return lax.broadcasted_iota(jnp.int32, shape, 1) < cols


def fold_blocks(total, cols):
    flipped = total.T
    return flipped[:cols] + flipped[cols:]


def sketch_sides(x):
    cols = LANES // 2
    high, low = split(x)
    first = left(x.shape, cols)
    own = jnp.where(first, high, turn(low, cols))
    other = jnp.where(first, turn(high, cols), low)
    return own.astype(BF16), other.astype(BF16)


def prepare_kernel(place_ref, near_ref, got_ref, a_ref, mine_ref, theirs_ref, *refs):
    outs, sems = refs[:-1], refs[-1]
    start = a_ref.shape[0] - sum(out.shape[0] for out in outs)
    copies = []
    for i, out in enumerate(outs):
        copies.append(pltpu.make_async_copy(a_ref.at[pl.ds(start, out.shape[0])], out, sems.at[i]))
        start += out.shape[0]
        copies[-1].start()
    cols = LANES // 2
    near, got = near_ref[...], got_ref[...]
    first = left(near.shape, cols)
    low = jnp.where(first, near, turn(got, cols))
    high = jnp.where(first, turn(near, cols), got)
    zero = place_ref[1] == 0
    mine_ref[...] = jnp.where(zero, low, high)
    theirs_ref[...] = jnp.where(zero, high, low)
    for copy in copies:
        copy.wait()


def near_kernel(own_ref, core_ref, mine_ref, y_ref, high_ref, low_ref):
    width = own_ref.shape[1]
    cols = LANES // 2
    rhs = jnp.concatenate(sketch_sides(mine_ref[...]), axis=0)
    for b in range(own_ref.shape[0] // LANES):
        cut = slice(b * LANES, (b + 1) * LANES)
        for s, ref in enumerate((own_ref, core_ref)):
            high, low = split(ref[cut, :])
            high_ref[cut, s * width : (s + 1) * width] = high.astype(BF16)
            low_ref[cut, s * width : (s + 1) * width] = low.astype(BF16)
    for b in range(own_ref.shape[0] // LANES):
        cut = slice(b * LANES, (b + 1) * LANES)
        total = dot(high_ref[cut, :], rhs) + dot(low_ref[cut, :], rhs)
        y_ref[b * cols : (b + 1) * cols, :] = fold_blocks(total, cols)


def far_kernel(start, side_ref, diagonal_ref, far_ref, near_ref, y_ref, high_ref, low_ref):
    width = side_ref.shape[1]
    cols = LANES // 2
    rhs = jnp.concatenate(sketch_sides(far_ref[...]), axis=0)
    for s, ref in enumerate((side_ref, diagonal_ref)):
        high, low = split(ref[...])
        high_ref[:, s * width : (s + 1) * width] = high.astype(BF16)
        low_ref[:, s * width : (s + 1) * width] = low.astype(BF16)
    for b in range(side_ref.shape[0] // LANES):
        cut = slice(b * LANES, (b + 1) * LANES)
        total = dot(high_ref[cut, :], rhs) + dot(low_ref[cut, :], rhs)
        at = (start // LANES + b) * cols
        y_ref[b * cols : (b + 1) * cols, :] = fold_blocks(total, cols) + near_ref[at : at + cols, :]


def unfold(total):
    cols = total.shape[0] // 2
    return total[:cols] + total[cols:]


def send_z(y, high_refs, low_refs, z_ref):
    lhs = jnp.concatenate(split(y), axis=0).astype(BF16)
    near = dot(lhs, high_refs[0][...]) + dot(lhs, low_refs[0][...])
    far, at = None, 0
    for high_ref, low_ref in zip(high_refs[1:], low_refs[1:]):
        cut = slice(at, at + high_ref.shape[0])
        term = dot(lhs[:, cut], high_ref[...]) + dot(lhs[:, cut], low_ref[...])
        far = term if far is None else far + term
        at += high_ref.shape[0]
    near, far = unfold(near), unfold(far)
    store_blocks(z_ref, 0, near)
    store_blocks(z_ref, (z_ref.shape[0] - TILE) // 2, far)
    z_ref[-TILE:, :] = jnp.broadcast_to(squares_row(y), (TILE, LANES))


def first_z_kernel(*refs):
    count = len(PARTS)
    cols = LANES // 2
    own, got = refs[:count], refs[count : 2 * count]
    high, low = refs[2 * count : 3 * count + 1], refs[3 * count + 1 : 4 * count + 2]
    y = jnp.concatenate([wide(a[...] + b[...], cols) for a, b in zip(own, got)], axis=1)
    send_z(y, high, low, refs[-1])


def scaled(own_ref, got_ref, count):
    cols = LANES // 2
    total = own_ref[...] + got_ref[...]
    scale = rms(total[-TILE:], count)
    return wide(total[:-TILE], cols) / to_column(scale[:1], cols), scale


def z_kernel(count, *refs):
    own_ref, got_ref = refs[:2]
    parts = len(PARTS) + 1
    high, low = refs[2 : 2 + parts], refs[2 + parts : 2 + 2 * parts]
    z_ref, scale_ref = refs[-2:]
    y, scale = scaled(own_ref, got_ref, count)
    scale_ref[...] = scale
    send_z(y, high, low, z_ref)


def product_y(z, high_refs, low_refs):
    cols = z.shape[0]
    rhs = jnp.concatenate(split(z), axis=0).T.astype(BF16)
    middle = rhs.shape[0] // 2
    rows, at = [], 0
    for high_ref, low_ref in zip(high_refs[1:], low_refs[1:]):
        for b in range(high_ref.shape[0] // LANES):
            near = slice(at, at + LANES)
            far = slice(b * LANES, (b + 1) * LANES)
            total = dot(high_refs[0][near, :], rhs[:middle]) + dot(low_refs[0][near, :], rhs[:middle])
            total += dot(high_ref[far, :], rhs[middle:]) + dot(low_ref[far, :], rhs[middle:])
            rows.append(fold_blocks(total, cols))
            at += LANES
    return rows


def y_kernel(count, *refs):
    own_ref, got_ref = refs[:2]
    parts = len(PARTS) + 1
    high, low = refs[2 : 2 + parts], refs[2 + parts : 2 + 2 * parts]
    y_ref, scale_ref = refs[-2:]
    z, scale = scaled(own_ref, got_ref, count)
    scale_ref[...] = scale
    cols = z.shape[0]
    for j, block in enumerate(product_y(z, high, low)):
        y_ref[j * cols : (j + 1) * cols, :] = block
    y_ref[-TILE:, :] = jnp.broadcast_to(squares_row(z), (TILE, LANES))


def last_y_kernel(count, place_ref, *refs):
    own_ref, got_ref = refs[:2]
    parts = len(PARTS) + 1
    high, low = refs[2 : 2 + parts], refs[2 + parts : 2 + 2 * parts]
    keep_ref, send_ref, scale_ref, z_ref = refs[-4:]
    z, scale = scaled(own_ref, got_ref, count)
    scale_ref[...] = scale
    store_blocks(z_ref, 0, z)
    cols = z.shape[0]
    blocks = product_y(z, high, low)
    middle = len(blocks) // 2
    zero = place_ref[2] == 0
    for j in range(middle):
        cut = slice(j * cols, (j + 1) * cols)
        keep_ref[cut, :] = jnp.where(zero, blocks[j], blocks[middle + j])
        send_ref[cut, :] = jnp.where(zero, blocks[middle + j], blocks[j])
    tail = jnp.broadcast_to(squares_row(z), (TILE, LANES))
    keep_ref[-TILE:, :] = tail
    send_ref[-TILE:, :] = tail


def side_kernel(count, place_ref, keep_ref, got_ref, *refs):
    scales, (own_ref, send_ref) = refs[:-2], refs[-2:]
    y, scale = scaled(keep_ref, got_ref, count)
    row = lax.broadcasted_iota(jnp.int32, (TILE, LANES), 0)
    tail = jnp.broadcast_to(squares_row(y), (TILE, LANES))
    for i, known in enumerate([ref[...] for ref in scales] + [scale]):
        tail = jnp.where(row == i, known, tail)
    middle = y.shape[1] // 2
    zero = place_ref[1] == 0
    store_blocks(own_ref, 0, jnp.where(zero, y[:, :middle], y[:, middle:]))
    store_blocks(send_ref, 0, jnp.where(zero, y[:, middle:], y[:, :middle]))
    own_ref[-TILE:, :] = tail
    send_ref[-TILE:, :] = tail


def core_kernel(place_ref, own_ref, got_ref, keep_ref, send_ref):
    cols = LANES // 2
    zero_side, zero_core = place_ref[1] == 0, place_ref[0] == 0
    own, got = own_ref[...], got_ref[...]
    for s, x in enumerate((jnp.where(zero_side, own, got), jnp.where(zero_side, got, own))):
        first, second, tail = x[:cols], x[cols : 2 * cols], x[2 * cols :]
        keep_ref[s * cols : (s + 1) * cols, :] = jnp.where(zero_core, first, second)
        send_ref[s * cols : (s + 1) * cols, :] = jnp.where(zero_core, second, first)
        at = 2 * cols + s * TILE
        keep_ref[at : at + TILE, :] = tail
        send_ref[at : at + TILE, :] = tail


def join_kernel(place_ref, keep_ref, got_ref, y_ref, known_ref):
    cols = LANES // 2
    zero = place_ref[0] == 0
    keep, got = keep_ref[...], got_ref[...]
    first = left((TILE, LANES), cols)
    for s, x in enumerate((jnp.where(zero, keep, got), jnp.where(zero, got, keep))):
        cut = slice(s * LANES, (s + 1) * LANES)
        y_ref[:, cut] = x[:LANES].T
        known_ref[:, cut] = jnp.where(first, x[LANES : LANES + TILE], turn(x[LANES + TILE :], cols))


def z_out_kernel(place_ref, near_ref, got_ref, core_ref, known_ref, z_ref):
    cols = LANES // 2
    zero_side, zero_core = place_ref[1] == 0, place_ref[0] == 0

    def side_order(own, other):
        pairs = [wide(jnp.where(zero_side, a, b), cols) for a, b in ((own, other), (other, own))]
        return jnp.concatenate(pairs, axis=0)

    middle = core_ref.shape[0] // 2
    mine = side_order(near_ref[:middle, :], got_ref[:middle, :])
    theirs = side_order(core_ref[:middle, :], core_ref[middle:, :])
    for s, x in enumerate((jnp.where(zero_core, mine, theirs), jnp.where(zero_core, theirs, mine))):
        cut = slice(s * LANES, (s + 1) * LANES)
        z_ref[:, cut] = x.T / known_ref[2 * ITERS - 1 : 2 * ITERS, cut]


def q_out_kernel(count, y_ref, known_ref, a_ref, b_ref, q_ref, scale_ref):
    last = 2 * ITERS
    scale = rms((a_ref[...] + b_ref[...])[last : last + 1], count)
    q_ref[...] = y_ref[...] / scale
    scale_ref[:last, :] = known_ref[:last, :]
    scale_ref[last:, :] = scale


def call(kernel, outs, *args, scalars=0, any_space=(), scratch=(), plain=False):
    specs = [pl.BlockSpec(memory_space=pltpu.SMEM)] * scalars
    for i in range(scalars, len(args)):
        specs.append(pl.BlockSpec(memory_space=pl.ANY if i in any_space else pltpu.VMEM))
    out_spec = pl.BlockSpec() if plain else pl.BlockSpec(memory_space=pltpu.VMEM)
    return pl.pallas_call(
        kernel,
        out_shape=[jax.ShapeDtypeStruct(shape, dtype) for shape, dtype in outs],
        in_specs=specs,
        out_specs=[out_spec] * len(outs),
        scratch_shapes=scratch,
        compiler_params=pltpu.CompilerParams(vmem_limit_bytes=16 * 1024 * 1024),
    )(*args)


def local(snapshots, sketch):
    groups = lax.axis_size("cell")
    places = lax.axis_size("snap")
    pairs = places // 4
    rows, width = snapshots.shape
    rank = sketch.shape[1]
    cols = rank // 4
    all_cells = rows * groups
    all_snaps = width * places
    place = lax.axis_index("snap")
    core = place % 2
    side = (place // 2) % 2
    pair = place // 4
    where = jnp.stack([core, side, pair]).astype(jnp.int32)
    same_seat = [[4 * p + s for p in range(pairs)] for s in range(4)]
    same_pair = [[4 * p + s for s in range(4)] for p in range(pairs)]

    def swap_core(x):
        return lax.ppermute(x, "snap", [(i, i ^ 1) for i in range(places)])

    def swap_side(x):
        return lax.ppermute(x, "snap", [(i, i ^ 2) for i in range(places)])

    def swap_pair(x):
        if pairs == 2:
            return lax.ppermute(x, "snap", [(i, i ^ 4) for i in range(places)])
        return lax.psum(x, "snap", axis_index_groups=same_seat) - x

    def swap_cell(x, step):
        def target(cell, seat):
            return cell ^ (1 if seat % 2 == step else 2)

        perm = [(c * places + i, target(c, i) * places + i) for c in range(groups) for i in range(places)]
        return lax.ppermute(x, ("cell", "snap"), perm)

    def cell_sum(x):
        if groups != 4:
            return lax.psum(x, "cell"), jnp.zeros_like(x)
        x = x + swap_cell(x, 0)
        return x, swap_cell(x, 1)

    def half(x, index):
        size = x.shape[1] // 2
        return lax.dynamic_slice_in_dim(x, index * size, size, 1)

    sizes = [n * rows // sum(PARTS) for n in PARTS]
    starts = [sum(sizes[:i]) for i in range(len(sizes))]

    core_block = swap_core(snapshots)
    side_chunks = [swap_side(snapshots[: sizes[0]])]
    got = swap_core(half(sketch, 1 - core))
    packed = ((width, LANES), F32)
    mine, theirs, *chunks = call(
        prepare_kernel,
        [packed, packed] + [((n, width), F32) for n in sizes[1:]],
        where, half(sketch, core), got, snapshots,
        scalars=1, any_space=(3,), scratch=[pltpu.SemaphoreType.DMA((len(sizes) - 1,))],
    )
    far = swap_side(theirs)
    side_chunks += [swap_side(c) for c in chunks]
    diagonal_chunks = [swap_core(c) for c in side_chunks]

    def factor(count):
        return [((count, 2 * width), BF16)] * 2

    near_y, *near = call(
        near_kernel, [((cols * rows // LANES, LANES), F32)] + factor(rows), snapshots, core_block, mine
    )
    high, low, own = [near[0]], [near[1]], []
    for i, size in enumerate(sizes):
        y, a_high, a_low = call(
            functools.partial(far_kernel, starts[i]),
            [((cols * size // LANES, LANES), F32)] + factor(size),
            side_chunks[i], diagonal_chunks[i], far, near_y,
        )
        high.append(a_high)
        low.append(a_low)
        own.append(y)
    got = [swap_pair(y) for y in own]

    sent_shape = ((cols * 4 * width // LANES + TILE, LANES), F32)
    y_shape = ((cols * rows // LANES + TILE, LANES), F32)
    scale_shape = ((TILE, LANES), F32)
    z_shape = ((cols * 4 * width // LANES, LANES), F32)
    (sent,) = call(first_z_kernel, [sent_shape], *own, *got, *high, *low)
    scales = []
    for section in range(ITERS - 1):
        a, b = cell_sum(sent)
        y, scale_y = call(
            functools.partial(y_kernel, all_cells), [y_shape, scale_shape], a, b, *high, *low
        )
        sent, scale_z = call(
            functools.partial(z_kernel, all_snaps), [sent_shape, scale_shape], y, swap_pair(y), *high, *low
        )
        scales += [scale_y, scale_z]
    a, b = cell_sum(sent)
    half_shape = ((cols * rows // LANES // 2 + TILE, LANES), F32)
    keep, send, scale, z = call(
        functools.partial(last_y_kernel, all_cells),
        [half_shape, half_shape, scale_shape, z_shape],
        where, a, b, *high, *low, scalars=1,
    )
    scales.append(scale)

    middle = z.shape[0] // 2
    z_near, z_far = z[:middle], z[middle:]

    if pairs == 2 and groups == 4:
        got = swap_pair(send)
        z_got = swap_side(z_far)
        z_core = swap_core(jnp.concatenate([z_near[middle // 2 :], z_got[middle // 2 :]], axis=0))
        quarter = ((2 * cols + TILE, LANES), F32)
        own, send = call(
            functools.partial(side_kernel, all_snaps), [quarter, quarter], where, keep, got, *scales, scalars=1
        )
        joint = ((2 * cols + 2 * TILE, LANES), F32)
        keep, send = call(core_kernel, [joint, joint], where, own, swap_side(send), scalars=1)
        y, known = call(
            join_kernel, [((LANES, rank), F32), ((TILE, rank), F32)], where, keep, swap_core(send), scalars=1
        )
        total = known + swap_pair(known)
        a, b = cell_sum(total)
        (z_out,) = call(
            z_out_kernel, [((width, rank), F32)], where, z_near, z_got, z_core, known, scalars=1, plain=True
        )
        q_out, scale_out = call(
            functools.partial(q_out_kernel, all_cells),
            [((LANES, rank), F32), ((2 * ITERS + 1, rank), F32)],
            y, known, a, b, plain=True,
        )
        return q_out, z_out, scale_out

    z_got = swap_side(z_far)
    z_core = swap_core(jnp.concatenate([z_near[middle // 2 :], z_got[middle // 2 :]], axis=0))
    first = jnp.where(pair == 0, keep[:-TILE], send[:-TILE])
    second = jnp.where(pair == 0, send[:-TILE], keep[:-TILE])
    y = jnp.concatenate([first, second], axis=0).reshape(-1, cols, LANES)
    y = jnp.moveaxis(y, 0, 1).reshape(cols, rows)
    y = lax.psum(y, "snap", axis_index_groups=same_seat)
    total = lax.psum(keep[-TILE:], "snap", axis_index_groups=same_seat)
    scales.append(rms(total, all_snaps))
    known = jnp.stack([s[0, :cols] for s in scales], axis=1)
    y = y / known[:, -1:]
    scale_y = rms(lax.psum(jnp.sum(y * y, axis=1, keepdims=True), "cell"), all_cells)
    y = y / scale_y
    gathered = lax.all_gather(jnp.concatenate([y, known, scale_y], axis=1), "snap", axis_index_groups=same_pair)
    gathered = gathered.reshape(2, 2, cols, -1).swapaxes(0, 1).reshape(rank, -1)
    mine = rows // places
    q_out = lax.dynamic_slice_in_dim(gathered, place * mine, mine, 1).T
    scale_out = gathered[:, rows:].T
    known = jnp.pad(scale_out, ((0, TILE - scale_out.shape[0]), (0, 0)))
    (z_out,) = call(z_out_kernel, [((width, rank), F32)], where, z_near, z_got, z_core, known, scalars=1)
    return q_out, z_out, scale_out


def solution(mesh):
    return jax.shard_map(
        local,
        mesh=mesh,
        in_specs=(P("cell", "snap"), P("snap", None)),
        out_specs=(P(("cell", "snap"), None), P("snap", None), P()),
        check_vma=False,
    )
```

```python
import functools

import jax
import jax.numpy as jnp
from jax import lax
from jax.experimental import pallas as pl
from jax.experimental.pallas import tpu as pltpu
from jax.sharding import PartitionSpec as P

ITERS = 2
EPS = 1e-05
LANES = 128
TILE = 8
CHIPS = 4
GROUPS = 4
HALVES = 2
BF16 = jnp.bfloat16
F32 = jnp.float32


def split(x):
    high = x.astype(BF16).astype(F32)
    return high, x - high


def dot(a, b):
    return lax.dot_general(a, b, (((1,), (0,)), ((), ())), preferred_element_type=F32)


def eye(cols):
    shape = (cols, LANES)
    return lax.broadcasted_iota(jnp.int32, shape, 0) == lax.broadcasted_iota(jnp.int32, shape, 1)


def to_column(row, cols):
    return jnp.sum(jnp.where(eye(cols), row, 0.0), axis=1, keepdims=True)


def to_row(column):
    return jnp.sum(jnp.where(eye(column.shape[0]), column, 0.0), axis=0, keepdims=True)


def squares_tile(x):
    row = to_row(jnp.sum(x * x, axis=1, keepdims=True))
    return jnp.broadcast_to(row, (TILE, LANES))


def rms(total, count):
    return jnp.sqrt(total / count + EPS)


def wide(x, cols):
    return jnp.concatenate([x[j * cols : (j + 1) * cols] for j in range(x.shape[0] // cols)], axis=1)


def store_blocks(ref, x):
    cols = x.shape[0]
    for j in range(x.shape[1] // LANES):
        ref[j * cols : (j + 1) * cols, :] = x[:, j * LANES : (j + 1) * LANES]


def turn(x, cols):
    return pltpu.roll(x, cols, 1)


def join_lanes(first, second, cols):
    left = lax.broadcasted_iota(jnp.int32, first.shape, 1) < cols
    return jnp.where(left, first, turn(second, cols))


def chunk_at(place_ref, shift):
    return lax.rem(place_ref[0] + shift + CHIPS, CHIPS)


def ordered_tiles(place_ref, tiles, scratch_ref):
    for shift, tile in enumerate(tiles):
        start = pl.multiple_of(chunk_at(place_ref, -shift) * TILE, TILE)
        scratch_ref[pl.ds(start, TILE), :] = tile
    total = scratch_ref[:TILE, :]
    for i in range(1, CHIPS):
        total += scratch_ref[i * TILE : (i + 1) * TILE, :]
    return total


def chunk_product(place_ref, shift, rows, rhs, high_ref, low_ref):
    cut = pl.ds(pl.multiple_of(chunk_at(place_ref, shift) * rows, rows), rows)
    total = dot(high_ref[cut, :], rhs) + dot(low_ref[cut, :], rhs)
    return total


def first_kernel(place_ref, own_ref, core_ref, near_ref, got_ref, *refs):
    sends, (high_ref, low_ref) = refs[:-2], refs[-2:]
    width = own_ref.shape[1]
    rows = own_ref.shape[0] // CHIPS
    for b in range(own_ref.shape[0] // LANES):
        cut = slice(b * LANES, (b + 1) * LANES)
        for s, ref in enumerate((own_ref, core_ref)):
            high, low = split(ref[cut, :])
            high_ref[cut, s * width : (s + 1) * width] = high.astype(BF16)
            low_ref[cut, s * width : (s + 1) * width] = low.astype(BF16)
    z = jnp.concatenate([near_ref[...], got_ref[...]], axis=0)
    rhs = jnp.concatenate(split(z), axis=1).astype(BF16)
    cols = LANES // HALVES
    for shift in range(CHIPS):
        total = chunk_product(place_ref, shift, rows, rhs, high_ref, low_ref)
        y = (total[:, :LANES] + total[:, LANES:]).T
        for h in range(HALVES):
            ref = sends[h * CHIPS + shift]
            store_blocks(ref, y[h * cols : (h + 1) * cols])
            ref[-TILE:, :] = jnp.zeros((TILE, LANES), F32)


def chunk_sum(count, place_ref, refs, scratch_ref):
    cols = LANES // HALVES
    total = refs[0][:-TILE, :]
    for ref in refs[1:]:
        total += ref[:-TILE, :]
    y = wide(total, cols)
    if count is None:
        return y, None
    scale = rms(ordered_tiles(place_ref, [ref[-TILE:, :] for ref in refs], scratch_ref), count)
    return y / to_column(scale[:1], cols), scale


def sum_kernel(count, place_ref, *refs):
    parts, outs, scratch_ref = refs[:CHIPS], refs[CHIPS:-1], refs[-1]
    y, scale = chunk_sum(count, place_ref, parts, scratch_ref)
    store_blocks(outs[0], y)
    outs[0][-TILE:, :] = squares_tile(y)
    if scale is not None:
        outs[1][...] = scale


def z_kernel(place_ref, *refs):
    parts, (high_ref, low_ref, z_ref, scratch_ref) = refs[:CHIPS], refs[CHIPS:]
    cols = LANES // HALVES
    rows = high_ref.shape[0] // CHIPS
    z = None
    for shift, ref in enumerate(parts):
        y = wide(ref[:-TILE, :], cols)
        lhs = jnp.concatenate(split(y), axis=0).astype(BF16)
        cut = pl.ds(pl.multiple_of(chunk_at(place_ref, -shift) * rows, rows), rows)
        term = dot(lhs, high_ref[cut, :]) + dot(lhs, low_ref[cut, :])
        z = term if z is None else z + term
    store_blocks(z_ref, z[:cols] + z[cols:])
    z_ref[-TILE:, :] = ordered_tiles(place_ref, [ref[-TILE:, :] for ref in parts], scratch_ref)


def y_kernel(count, place_ref, a_ref, b_ref, high_ref, low_ref, *refs):
    sends, scale_ref, z_refs = refs[:CHIPS], refs[CHIPS], refs[CHIPS + 1 :]
    cols = LANES // HALVES
    rows = high_ref.shape[0] // CHIPS
    total = a_ref[...] + b_ref[...]
    scale = rms(total[-TILE:], count)
    scale_ref[...] = scale
    z = wide(total[:-TILE], cols) / to_column(scale[:1], cols)
    for z_ref in z_refs:
        store_blocks(z_ref, z)
    tail = squares_tile(z)
    rhs = jnp.concatenate(split(z), axis=0).T.astype(BF16)
    for shift, ref in enumerate(sends):
        y = chunk_product(place_ref, shift, rows, rhs, high_ref, low_ref).T
        store_blocks(ref, y[:cols] + y[cols:])
        ref[-TILE:, :] = tail


def last_kernel(count, place_ref, first_ref, *refs):
    parts, scales = refs[:CHIPS], refs[CHIPS:-3]
    keep_ref, send_ref, scratch_ref = refs[-3:]
    cols = LANES // HALVES
    y, scale = chunk_sum(count, place_ref, parts, scratch_ref)
    middle = (len(scales) + 1) // 2
    row = lax.broadcasted_iota(jnp.int32, (TILE, LANES), 0)
    tail = join_lanes(first_ref[-TILE:, :], squares_tile(y), cols)
    second = [ref[...] for ref in scales[middle:]] + [scale]
    for i, (a_ref, b) in enumerate(zip(scales[:middle], second)):
        tail = jnp.where(row == i, join_lanes(a_ref[...], b, cols), tail)
    zero = place_ref[1] == 0
    blocks = ((first_ref[:cols, :], first_ref[cols : 2 * cols, :]), (y[:, :LANES], y[:, LANES:]))
    for h, (a, b) in enumerate(blocks):
        cut = slice(h * cols, (h + 1) * cols)
        keep_ref[cut, :] = jnp.where(zero, a, b)
        send_ref[cut, :] = jnp.where(zero, b, a)
    keep_ref[-TILE:, :] = tail
    send_ref[-TILE:, :] = tail


def join_kernel(place_ref, keep_ref, got_ref, y_ref, known_ref):
    zero = place_ref[1] == 0
    keep, got = keep_ref[...], got_ref[...]
    for s, x in enumerate((jnp.where(zero, keep, got), jnp.where(zero, got, keep))):
        cut = slice(s * LANES, (s + 1) * LANES)
        y_ref[:, cut] = x[:LANES].T
        known_ref[:, cut] = x[LANES:]


def z_out_kernel(place_ref, first_ref, second_ref, got_first_ref, got_second_ref, known_ref, z_ref):
    cols = LANES // HALVES
    zero = place_ref[1] == 0
    own_rows = first_ref.shape[0] // 2
    mine = jnp.concatenate([wide(ref[:own_rows, :], cols) for ref in (first_ref, second_ref)], axis=0)
    theirs = jnp.concatenate([wide(ref[...], cols) for ref in (got_first_ref, got_second_ref)], axis=0)
    for s, x in enumerate((jnp.where(zero, mine, theirs), jnp.where(zero, theirs, mine))):
        cut = slice(s * LANES, (s + 1) * LANES)
        z_ref[:, cut] = x.T / known_ref[2 * ITERS - 1 : 2 * ITERS, cut]


def q_out_kernel(count, y_ref, known_ref, a_ref, b_ref, q_ref, scale_ref):
    last = 2 * ITERS
    scale = rms((a_ref[...] + b_ref[...])[last : last + 1], count)
    q_ref[...] = y_ref[...] / scale
    scale_ref[:last, :] = known_ref[:last, :]
    scale_ref[last:, :] = scale


def call(kernel, outs, *args, scalars=1, plain=False, tiles=False):
    specs = [pl.BlockSpec(memory_space=pltpu.SMEM)] * scalars
    specs += [pl.BlockSpec(memory_space=pltpu.VMEM)] * (len(args) - scalars)
    out_spec = pl.BlockSpec() if plain else pl.BlockSpec(memory_space=pltpu.VMEM)
    return pl.pallas_call(
        kernel,
        out_shape=[jax.ShapeDtypeStruct(shape, dtype) for shape, dtype in outs],
        in_specs=specs,
        out_specs=[out_spec] * len(outs),
        scratch_shapes=[pltpu.VMEM((CHIPS * TILE, LANES), F32)] if tiles else [],
        compiler_params=pltpu.CompilerParams(vmem_limit_bytes=16 * 1024 * 1024),
    )(*args)


def general(snapshots, sketch):
    high = lax.Precision.HIGHEST
    all_cells = snapshots.shape[0] * lax.axis_size("cell")
    all_snaps = snapshots.shape[1] * lax.axis_size("snap")
    z, scales = sketch, []
    for section in range(ITERS + 1):
        partial = jnp.dot(snapshots, z, precision=high, preferred_element_type=F32)
        y = lax.psum_scatter(partial, "snap", scatter_dimension=0, tiled=True)
        scale = rms(lax.psum(jnp.sum(y * y, axis=0), ("cell", "snap")), all_cells)
        scales.append(scale)
        q = y / scale
        if section < ITERS:
            whole = lax.all_gather(q, "snap", axis=0, tiled=True)
            partial = jnp.dot(snapshots.T, whole, precision=high, preferred_element_type=F32)
            z = lax.psum(partial, "cell")
            scale = rms(lax.psum(jnp.sum(z * z, axis=0), "snap"), all_snaps)
            scales.append(scale)
            z = z / scale
    return q, z, jnp.stack(scales)


def local(snapshots, sketch):
    groups = lax.axis_size("cell")
    places = lax.axis_size("snap")
    rows, width = snapshots.shape
    rank = sketch.shape[1]
    if groups != GROUPS or places != 2 * CHIPS or rank != 2 * LANES or rows % (CHIPS * LANES) or width % LANES:
        return general(snapshots, sketch)
    cols = LANES // HALVES
    all_cells = rows * groups
    all_snaps = width * places
    seat = lax.axis_index("snap")
    core, chip = seat % 2, seat // 2
    place = jnp.stack([chip, core]).astype(jnp.int32)

    def swap(x, bits):
        return lax.ppermute(x, "snap", [(i, i ^ bits) for i in range(places)])

    def shift(x, d):
        return lax.ppermute(x, "snap", [(i, (i + 2 * d) % places) for i in range(places)])

    def swap_cell(x, step):
        def target(cell, i):
            return cell ^ (1 if i % 2 == step else 2)

        perm = [(c * places + i, target(c, i) * places + i) for c in range(groups) for i in range(places)]
        return lax.ppermute(x, ("cell", "snap"), perm)

    def cell_pair(x):
        x = x + swap_cell(x, 0)
        return x, swap_cell(x, 1)

    def scatter(parts):
        return [parts[0]] + [shift(parts[d], d) for d in range(1, CHIPS)]

    def gather(part):
        return [part] + [shift(part, d) for d in range(1, CHIPS)]

    def sketch_half(index):
        return lax.dynamic_slice_in_dim(sketch, index * LANES, LANES, 1)

    chunk_shape = ((cols * rows // CHIPS // LANES + TILE, LANES), F32)
    z_shape = ((cols * 2 * width // LANES + TILE, LANES), F32)
    out_shape = ((cols * 2 * width // LANES, LANES), F32)
    scale_shape = ((TILE, LANES), F32)
    factor = ((rows, 2 * width), BF16)

    *parts, high, low = call(
        first_kernel,
        [chunk_shape] * (HALVES * CHIPS) + [factor, factor],
        place, snapshots, swap(snapshots, 1), sketch_half(core), swap(sketch_half(1 - core), 1),
    )
    sends = [parts[h * CHIPS : (h + 1) * CHIPS] for h in range(HALVES)]
    scales = [[] for _ in range(HALVES)]
    z_parts = [None] * HALVES
    for section in range(ITERS):
        for h in range(HALVES):
            count = all_snaps if section else None
            y, *scale = call(
                functools.partial(sum_kernel, count),
                [chunk_shape] + [scale_shape] * (section > 0),
                place, *scatter(sends[h]), tiles=True,
            )
            scales[h] += scale
            (z,) = call(z_kernel, [z_shape], place, *gather(y), high, low, tiles=True)
            last = section == ITERS - 1
            *sends[h], scale = call(
                functools.partial(y_kernel, all_cells),
                [chunk_shape] * CHIPS + [scale_shape] + [out_shape] * last,
                place, *cell_pair(z), high, low,
            )[: CHIPS + 1 + last]
            if last:
                scale, z_parts[h] = sends[h].pop(), scale
            scales[h].append(scale)

    got_z = [swap(z[z.shape[0] // 2 :], 1) for z in z_parts]
    first, scale = call(
        functools.partial(sum_kernel, all_snaps), [chunk_shape, scale_shape],
        place, *scatter(sends[0]), tiles=True,
    )
    scales[0].append(scale)
    joint = ((LANES + TILE, LANES), F32)
    keep, send = call(
        functools.partial(last_kernel, all_snaps), [joint, joint],
        place, first, *scatter(sends[1]), *scales[0], *scales[1], tiles=True,
    )
    y, known = call(join_kernel, [((LANES, rank), F32), ((TILE, rank), F32)], place, keep, swap(send, 1))
    total = known + swap(known, 2)
    total = total + swap(total, 4)
    a, b = cell_pair(total)
    (z_out,) = call(z_out_kernel, [((width, rank), F32)], place, *z_parts, *got_z, known, plain=True)
    q_out, scale_out = call(
        functools.partial(q_out_kernel, all_cells),
        [((LANES, rank), F32), ((2 * ITERS + 1, rank), F32)],
        y, known, a, b, scalars=0, plain=True,
    )
    return q_out, z_out, scale_out


def solution(mesh):
    return jax.shard_map(
        local,
        mesh=mesh,
        in_specs=(P("cell", "snap"), P("snap", None)),
        out_specs=(P(("cell", "snap"), None), P("snap", None), P()),
        check_vma=False,
    )
```

```python
import functools

import jax
import jax.numpy as jnp
from jax import lax
from jax.experimental import pallas as pl
from jax.experimental.pallas import tpu as pltpu
from jax.sharding import PartitionSpec as P

ITERS = 2
EPS = 1e-05
LANES = 128
TILE = 8
HALVES = 2
QUARTER = 64
COLS = QUARTER // HALVES
SHARES = (3, 1)
BF16 = jnp.bfloat16
F32 = jnp.float32


def split(x):
    high = x.astype(BF16).astype(F32)
    return high, x - high


def dot(a, b):
    return lax.dot_general(a, b, (((1,), (0,)), ((), ())), preferred_element_type=F32)


def eye(cols):
    shape = (cols, LANES)
    return lax.broadcasted_iota(jnp.int32, shape, 0) == lax.broadcasted_iota(jnp.int32, shape, 1)


def to_column(row, cols):
    return jnp.sum(jnp.where(eye(cols), row, 0.0), axis=1, keepdims=True)


def to_row(column):
    return jnp.sum(jnp.where(eye(column.shape[0]), column, 0.0), axis=0, keepdims=True)


def squares_tile(x):
    row = to_row(jnp.sum(x * x, axis=1, keepdims=True))
    return jnp.broadcast_to(row, (TILE, LANES))


def rms(total, count):
    return jnp.sqrt(total / count + EPS)


def wide(x, cols):
    return jnp.concatenate([x[j * cols : (j + 1) * cols] for j in range(x.shape[0] // cols)], axis=1)


def store_blocks(ref, start, x):
    cols = x.shape[0]
    for j in range(x.shape[1] // LANES):
        ref[start + j * cols : start + (j + 1) * cols, :] = x[:, j * LANES : (j + 1) * LANES]


def turn(x, cols):
    return pltpu.roll(x, cols, 1)


def join_lanes(first, second, cols):
    left = lax.broadcasted_iota(jnp.int32, first.shape, 1) < cols
    return jnp.where(left, first, turn(second, cols))


def unfold(total):
    cols = total.shape[0] // 2
    return total[:cols] + total[cols:]


def sketch_side(place_ref, x):
    x = jnp.where(place_ref[0] == 0, x, turn(x, QUARTER))
    return join_lanes(*split(x), QUARTER).astype(BF16)


def store_factors(high_ref, low_ref, blocks):
    for s, block in enumerate(blocks):
        high, low = split(block)
        cut = slice(s * block.shape[1], (s + 1) * block.shape[1])
        high_ref[:, cut] = high.astype(BF16)
        low_ref[:, cut] = low.astype(BF16)


def prepare_kernel(place_ref, sketch_ref, a_ref, mine_ref, first_ref, sem):
    lead = sketch_ref.shape[0] // 2
    count = first_ref.shape[0] - lead
    copy = pltpu.make_async_copy(a_ref.at[pl.ds(0, count)], first_ref.at[pl.ds(lead, count)], sem)
    copy.start()
    near, far = sketch_ref[:, :LANES], sketch_ref[:, LANES:]
    low = join_lanes(near, far, QUARTER)
    high = join_lanes(turn(near, QUARTER), turn(far, QUARTER), QUARTER)
    zero = place_ref[1] == 0
    mine_ref[...] = jnp.where(zero, low, high)
    theirs = jnp.where(zero, high, low)
    first_ref[:lead, :LANES] = theirs[:lead]
    first_ref[:lead, LANES:] = theirs[lead:]
    copy.wait()


def near_kernel(place_ref, own_ref, core_ref, mine_ref, got_ref, y_ref, high_ref, low_ref, rest_ref):
    rest_ref[...] = own_ref[own_ref.shape[0] - rest_ref.shape[0] :, :]
    store_factors(high_ref, low_ref, (own_ref[...], core_ref[...]))
    rhs = jnp.concatenate([sketch_side(place_ref, ref[...]) for ref in (mine_ref, got_ref)], axis=0)
    for b in range(own_ref.shape[0] // LANES):
        cut = slice(b * LANES, (b + 1) * LANES)
        total = dot(high_ref[cut, :], rhs) + dot(low_ref[cut, :], rhs)
        y_ref[b * QUARTER : (b + 1) * QUARTER, :] = unfold(total.T)


def far_kernel(start, skip, place_ref, side_ref, diagonal_ref, *refs):
    sketches, (near_ref, y_ref, high_ref, low_ref) = refs[:-4], refs[-4:]
    if not sketches:
        sketches = (side_ref, diagonal_ref)
    store_factors(high_ref, low_ref, (side_ref[skip:, :], diagonal_ref[skip:, :]))
    rhs = []
    for ref in sketches:
        for s in range(2):
            rhs.append(sketch_side(place_ref, ref[:LANES, s * LANES : (s + 1) * LANES]))
    rhs = jnp.concatenate(rhs, axis=0)
    for b in range(high_ref.shape[0] // LANES):
        cut = slice(b * LANES, (b + 1) * LANES)
        total = dot(high_ref[cut, :], rhs) + dot(low_ref[cut, :], rhs)
        at = (start // LANES + b) * QUARTER
        y_ref[b * QUARTER : (b + 1) * QUARTER, :] = unfold(total.T) + near_ref[at : at + QUARTER, :]


def send_z(y, high_refs, low_refs, z_ref):
    lhs = jnp.concatenate(split(y), axis=0).astype(BF16)
    near = dot(lhs, high_refs[0][...]) + dot(lhs, low_refs[0][...])
    far, at = None, 0
    for high_ref, low_ref in zip(high_refs[1:], low_refs[1:]):
        cut = slice(at, at + high_ref.shape[0])
        term = dot(lhs[:, cut], high_ref[...]) + dot(lhs[:, cut], low_ref[...])
        far = term if far is None else far + term
        at += high_ref.shape[0]
    store_blocks(z_ref, 0, unfold(near))
    store_blocks(z_ref, (z_ref.shape[0] - TILE) // 2, unfold(far))
    z_ref[-TILE:, :] = squares_tile(y)


def factors(refs):
    count = len(SHARES) + 1
    return refs[:count], refs[count : 2 * count]


def first_z_kernel(h, *refs):
    count = len(SHARES)
    high, low = factors(refs[2 * count :])
    pieces = []
    for a_ref, b_ref in zip(refs[:count], refs[count : 2 * count]):
        for j in range(a_ref.shape[0] // QUARTER):
            cut = slice(j * QUARTER + h * COLS, j * QUARTER + (h + 1) * COLS)
            pieces.append(a_ref[cut, :] + b_ref[cut, :])
    send_z(jnp.concatenate(pieces, axis=1), high, low, refs[-1])


def scaled(own_ref, got_ref, count):
    total = own_ref[...] + got_ref[...]
    scale = rms(total[-TILE:], count)
    return wide(total[:-TILE], COLS) / to_column(scale[:1], COLS), scale


def z_kernel(count, *refs):
    high, low = factors(refs[2:])
    z_ref, scale_ref = refs[-2:]
    y, scale = scaled(refs[0], refs[1], count)
    scale_ref[...] = scale
    send_z(y, high, low, z_ref)


def y_kernel(count, *refs):
    high_refs, low_refs = factors(refs[2:])
    y_ref, scale_ref, *z_refs = refs[2 + 2 * len(high_refs) :]
    z, scale = scaled(refs[0], refs[1], count)
    scale_ref[...] = scale
    for z_ref in z_refs:
        store_blocks(z_ref, 0, z)
    y_ref[-TILE:, :] = squares_tile(z)
    rhs = jnp.concatenate(split(z), axis=0).T.astype(BF16)
    middle = rhs.shape[0] // 2
    at = 0
    for high_ref, low_ref in zip(high_refs[1:], low_refs[1:]):
        for b in range(high_ref.shape[0] // LANES):
            near = slice(at * LANES, (at + 1) * LANES)
            far = slice(b * LANES, (b + 1) * LANES)
            total = dot(high_refs[0][near, :], rhs[:middle]) + dot(low_refs[0][near, :], rhs[:middle])
            total += dot(high_ref[far, :], rhs[middle:]) + dot(low_ref[far, :], rhs[middle:])
            y_ref[at * COLS : (at + 1) * COLS, :] = unfold(total.T)
            at += 1


def end_kernel(count, carried, place_ref, own_ref, got_ref, *refs):
    parts, scales, (keep_ref, send_ref, y_ref) = refs[:carried], refs[carried:-3], refs[-3:]
    y, scale = scaled(own_ref, got_ref, count)
    store_blocks(y_ref, 0, y)
    row = lax.broadcasted_iota(jnp.int32, (TILE, LANES), 0)
    tail = squares_tile(y)
    for i, known in enumerate([ref[...] for ref in scales] + [scale]):
        tail = jnp.where(row == i, known, tail)
    size = 2 * COLS
    for ref, chip in ((keep_ref, place_ref[2]), (send_ref, place_ref[3])):
        start = pl.multiple_of(chip * size, size)
        ref[:size, :] = y_ref[pl.ds(start, size), :]
        ref[size : size + TILE, :] = tail
    at = size + TILE
    for ref in parts:
        middle = ref.shape[0] // 2
        send_ref[at : at + middle, :] = ref[middle:, :]
        at += middle


def core_kernel(place_ref, *refs):
    keeps, gots, parts = (refs[i * HALVES : (i + 1) * HALVES] for i in range(3))
    keep_ref, send_ref = refs[3 * HALVES :]
    zero_side, zero_core = place_ref[1] == 0, place_ref[0] == 0
    tail = None
    for s in range(2):
        for h in range(HALVES):
            a, b = keeps[h][...], gots[h][: keeps[h].shape[0], :]
            x = jnp.where(zero_side, a, b) if s == 0 else jnp.where(zero_side, b, a)
            first, second, known = x[:COLS], x[COLS : 2 * COLS], x[2 * COLS :]
            at = (s * HALVES + h) * COLS
            keep_ref[at : at + COLS, :] = jnp.where(zero_core, first, second)
            send_ref[at : at + COLS, :] = jnp.where(zero_core, second, first)
            tail = known if tail is None else join_lanes(tail, known, at)
    keep_ref[LANES : LANES + TILE, :] = tail
    send_ref[LANES : LANES + TILE, :] = tail
    size = 2 * COLS
    for h, ref in enumerate(parts):
        at = LANES + TILE + h * size
        send_ref[at : at + size, :] = ref[size : 2 * size, :]
        at += HALVES * size
        start = keeps[0].shape[0] + (2 * h + 1) * size
        send_ref[at : at + size, :] = gots[0][start : start + size, :]


def join_kernel(place_ref, keep_ref, got_ref, y_ref, known_ref):
    zero = place_ref[0] == 0
    keep, got = keep_ref[...], got_ref[: LANES + TILE, :]
    for s, x in enumerate((jnp.where(zero, keep, got), jnp.where(zero, got, keep))):
        cut = slice(s * LANES, (s + 1) * LANES)
        y_ref[:, cut] = x[:LANES].T
        known_ref[:, cut] = x[LANES:]


def z_out_kernel(place_ref, *refs):
    parts, (side_ref, core_ref, known_ref, z_ref) = refs[:HALVES], refs[HALVES:]
    zero_side, zero_core = place_ref[1] == 0, place_ref[0] == 0
    size = 2 * COLS
    side_at, core_at = size + TILE, LANES + TILE
    mine = [ref[:size, :] for ref in parts]
    side = [side_ref[side_at + 2 * h * size : side_at + (2 * h + 1) * size, :] for h in range(HALVES)]
    core = [core_ref[core_at + h * size : core_at + (h + 1) * size, :] for h in range(2 * HALVES)]

    def side_order(own, other):
        low = [jnp.where(zero_side, a, b) for a, b in zip(own, other)]
        high = [jnp.where(zero_side, b, a) for a, b in zip(own, other)]
        return jnp.concatenate([wide(x, COLS) for x in low + high], axis=0)

    ours, theirs = side_order(mine, side), side_order(core[:HALVES], core[HALVES:])
    for s, x in enumerate((jnp.where(zero_core, ours, theirs), jnp.where(zero_core, theirs, ours))):
        cut = slice(s * LANES, (s + 1) * LANES)
        z_ref[:, cut] = x.T / known_ref[2 * ITERS - 1 : 2 * ITERS, cut]


def q_out_kernel(count, y_ref, known_ref, a_ref, b_ref, q_ref, scale_ref):
    last = 2 * ITERS
    scale = rms((a_ref[...] + b_ref[...])[last : last + 1], count)
    q_ref[...] = y_ref[...] / scale
    scale_ref[:last, :] = known_ref[:last, :]
    scale_ref[last:, :] = scale


def call(kernel, outs, *args, scalars=1, plain=False, in_place=(), scratch=()):
    specs = [pl.BlockSpec(memory_space=pltpu.SMEM)] * scalars
    for i in range(scalars, len(args)):
        specs.append(pl.BlockSpec(memory_space=pltpu.HBM if i in in_place else pltpu.VMEM))
    out_spec = pl.BlockSpec() if plain else pl.BlockSpec(memory_space=pltpu.VMEM)
    return pl.pallas_call(
        kernel,
        out_shape=[jax.ShapeDtypeStruct(shape, dtype) for shape, dtype in outs],
        in_specs=specs,
        out_specs=[out_spec] * len(outs),
        scratch_shapes=scratch,
        compiler_params=pltpu.CompilerParams(vmem_limit_bytes=16 * 1024 * 1024),
    )(*args)


def general(snapshots, sketch):
    high = lax.Precision.HIGHEST
    all_cells = snapshots.shape[0] * lax.axis_size("cell")
    all_snaps = snapshots.shape[1] * lax.axis_size("snap")
    z, scales = sketch, []
    for section in range(ITERS + 1):
        partial = jnp.dot(snapshots, z, precision=high, preferred_element_type=F32)
        y = lax.psum_scatter(partial, "snap", scatter_dimension=0, tiled=True)
        scale = rms(lax.psum(jnp.sum(y * y, axis=0), ("cell", "snap")), all_cells)
        scales.append(scale)
        q = y / scale
        if section < ITERS:
            whole = lax.all_gather(q, "snap", axis=0, tiled=True)
            partial = jnp.dot(snapshots.T, whole, precision=high, preferred_element_type=F32)
            z = lax.psum(partial, "cell")
            scale = rms(lax.psum(jnp.sum(z * z, axis=0), "snap"), all_snaps)
            scales.append(scale)
            z = z / scale
    return q, z, jnp.stack(scales)


def local(snapshots, sketch):
    groups = lax.axis_size("cell")
    places = lax.axis_size("snap")
    rows, width = snapshots.shape
    rank = sketch.shape[1]
    fits = groups == 4 and places == 8 and rank == 4 * QUARTER and rows == 8 * LANES and width == 2 * LANES
    if not fits:
        return general(snapshots, sketch)
    all_cells = rows * groups
    all_snaps = width * places
    seat = lax.axis_index("snap")
    chip = seat // 2
    place = jnp.stack([seat % 2, chip % 2, chip, chip ^ 1]).astype(jnp.int32)

    def swap(x, bits):
        return lax.ppermute(x, "snap", [(i, i ^ bits) for i in range(places)])

    swap_core = functools.partial(swap, bits=1)
    swap_side = functools.partial(swap, bits=2)
    swap_pair = functools.partial(swap, bits=4)

    def swap_cell(x, step):
        def target(cell, i):
            return cell ^ (1 if i % 2 == step else 2)

        perm = [(c * places + i, target(c, i) * places + i) for c in range(groups) for i in range(places)]
        return lax.ppermute(x, ("cell", "snap"), perm)

    def cell_pair(x):
        x = x + swap_cell(x, 0)
        return x, swap_cell(x, 1)

    sizes = [n * rows // sum(SHARES) for n in SHARES]
    lead = width // 2

    def factor(count):
        return [((count, 2 * width), BF16)] * 2

    mine, first = call(
        prepare_kernel, [((width, LANES), F32), ((lead + sizes[0], width), F32)],
        place, sketch, snapshots, in_place=(2,), scratch=[pltpu.SemaphoreType.DMA],
    )
    side_first = swap_side(first)
    near_y, near_high, near_low, rest = call(
        near_kernel,
        [((rows // LANES * QUARTER, LANES), F32)] + factor(rows) + [((sizes[1], width), F32)],
        place, snapshots, swap_core(snapshots), mine, swap_core(mine),
    )
    side_rest = swap_side(rest)
    side_first, near_y = lax.optimization_barrier((side_first, near_y))
    core_first = swap_core(side_first)
    own_first, high_first, low_first = call(
        functools.partial(far_kernel, 0, lead),
        [((sizes[0] // LANES * QUARTER, LANES), F32)] + factor(sizes[0]),
        place, side_first, core_first, near_y,
    )
    side_rest, own_first = lax.optimization_barrier((side_rest, own_first))
    own_rest, high_rest, low_rest = call(
        functools.partial(far_kernel, sizes[0], 0),
        [((sizes[1] // LANES * QUARTER, LANES), F32)] + factor(sizes[1]),
        place, side_rest, swap_core(side_rest), side_first, core_first, near_y,
    )
    matrix = (near_high, high_first, high_rest, near_low, low_first, low_rest)
    own = (own_first, own_rest)
    got = tuple(swap_pair(y) for y in own)

    flat = (COLS * rows // LANES + TILE, LANES)
    sent_shape = ((COLS * 4 * width // LANES + TILE, LANES), F32)
    y_shape = (flat, F32)
    scale_shape = ((TILE, LANES), F32)
    z_shape = ((COLS * 4 * width // LANES, LANES), F32)
    scales = [[] for _ in range(HALVES)]
    sent = [
        call(functools.partial(first_z_kernel, h), [sent_shape], *own, *got, *matrix, scalars=0)[0]
        for h in range(HALVES)
    ]
    ys, zs = [None] * HALVES, [None] * HALVES
    for section in range(ITERS):
        last = section == ITERS - 1
        for h in range(HALVES):
            ys[h], scale, *z = call(
                functools.partial(y_kernel, all_cells), [y_shape, scale_shape] + [z_shape] * last,
                *cell_pair(sent[h]), *matrix, scalars=0,
            )
            scales[h].append(scale)
            if last:
                zs[h] = z[0]
                continue
            sent[h], scale = call(
                functools.partial(z_kernel, all_snaps), [sent_shape, scale_shape],
                ys[h], swap_pair(ys[h]), *matrix, scalars=0,
            )
            scales[h].append(scale)

    small = (2 * COLS + TILE, LANES)
    carried = HALVES * z_shape[0][0] // 2
    keeps, gots = [], []
    for h in range(HALVES):
        parts = zs if h == 0 else []
        keep, send, _ = call(
            functools.partial(end_kernel, all_snaps, len(parts)),
            [(small, F32), ((small[0] + carried * (h == 0), LANES), F32), ((flat[0] - TILE, LANES), F32)],
            place, ys[h], swap_pair(ys[h]), *parts, *scales[h],
        )
        keeps.append(keep)
        gots.append(swap_side(send))
    keep, send = call(
        core_kernel, [((LANES + TILE, LANES), F32), ((LANES + TILE + carried, LANES), F32)],
        place, *keeps, *gots, *zs,
    )
    core_got = swap_core(send)
    y, known = call(join_kernel, [((LANES, rank), F32), ((TILE, rank), F32)], place, keep, core_got)
    a, b = cell_pair(known)
    (z_out,) = call(z_out_kernel, [((width, rank), F32)], place, *zs, gots[0], core_got, known, plain=True)
    q_out, scale_out = call(
        functools.partial(q_out_kernel, all_cells),
        [((LANES, rank), F32), ((2 * ITERS + 1, rank), F32)],
        y, known, a, b, scalars=0, plain=True,
    )
    return q_out, z_out, scale_out


def solution(mesh):
    return jax.shard_map(
        local,
        mesh=mesh,
        in_specs=(P("cell", "snap"), P("snap", None)),
        out_specs=(P(("cell", "snap"), None), P("snap", None), P()),
        check_vma=False,
    )
```

```python
import functools

import jax
import jax.numpy as jnp
from jax import lax
from jax.experimental import pallas as pl
from jax.experimental.pallas import tpu as pltpu
from jax.sharding import PartitionSpec as P

ITERS = 2
EPS = 1e-05
LANES = 128
TILE = 8
CHIPS = 4
GROUPS = 4
HALVES = 2
BF16 = jnp.bfloat16
F32 = jnp.float32


def split(x):
    high = x.astype(BF16).astype(F32)
    return high, x - high


def dot(a, b):
    return lax.dot_general(a, b, (((1,), (0,)), ((), ())), preferred_element_type=F32)


def eye(cols):
    shape = (cols, LANES)
    return lax.broadcasted_iota(jnp.int32, shape, 0) == lax.broadcasted_iota(jnp.int32, shape, 1)


def to_column(row, cols):
    return jnp.sum(jnp.where(eye(cols), row, 0.0), axis=1, keepdims=True)


def to_row(column):
    return jnp.sum(jnp.where(eye(column.shape[0]), column, 0.0), axis=0, keepdims=True)


def squares_tile(x):
    row = to_row(jnp.sum(x * x, axis=1, keepdims=True))
    return jnp.broadcast_to(row, (TILE, LANES))


def rms(total, count):
    return jnp.sqrt(total / count + EPS)


def wide(x, cols):
    return jnp.concatenate([x[j * cols : (j + 1) * cols] for j in range(x.shape[0] // cols)], axis=1)


def store_blocks(ref, x):
    cols = x.shape[0]
    for j in range(x.shape[1] // LANES):
        ref[j * cols : (j + 1) * cols, :] = x[:, j * LANES : (j + 1) * LANES]


def turn(x, cols):
    return pltpu.roll(x, cols, 1)


def join_lanes(first, second, cols):
    left = lax.broadcasted_iota(jnp.int32, first.shape, 1) < cols
    return jnp.where(left, first, turn(second, cols))


def chunk_at(place_ref, other):
    return place_ref[0] ^ other


def ordered_tiles(place_ref, tiles, scratch_ref):
    for other, tile in enumerate(tiles):
        start = pl.multiple_of(chunk_at(place_ref, other) * TILE, TILE)
        scratch_ref[pl.ds(start, TILE), :] = tile
    total = scratch_ref[:TILE, :]
    for i in range(1, CHIPS):
        total += scratch_ref[i * TILE : (i + 1) * TILE, :]
    return total


def chunk_product(place_ref, other, rows, rhs, high_ref, low_ref):
    cut = pl.ds(pl.multiple_of(chunk_at(place_ref, other) * rows, rows), rows)
    total = dot(high_ref[cut, :], rhs) + dot(low_ref[cut, :], rhs)
    return total


def first_kernel(place_ref, own_ref, core_ref, near_ref, got_ref, *refs):
    sends, (high_ref, low_ref) = refs[:-2], refs[-2:]
    width = own_ref.shape[1]
    rows = own_ref.shape[0] // CHIPS
    for b in range(own_ref.shape[0] // LANES):
        cut = slice(b * LANES, (b + 1) * LANES)
        for s, ref in enumerate((own_ref, core_ref)):
            high, low = split(ref[cut, :])
            high_ref[cut, s * width : (s + 1) * width] = high.astype(BF16)
            low_ref[cut, s * width : (s + 1) * width] = low.astype(BF16)
    z = jnp.concatenate([near_ref[...], got_ref[...]], axis=0)
    rhs = jnp.concatenate(split(z), axis=1).astype(BF16)
    cols = LANES // HALVES
    for other in range(CHIPS):
        total = chunk_product(place_ref, other, rows, rhs, high_ref, low_ref)
        y = (total[:, :LANES] + total[:, LANES:]).T
        for h in range(HALVES):
            ref = sends[h * CHIPS + other]
            store_blocks(ref, y[h * cols : (h + 1) * cols])
            ref[-TILE:, :] = jnp.zeros((TILE, LANES), F32)


def chunk_sum(count, place_ref, refs, scratch_ref):
    cols = LANES // HALVES
    total = refs[0][:-TILE, :]
    for ref in refs[1:]:
        total += ref[:-TILE, :]
    y = wide(total, cols)
    if count is None:
        return y, None
    scale = rms(ordered_tiles(place_ref, [ref[-TILE:, :] for ref in refs], scratch_ref), count)
    return y / to_column(scale[:1], cols), scale


def sum_kernel(count, place_ref, *refs):
    parts, outs, scratch_ref = refs[:CHIPS], refs[CHIPS:-1], refs[-1]
    y, scale = chunk_sum(count, place_ref, parts, scratch_ref)
    store_blocks(outs[0], y)
    outs[0][-TILE:, :] = squares_tile(y)
    if scale is not None:
        outs[1][...] = scale


def z_kernel(place_ref, *refs):
    parts, (high_ref, low_ref, z_ref, scratch_ref) = refs[:CHIPS], refs[CHIPS:]
    cols = LANES // HALVES
    rows = high_ref.shape[0] // CHIPS
    z = None
    for other, ref in enumerate(parts):
        y = wide(ref[:-TILE, :], cols)
        lhs = jnp.concatenate(split(y), axis=0).astype(BF16)
        cut = pl.ds(pl.multiple_of(chunk_at(place_ref, other) * rows, rows), rows)
        term = dot(lhs, high_ref[cut, :]) + dot(lhs, low_ref[cut, :])
        z = term if z is None else z + term
    store_blocks(z_ref, z[:cols] + z[cols:])
    z_ref[-TILE:, :] = ordered_tiles(place_ref, [ref[-TILE:, :] for ref in parts], scratch_ref)


def y_kernel(count, place_ref, a_ref, b_ref, high_ref, low_ref, *refs):
    sends, scale_ref, z_refs = refs[:CHIPS], refs[CHIPS], refs[CHIPS + 1 :]
    cols = LANES // HALVES
    rows = high_ref.shape[0] // CHIPS
    total = a_ref[...] + b_ref[...]
    scale = rms(total[-TILE:], count)
    scale_ref[...] = scale
    z = wide(total[:-TILE], cols) / to_column(scale[:1], cols)
    for z_ref in z_refs:
        store_blocks(z_ref, z)
    tail = squares_tile(z)
    rhs = jnp.concatenate(split(z), axis=0).T.astype(BF16)
    for other, ref in enumerate(sends):
        y = chunk_product(place_ref, other, rows, rhs, high_ref, low_ref).T
        store_blocks(ref, y[:cols] + y[cols:])
        ref[-TILE:, :] = tail


def last_kernel(count, place_ref, first_ref, *refs):
    parts, scales = refs[:CHIPS], refs[CHIPS:-3]
    keep_ref, send_ref, scratch_ref = refs[-3:]
    cols = LANES // HALVES
    y, scale = chunk_sum(count, place_ref, parts, scratch_ref)
    middle = (len(scales) + 1) // 2
    row = lax.broadcasted_iota(jnp.int32, (TILE, LANES), 0)
    tail = join_lanes(first_ref[-TILE:, :], squares_tile(y), cols)
    second = [ref[...] for ref in scales[middle:]] + [scale]
    for i, (a_ref, b) in enumerate(zip(scales[:middle], second)):
        tail = jnp.where(row == i, join_lanes(a_ref[...], b, cols), tail)
    zero = place_ref[1] == 0
    blocks = ((first_ref[:cols, :], first_ref[cols : 2 * cols, :]), (y[:, :LANES], y[:, LANES:]))
    for h, (a, b) in enumerate(blocks):
        cut = slice(h * cols, (h + 1) * cols)
        keep_ref[cut, :] = jnp.where(zero, a, b)
        send_ref[cut, :] = jnp.where(zero, b, a)
    keep_ref[-TILE:, :] = tail
    send_ref[-TILE:, :] = tail


def join_kernel(place_ref, keep_ref, got_ref, y_ref, known_ref):
    zero = place_ref[1] == 0
    keep, got = keep_ref[...], got_ref[...]
    for s, x in enumerate((jnp.where(zero, keep, got), jnp.where(zero, got, keep))):
        cut = slice(s * LANES, (s + 1) * LANES)
        y_ref[:, cut] = x[:LANES].T
        known_ref[:, cut] = x[LANES:]


def z_out_kernel(place_ref, first_ref, second_ref, got_first_ref, got_second_ref, known_ref, z_ref):
    cols = LANES // HALVES
    zero = place_ref[1] == 0
    own_rows = first_ref.shape[0] // 2
    mine = jnp.concatenate([wide(ref[:own_rows, :], cols) for ref in (first_ref, second_ref)], axis=0)
    theirs = jnp.concatenate([wide(ref[...], cols) for ref in (got_first_ref, got_second_ref)], axis=0)
    for s, x in enumerate((jnp.where(zero, mine, theirs), jnp.where(zero, theirs, mine))):
        cut = slice(s * LANES, (s + 1) * LANES)
        z_ref[:, cut] = x.T / known_ref[2 * ITERS - 1 : 2 * ITERS, cut]


def q_out_kernel(count, y_ref, known_ref, a_ref, b_ref, q_ref, scale_ref):
    last = 2 * ITERS
    scale = rms((a_ref[...] + b_ref[...])[last : last + 1], count)
    q_ref[...] = y_ref[...] / scale
    scale_ref[:last, :] = known_ref[:last, :]
    scale_ref[last:, :] = scale


def call(kernel, outs, *args, scalars=1, plain=False, tiles=False):
    specs = [pl.BlockSpec(memory_space=pltpu.SMEM)] * scalars
    specs += [pl.BlockSpec(memory_space=pltpu.VMEM)] * (len(args) - scalars)
    out_spec = pl.BlockSpec() if plain else pl.BlockSpec(memory_space=pltpu.VMEM)
    return pl.pallas_call(
        kernel,
        out_shape=[jax.ShapeDtypeStruct(shape, dtype) for shape, dtype in outs],
        in_specs=specs,
        out_specs=[out_spec] * len(outs),
        scratch_shapes=[pltpu.VMEM((CHIPS * TILE, LANES), F32)] if tiles else [],
        compiler_params=pltpu.CompilerParams(vmem_limit_bytes=16 * 1024 * 1024),
    )(*args)


def general(snapshots, sketch):
    high = lax.Precision.HIGHEST
    all_cells = snapshots.shape[0] * lax.axis_size("cell")
    all_snaps = snapshots.shape[1] * lax.axis_size("snap")
    z, scales = sketch, []
    for section in range(ITERS + 1):
        partial = jnp.dot(snapshots, z, precision=high, preferred_element_type=F32)
        y = lax.psum_scatter(partial, "snap", scatter_dimension=0, tiled=True)
        scale = rms(lax.psum(jnp.sum(y * y, axis=0), ("cell", "snap")), all_cells)
        scales.append(scale)
        q = y / scale
        if section < ITERS:
            whole = lax.all_gather(q, "snap", axis=0, tiled=True)
            partial = jnp.dot(snapshots.T, whole, precision=high, preferred_element_type=F32)
            z = lax.psum(partial, "cell")
            scale = rms(lax.psum(jnp.sum(z * z, axis=0), "snap"), all_snaps)
            scales.append(scale)
            z = z / scale
    return q, z, jnp.stack(scales)


def local(snapshots, sketch):
    groups = lax.axis_size("cell")
    places = lax.axis_size("snap")
    rows, width = snapshots.shape
    rank = sketch.shape[1]
    if groups != GROUPS or places != 2 * CHIPS or rank != 2 * LANES or rows % (CHIPS * LANES) or width % LANES:
        return general(snapshots, sketch)
    cols = LANES // HALVES
    all_cells = rows * groups
    all_snaps = width * places
    seat = lax.axis_index("snap")
    core, chip = seat % 2, seat // 2
    place = jnp.stack([chip, core]).astype(jnp.int32)

    def swap(x, bits):
        return lax.ppermute(x, "snap", [(i, i ^ bits) for i in range(places)])

    def swap_cell(x, step):
        def target(cell, i):
            return cell ^ (1 if i % 2 == step else 2)

        perm = [(c * places + i, target(c, i) * places + i) for c in range(groups) for i in range(places)]
        return lax.ppermute(x, ("cell", "snap"), perm)

    def cell_pair(x):
        x = x + swap_cell(x, 0)
        return x, swap_cell(x, 1)

    def scatter(parts):
        return [parts[0]] + [swap(parts[d], 2 * d) for d in range(1, CHIPS)]

    def gather(part):
        return [part] + [swap(part, 2 * d) for d in range(1, CHIPS)]

    def sketch_half(index):
        return lax.dynamic_slice_in_dim(sketch, index * LANES, LANES, 1)

    chunk_shape = ((cols * rows // CHIPS // LANES + TILE, LANES), F32)
    z_shape = ((cols * 2 * width // LANES + TILE, LANES), F32)
    out_shape = ((cols * 2 * width // LANES, LANES), F32)
    scale_shape = ((TILE, LANES), F32)
    factor = ((rows, 2 * width), BF16)

    *parts, high, low = call(
        first_kernel,
        [chunk_shape] * (HALVES * CHIPS) + [factor, factor],
        place, snapshots, swap(snapshots, 1), sketch_half(core), swap(sketch_half(1 - core), 1),
    )
    sends = [parts[h * CHIPS : (h + 1) * CHIPS] for h in range(HALVES)]
    scales = [[] for _ in range(HALVES)]
    z_parts = [None] * HALVES
    for section in range(ITERS):
        for h in range(HALVES):
            count = all_snaps if section else None
            y, *scale = call(
                functools.partial(sum_kernel, count),
                [chunk_shape] + [scale_shape] * (section > 0),
                place, *scatter(sends[h]), tiles=True,
            )
            scales[h] += scale
            (z,) = call(z_kernel, [z_shape], place, *gather(y), high, low, tiles=True)
            last = section == ITERS - 1
            *sends[h], scale = call(
                functools.partial(y_kernel, all_cells),
                [chunk_shape] * CHIPS + [scale_shape] + [out_shape] * last,
                place, *cell_pair(z), high, low,
            )[: CHIPS + 1 + last]
            if last:
                scale, z_parts[h] = sends[h].pop(), scale
            scales[h].append(scale)

    got_z = [swap(z[z.shape[0] // 2 :], 1) for z in z_parts]
    first, scale = call(
        functools.partial(sum_kernel, all_snaps), [chunk_shape, scale_shape],
        place, *scatter(sends[0]), tiles=True,
    )
    scales[0].append(scale)
    joint = ((LANES + TILE, LANES), F32)
    keep, send = call(
        functools.partial(last_kernel, all_snaps), [joint, joint],
        place, first, *scatter(sends[1]), *scales[0], *scales[1], tiles=True,
    )
    y, known = call(join_kernel, [((LANES, rank), F32), ((TILE, rank), F32)], place, keep, swap(send, 1))
    total = known + swap(known, 2)
    total = total + swap(total, 4)
    a, b = cell_pair(total)
    (z_out,) = call(z_out_kernel, [((width, rank), F32)], place, *z_parts, *got_z, known, plain=True)
    q_out, scale_out = call(
        functools.partial(q_out_kernel, all_cells),
        [((LANES, rank), F32), ((2 * ITERS + 1, rank), F32)],
        y, known, a, b, scalars=0, plain=True,
    )
    return q_out, z_out, scale_out


def solution(mesh):
    return jax.shard_map(
        local,
        mesh=mesh,
        in_specs=(P("cell", "snap"), P("snap", None)),
        out_specs=(P(("cell", "snap"), None), P("snap", None), P()),
        check_vma=False,
    )
```

```python
import functools

import jax
import jax.numpy as jnp
from jax import lax
from jax.experimental import pallas as pl
from jax.experimental.pallas import tpu as pltpu
from jax.sharding import PartitionSpec as P

ITERS = 2
EPS = 1e-05
LANES = 128
TILE = 8
HALVES = 2
QUARTER = 64
COLS = QUARTER // HALVES
BLOCKS = 3
BF16 = jnp.bfloat16
F32 = jnp.float32


def split(x):
    high = x.astype(BF16).astype(F32)
    return high, x - high


def dot(a, b):
    return lax.dot_general(a, b, (((1,), (0,)), ((), ())), preferred_element_type=F32)


def eye(cols):
    shape = (cols, LANES)
    return lax.broadcasted_iota(jnp.int32, shape, 0) == lax.broadcasted_iota(jnp.int32, shape, 1)


def to_column(row, cols):
    return jnp.sum(jnp.where(eye(cols), row, 0.0), axis=1, keepdims=True)


def to_row(column):
    return jnp.sum(jnp.where(eye(column.shape[0]), column, 0.0), axis=0, keepdims=True)


def squares_tile(x):
    row = to_row(jnp.sum(x * x, axis=1, keepdims=True))
    return jnp.broadcast_to(row, (TILE, LANES))


def rms(total, count):
    return jnp.sqrt(total / count + EPS)


def wide(x, cols):
    return jnp.concatenate([x[j * cols : (j + 1) * cols] for j in range(x.shape[0] // cols)], axis=1)


def store_blocks(ref, start, x):
    cols = x.shape[0]
    for j in range(x.shape[1] // LANES):
        ref[start + j * cols : start + (j + 1) * cols, :] = x[:, j * LANES : (j + 1) * LANES]


def turn(x, cols):
    return pltpu.roll(x, cols, 1)


def join_lanes(first, second, cols):
    left = lax.broadcasted_iota(jnp.int32, first.shape, 1) < cols
    return jnp.where(left, first, turn(second, cols))


def unfold(total):
    cols = total.shape[0] // 2
    return total[:cols] + total[cols:]


def sketch_side(place_ref, x):
    x = jnp.where(place_ref[0] == 0, x, turn(x, QUARTER))
    return join_lanes(*split(x), QUARTER).astype(BF16)


def store_factors(high_ref, low_ref, blocks):
    for s, block in enumerate(blocks):
        high, low = split(block)
        cut = slice(s * block.shape[1], (s + 1) * block.shape[1])
        high_ref[:, cut] = high.astype(BF16)
        low_ref[:, cut] = low.astype(BF16)


def prepare_kernel(place_ref, sketch_ref, mine_ref, theirs_ref):
    near, far = sketch_ref[:, :LANES], sketch_ref[:, LANES:]
    low = join_lanes(near, far, QUARTER)
    high = join_lanes(turn(near, QUARTER), turn(far, QUARTER), QUARTER)
    zero = place_ref[1] == 0
    mine_ref[...] = jnp.where(zero, low, high)
    theirs_ref[...] = jnp.where(zero, high, low)


def near_kernel(place_ref, own_ref, core_ref, mine_ref, got_ref, y_ref, high_ref, low_ref):
    store_factors(high_ref, low_ref, (own_ref[...], core_ref[...]))
    rhs = jnp.concatenate([sketch_side(place_ref, ref[...]) for ref in (mine_ref, got_ref)], axis=0)
    for b in range(own_ref.shape[0] // LANES):
        cut = slice(b * LANES, (b + 1) * LANES)
        total = dot(high_ref[cut, :], rhs) + dot(low_ref[cut, :], rhs)
        y_ref[b * QUARTER : (b + 1) * QUARTER, :] = unfold(total.T)


def split_kernel(side_ref, high_ref, low_ref):
    store_factors(high_ref, low_ref, (side_ref[...],))


def far_kernel(place_ref, high_side_ref, low_side_ref, diagonal_ref, sketch_ref, core_sketch_ref, near_ref, *refs):
    *halves, high_ref, low_ref = refs
    store_factors(high_ref, low_ref, (diagonal_ref[...],))
    side = sketch_side(place_ref, sketch_ref[...])
    diagonal = sketch_side(place_ref, core_sketch_ref[...])
    for b in range(high_ref.shape[0] // LANES):
        cut = slice(b * LANES, (b + 1) * LANES)
        total = dot(high_side_ref[cut, :], side) + dot(low_side_ref[cut, :], side)
        total += dot(high_ref[cut, :], diagonal) + dot(low_ref[cut, :], diagonal)
        y = unfold(total.T) + near_ref[b * QUARTER : (b + 1) * QUARTER, :]
        for h, ref in enumerate(halves):
            ref[b * COLS : (b + 1) * COLS, :] = y[h * COLS : (h + 1) * COLS]


def send_z(y, high_refs, low_refs, z_ref):
    lhs = jnp.concatenate(split(y), axis=0).astype(BF16)
    at = 0
    for high_ref, low_ref in zip(high_refs, low_refs):
        z = unfold(dot(lhs, high_ref[...]) + dot(lhs, low_ref[...]))
        store_blocks(z_ref, at, z)
        at += z.size // LANES
    z_ref[-TILE:, :] = squares_tile(y)


def factors(refs):
    return refs[:BLOCKS], refs[BLOCKS : 2 * BLOCKS]


def first_z_kernel(a_ref, b_ref, *refs):
    high, low = factors(refs)
    send_z(wide(a_ref[...] + b_ref[...], COLS), high, low, refs[-1])


def scaled(own_ref, got_ref, count):
    total = own_ref[...] + got_ref[...]
    scale = rms(total[-TILE:], count)
    return wide(total[:-TILE], COLS) / to_column(scale[:1], COLS), scale


def z_kernel(count, *refs):
    high, low = factors(refs[2:])
    z_ref, scale_ref = refs[-2:]
    y, scale = scaled(refs[0], refs[1], count)
    scale_ref[...] = scale
    send_z(y, high, low, z_ref)


def y_kernel(count, *refs):
    high_refs, low_refs = factors(refs[2:])
    y_ref, scale_ref, *z_refs = refs[2 + 2 * len(high_refs) :]
    z, scale = scaled(refs[0], refs[1], count)
    scale_ref[...] = scale
    for z_ref in z_refs:
        store_blocks(z_ref, 0, z)
    y_ref[-TILE:, :] = squares_tile(z)
    rhs = jnp.concatenate(split(z), axis=0).T.astype(BF16)
    for b in range(high_refs[0].shape[0] // LANES):
        cut = slice(b * LANES, (b + 1) * LANES)
        total, at = None, 0
        for high_ref, low_ref in zip(high_refs, low_refs):
            part = rhs[at : at + high_ref.shape[1]]
            term = dot(high_ref[cut, :], part) + dot(low_ref[cut, :], part)
            total = term if total is None else total + term
            at += high_ref.shape[1]
        y_ref[b * COLS : (b + 1) * COLS, :] = unfold(total.T)


def end_kernel(count, carried, place_ref, own_ref, got_ref, *refs):
    parts, scales, (keep_ref, send_ref, y_ref) = refs[:carried], refs[carried:-3], refs[-3:]
    y, scale = scaled(own_ref, got_ref, count)
    store_blocks(y_ref, 0, y)
    row = lax.broadcasted_iota(jnp.int32, (TILE, LANES), 0)
    tail = squares_tile(y)
    for i, known in enumerate([ref[...] for ref in scales] + [scale]):
        tail = jnp.where(row == i, known, tail)
    size = 2 * COLS
    for ref, chip in ((keep_ref, place_ref[2]), (send_ref, place_ref[3])):
        start = pl.multiple_of(chip * size, size)
        ref[:size, :] = y_ref[pl.ds(start, size), :]
        ref[size : size + TILE, :] = tail
    at = size + TILE
    for ref in parts:
        middle = ref.shape[0] // 2
        send_ref[at : at + middle, :] = ref[middle:, :]
        at += middle


def core_kernel(place_ref, *refs):
    keeps, gots, parts = (refs[i * HALVES : (i + 1) * HALVES] for i in range(3))
    keep_ref, send_ref = refs[3 * HALVES :]
    zero_side, zero_core = place_ref[1] == 0, place_ref[0] == 0
    tail = None
    for s in range(2):
        for h in range(HALVES):
            a, b = keeps[h][...], gots[h][: keeps[h].shape[0], :]
            x = jnp.where(zero_side, a, b) if s == 0 else jnp.where(zero_side, b, a)
            first, second, known = x[:COLS], x[COLS : 2 * COLS], x[2 * COLS :]
            at = (s * HALVES + h) * COLS
            keep_ref[at : at + COLS, :] = jnp.where(zero_core, first, second)
            send_ref[at : at + COLS, :] = jnp.where(zero_core, second, first)
            tail = known if tail is None else join_lanes(tail, known, at)
    keep_ref[LANES : LANES + TILE, :] = tail
    send_ref[LANES : LANES + TILE, :] = tail
    size = 2 * COLS
    for h, ref in enumerate(parts):
        at = LANES + TILE + h * size
        send_ref[at : at + size, :] = ref[size : 2 * size, :]
        at += HALVES * size
        start = keeps[0].shape[0] + (2 * h + 1) * size
        send_ref[at : at + size, :] = gots[0][start : start + size, :]


def join_kernel(place_ref, keep_ref, got_ref, y_ref, known_ref):
    zero = place_ref[0] == 0
    keep, got = keep_ref[...], got_ref[: LANES + TILE, :]
    for s, x in enumerate((jnp.where(zero, keep, got), jnp.where(zero, got, keep))):
        cut = slice(s * LANES, (s + 1) * LANES)
        y_ref[:, cut] = x[:LANES].T
        known_ref[:, cut] = x[LANES:]


def z_out_kernel(place_ref, *refs):
    parts, (side_ref, core_ref, known_ref, z_ref) = refs[:HALVES], refs[HALVES:]
    zero_side, zero_core = place_ref[1] == 0, place_ref[0] == 0
    size = 2 * COLS
    side_at, core_at = size + TILE, LANES + TILE
    mine = [ref[:size, :] for ref in parts]
    side = [side_ref[side_at + 2 * h * size : side_at + (2 * h + 1) * size, :] for h in range(HALVES)]
    core = [core_ref[core_at + h * size : core_at + (h + 1) * size, :] for h in range(2 * HALVES)]

    def side_order(own, other):
        low = [jnp.where(zero_side, a, b) for a, b in zip(own, other)]
        high = [jnp.where(zero_side, b, a) for a, b in zip(own, other)]
        return jnp.concatenate([wide(x, COLS) for x in low + high], axis=0)

    ours, theirs = side_order(mine, side), side_order(core[:HALVES], core[HALVES:])
    for s, x in enumerate((jnp.where(zero_core, ours, theirs), jnp.where(zero_core, theirs, ours))):
        cut = slice(s * LANES, (s + 1) * LANES)
        z_ref[:, cut] = x.T / known_ref[2 * ITERS - 1 : 2 * ITERS, cut]


def q_out_kernel(count, y_ref, known_ref, a_ref, b_ref, q_ref, scale_ref):
    last = 2 * ITERS
    scale = rms((a_ref[...] + b_ref[...])[last : last + 1], count)
    q_ref[...] = y_ref[...] / scale
    scale_ref[:last, :] = known_ref[:last, :]
    scale_ref[last:, :] = scale


def call(kernel, outs, *args, scalars=1, plain=False):
    specs = [pl.BlockSpec(memory_space=pltpu.SMEM)] * scalars
    specs += [pl.BlockSpec(memory_space=pltpu.VMEM)] * (len(args) - scalars)
    out_spec = pl.BlockSpec() if plain else pl.BlockSpec(memory_space=pltpu.VMEM)
    return pl.pallas_call(
        kernel,
        out_shape=[jax.ShapeDtypeStruct(shape, dtype) for shape, dtype in outs],
        in_specs=specs,
        out_specs=[out_spec] * len(outs),
        compiler_params=pltpu.CompilerParams(vmem_limit_bytes=16 * 1024 * 1024),
    )(*args)


def general(snapshots, sketch):
    high = lax.Precision.HIGHEST
    all_cells = snapshots.shape[0] * lax.axis_size("cell")
    all_snaps = snapshots.shape[1] * lax.axis_size("snap")
    z, scales = sketch, []
    for section in range(ITERS + 1):
        partial = jnp.dot(snapshots, z, precision=high, preferred_element_type=F32)
        y = lax.psum_scatter(partial, "snap", scatter_dimension=0, tiled=True)
        scale = rms(lax.psum(jnp.sum(y * y, axis=0), ("cell", "snap")), all_cells)
        scales.append(scale)
        q = y / scale
        if section < ITERS:
            whole = lax.all_gather(q, "snap", axis=0, tiled=True)
            partial = jnp.dot(snapshots.T, whole, precision=high, preferred_element_type=F32)
            z = lax.psum(partial, "cell")
            scale = rms(lax.psum(jnp.sum(z * z, axis=0), "snap"), all_snaps)
            scales.append(scale)
            z = z / scale
    return q, z, jnp.stack(scales)


def local(snapshots, sketch):
    groups = lax.axis_size("cell")
    places = lax.axis_size("snap")
    rows, width = snapshots.shape
    rank = sketch.shape[1]
    fits = groups == 4 and places == 8 and rank == 4 * QUARTER and rows == 8 * LANES and width == 2 * LANES
    if not fits:
        return general(snapshots, sketch)
    all_cells = rows * groups
    all_snaps = width * places
    seat = lax.axis_index("snap")
    chip = seat // 2
    place = jnp.stack([seat % 2, chip % 2, chip, chip ^ 1]).astype(jnp.int32)

    def swap(x, bits):
        return lax.ppermute(x, "snap", [(i, i ^ bits) for i in range(places)])

    swap_core = functools.partial(swap, bits=1)
    swap_side = functools.partial(swap, bits=2)
    swap_pair = functools.partial(swap, bits=4)

    def swap_cell(x, step):
        def target(cell, i):
            return cell ^ (1 if i % 2 == step else 2)

        perm = [(c * places + i, target(c, i) * places + i) for c in range(groups) for i in range(places)]
        return lax.ppermute(x, ("cell", "snap"), perm)

    def cell_pair(x):
        x = x + swap_cell(x, 0)
        return x, swap_cell(x, 1)

    def factor(count):
        return [((rows, count * width), BF16)] * 2

    side_block = swap_side(snapshots)
    packed = ((width, LANES), F32)
    mine, theirs = call(prepare_kernel, [packed, packed], place, sketch)
    near_y, *near = call(
        near_kernel, [((rows // LANES * QUARTER, LANES), F32)] + factor(2),
        place, snapshots, swap_core(snapshots), mine, swap_core(mine),
    )
    side_sketch = swap_side(theirs)
    side_block, near_y = lax.optimization_barrier((side_block, near_y))
    side = call(split_kernel, factor(1), side_block, scalars=0)
    half_shape = ((rows // LANES * COLS, LANES), F32)
    *own, high, low = call(
        far_kernel, [half_shape] * HALVES + factor(1),
        place, *side, swap_core(side_block), side_sketch, swap_core(side_sketch), near_y,
    )
    matrix = (near[0], side[0], high, near[1], side[1], low)

    flat = (COLS * rows // LANES + TILE, LANES)
    sent_shape = ((COLS * 4 * width // LANES + TILE, LANES), F32)
    y_shape = (flat, F32)
    scale_shape = ((TILE, LANES), F32)
    z_shape = ((COLS * 4 * width // LANES, LANES), F32)
    scales = [[] for _ in range(HALVES)]
    sent = [call(first_z_kernel, [sent_shape], y, swap_pair(y), *matrix, scalars=0)[0] for y in own]
    ys, zs = [None] * HALVES, [None] * HALVES
    for section in range(ITERS):
        last = section == ITERS - 1
        for h in range(HALVES):
            ys[h], scale, *z = call(
                functools.partial(y_kernel, all_cells), [y_shape, scale_shape] + [z_shape] * last,
                *cell_pair(sent[h]), *matrix, scalars=0,
            )
            scales[h].append(scale)
            if last:
                zs[h] = z[0]
                continue
            sent[h], scale = call(
                functools.partial(z_kernel, all_snaps), [sent_shape, scale_shape],
                ys[h], swap_pair(ys[h]), *matrix, scalars=0,
            )
            scales[h].append(scale)

    small = (2 * COLS + TILE, LANES)
    carried = HALVES * z_shape[0][0] // 2
    keeps, gots = [], []
    for h in range(HALVES):
        parts = zs if h == 0 else []
        keep, send, _ = call(
            functools.partial(end_kernel, all_snaps, len(parts)),
            [(small, F32), ((small[0] + carried * (h == 0), LANES), F32), ((flat[0] - TILE, LANES), F32)],
            place, ys[h], swap_pair(ys[h]), *parts, *scales[h],
        )
        keeps.append(keep)
        gots.append(swap_side(send))
    keep, send = call(
        core_kernel, [((LANES + TILE, LANES), F32), ((LANES + TILE + carried, LANES), F32)],
        place, *keeps, *gots, *zs,
    )
    core_got = swap_core(send)
    y, known = call(join_kernel, [((LANES, rank), F32), ((TILE, rank), F32)], place, keep, core_got)
    a, b = cell_pair(known)
    (z_out,) = call(z_out_kernel, [((width, rank), F32)], place, *zs, gots[0], core_got, known, plain=True)
    q_out, scale_out = call(
        functools.partial(q_out_kernel, all_cells),
        [((LANES, rank), F32), ((2 * ITERS + 1, rank), F32)],
        y, known, a, b, scalars=0, plain=True,
    )
    return q_out, z_out, scale_out


def solution(mesh):
    return jax.shard_map(
        local,
        mesh=mesh,
        in_specs=(P("cell", "snap"), P("snap", None)),
        out_specs=(P(("cell", "snap"), None), P("snap", None), P()),
        check_vma=False,
    )
```

```python
import functools

import jax
import jax.numpy as jnp
from jax import lax
from jax.experimental import pallas as pl
from jax.experimental.pallas import tpu as pltpu
from jax.sharding import PartitionSpec as P

ITERS = 2
EPS = 1e-05
LANES = 128
TILE = 8
HALVES = 2
QUARTER = 64
COLS = QUARTER // HALVES
BLOCKS = 3
BF16 = jnp.bfloat16
F32 = jnp.float32


def position():
    seat = lax.axis_index("snap")
    core, chip = lax.rem(seat, 2), lax.div(seat, 2)
    return core, lax.rem(chip, 2), chip


def split(x):
    high = x.astype(BF16).astype(F32)
    return high, x - high


def dot(a, b):
    return lax.dot_general(a, b, (((1,), (0,)), ((), ())), preferred_element_type=F32)


def eye(cols):
    shape = (cols, LANES)
    return lax.broadcasted_iota(jnp.int32, shape, 0) == lax.broadcasted_iota(jnp.int32, shape, 1)


def to_column(row, cols):
    return jnp.sum(jnp.where(eye(cols), row, 0.0), axis=1, keepdims=True)


def to_row(column):
    return jnp.sum(jnp.where(eye(column.shape[0]), column, 0.0), axis=0, keepdims=True)


def squares_tile(x):
    row = to_row(jnp.sum(x * x, axis=1, keepdims=True))
    return jnp.broadcast_to(row, (TILE, LANES))


def rms(total, count):
    return jnp.sqrt(total / count + EPS)


def wide(x, cols):
    return jnp.concatenate([x[j * cols : (j + 1) * cols] for j in range(x.shape[0] // cols)], axis=1)


def store_blocks(ref, start, x):
    cols = x.shape[0]
    for j in range(x.shape[1] // LANES):
        ref[start + j * cols : start + (j + 1) * cols, :] = x[:, j * LANES : (j + 1) * LANES]


def turn(x, cols):
    return pltpu.roll(x, cols, 1)


def join_lanes(first, second, cols):
    left = lax.broadcasted_iota(jnp.int32, first.shape, 1) < cols
    return jnp.where(left, first, turn(second, cols))


def unfold(total):
    cols = total.shape[0] // 2
    return total[:cols] + total[cols:]


def sketch_sides(x):
    high, low = split(x)
    own = join_lanes(high, low, QUARTER)
    other = join_lanes(turn(high, QUARTER), turn(low, QUARTER), QUARTER)
    return own.astype(BF16), other.astype(BF16)


def store_factors(high_ref, low_ref, blocks):
    for s, block in enumerate(blocks):
        high, low = split(block)
        cut = slice(s * block.shape[1], (s + 1) * block.shape[1])
        high_ref[:, cut] = high.astype(BF16)
        low_ref[:, cut] = low.astype(BF16)


def prepare_kernel(near_ref, got_ref, mine_ref, theirs_ref):
    near, got = near_ref[...], got_ref[...]
    low = join_lanes(near, got, QUARTER)
    high = join_lanes(turn(near, QUARTER), turn(got, QUARTER), QUARTER)
    zero = position()[1] == 0
    mine_ref[...] = jnp.where(zero, low, high)
    theirs_ref[...] = jnp.where(zero, high, low)


def near_kernel(own_ref, core_ref, sketch_ref, y_ref, high_ref, low_ref):
    store_factors(high_ref, low_ref, (own_ref[...], core_ref[...]))
    rhs = jnp.concatenate(sketch_sides(sketch_ref[...]), axis=0)
    for b in range(own_ref.shape[0] // LANES):
        cut = slice(b * LANES, (b + 1) * LANES)
        total = dot(high_ref[cut, :], rhs) + dot(low_ref[cut, :], rhs)
        y_ref[b * QUARTER : (b + 1) * QUARTER, :] = unfold(total.T)


def side_kernel(side_ref, sketch_ref, near_ref, y_ref, high_ref, low_ref):
    store_factors(high_ref, low_ref, (side_ref[...],))
    rhs = sketch_sides(sketch_ref[...])[0]
    for b in range(high_ref.shape[0] // LANES):
        cut = slice(b * LANES, (b + 1) * LANES)
        total = dot(high_ref[cut, :], rhs) + dot(low_ref[cut, :], rhs)
        out = slice(b * QUARTER, (b + 1) * QUARTER)
        y_ref[out, :] = unfold(total.T) + near_ref[out, :]


def far_kernel(diagonal_ref, sketch_ref, near_ref, *refs):
    *halves, high_ref, low_ref = refs
    store_factors(high_ref, low_ref, (diagonal_ref[...],))
    rhs = sketch_sides(sketch_ref[...])[1]
    for b in range(high_ref.shape[0] // LANES):
        cut = slice(b * LANES, (b + 1) * LANES)
        total = dot(high_ref[cut, :], rhs) + dot(low_ref[cut, :], rhs)
        y = unfold(total.T) + near_ref[b * QUARTER : (b + 1) * QUARTER, :]
        for h, ref in enumerate(halves):
            ref[b * COLS : (b + 1) * COLS, :] = y[h * COLS : (h + 1) * COLS]


def send_z(y, high_refs, low_refs, z_ref):
    lhs = jnp.concatenate(split(y), axis=0).astype(BF16)
    at = 0
    for high_ref, low_ref in zip(high_refs, low_refs):
        z = unfold(dot(lhs, high_ref[...]) + dot(lhs, low_ref[...]))
        store_blocks(z_ref, at, z)
        at += z.size // LANES
    z_ref[-TILE:, :] = squares_tile(y)


def factors(refs):
    return refs[:BLOCKS], refs[BLOCKS : 2 * BLOCKS]


def first_z_kernel(a_ref, b_ref, *refs):
    high, low = factors(refs)
    send_z(wide(a_ref[...] + b_ref[...], COLS), high, low, refs[-1])


def scaled(own_ref, got_ref, count):
    total = own_ref[...] + got_ref[...]
    scale = rms(total[-TILE:], count)
    return wide(total[:-TILE], COLS) / to_column(scale[:1], COLS), scale


def z_kernel(count, *refs):
    high, low = factors(refs[2:])
    z_ref, scale_ref = refs[-2:]
    y, scale = scaled(refs[0], refs[1], count)
    scale_ref[...] = scale
    send_z(y, high, low, z_ref)


def y_kernel(count, *refs):
    high_refs, low_refs = factors(refs[2:])
    y_ref, scale_ref, *z_refs = refs[2 + 2 * len(high_refs) :]
    z, scale = scaled(refs[0], refs[1], count)
    scale_ref[...] = scale
    for z_ref in z_refs:
        store_blocks(z_ref, 0, z)
    y_ref[-TILE:, :] = squares_tile(z)
    rhs = jnp.concatenate(split(z), axis=0).T.astype(BF16)
    total, at = None, 0
    for high_ref, low_ref in zip(high_refs, low_refs):
        part = rhs[at : at + high_ref.shape[1]]
        term = dot(high_ref[...], part) + dot(low_ref[...], part)
        total = term if total is None else total + term
        at += high_ref.shape[1]
    for b in range(total.shape[0] // LANES):
        y_ref[b * COLS : (b + 1) * COLS, :] = unfold(total[b * LANES : (b + 1) * LANES].T)


def end_kernel(count, carried, own_ref, got_ref, *refs):
    parts, scales, (keep_ref, send_ref, y_ref) = refs[:carried], refs[carried:-3], refs[-3:]
    y, scale = scaled(own_ref, got_ref, count)
    store_blocks(y_ref, 0, y)
    row = lax.broadcasted_iota(jnp.int32, (TILE, LANES), 0)
    tail = squares_tile(y)
    for i, known in enumerate([ref[...] for ref in scales] + [scale]):
        tail = jnp.where(row == i, known, tail)
    size = 2 * COLS
    chip = position()[2]
    for ref, owner in ((keep_ref, chip), (send_ref, chip ^ 1)):
        start = pl.multiple_of(owner * size, size)
        ref[:size, :] = y_ref[pl.ds(start, size), :]
        ref[size : size + TILE, :] = tail
    at = size + TILE
    for ref in parts:
        middle = ref.shape[0] // 2
        send_ref[at : at + middle, :] = ref[middle:, :]
        at += middle


def core_kernel(*refs):
    keeps, gots, parts = (refs[i * HALVES : (i + 1) * HALVES] for i in range(3))
    keep_ref, send_ref = refs[3 * HALVES :]
    core, side, _ = position()
    zero_side, zero_core = side == 0, core == 0
    tail = None
    for s in range(2):
        for h in range(HALVES):
            a, b = keeps[h][...], gots[h][: keeps[h].shape[0], :]
            x = jnp.where(zero_side, a, b) if s == 0 else jnp.where(zero_side, b, a)
            first, second, known = x[:COLS], x[COLS : 2 * COLS], x[2 * COLS :]
            at = (s * HALVES + h) * COLS
            keep_ref[at : at + COLS, :] = jnp.where(zero_core, first, second)
            send_ref[at : at + COLS, :] = jnp.where(zero_core, second, first)
            tail = known if tail is None else join_lanes(tail, known, at)
    keep_ref[LANES : LANES + TILE, :] = tail
    send_ref[LANES : LANES + TILE, :] = tail
    size = 2 * COLS
    for h, ref in enumerate(parts):
        at = LANES + TILE + h * size
        send_ref[at : at + size, :] = ref[size : 2 * size, :]
        at += HALVES * size
        start = keeps[0].shape[0] + (2 * h + 1) * size
        send_ref[at : at + size, :] = gots[0][start : start + size, :]


def join_kernel(keep_ref, got_ref, y_ref, known_ref):
    zero = position()[0] == 0
    keep, got = keep_ref[...], got_ref[: LANES + TILE, :]
    for s, x in enumerate((jnp.where(zero, keep, got), jnp.where(zero, got, keep))):
        cut = slice(s * LANES, (s + 1) * LANES)
        y_ref[:, cut] = x[:LANES].T
        known_ref[:, cut] = x[LANES:]


def z_out_kernel(*refs):
    parts, (side_ref, core_ref, known_ref, z_ref) = refs[:HALVES], refs[HALVES:]
    zero_core, zero_side = (flag == 0 for flag in position()[:2])
    size = 2 * COLS
    side_at, core_at = size + TILE, LANES + TILE
    mine = [ref[:size, :] for ref in parts]
    side = [side_ref[side_at + 2 * h * size : side_at + (2 * h + 1) * size, :] for h in range(HALVES)]
    core = [core_ref[core_at + h * size : core_at + (h + 1) * size, :] for h in range(2 * HALVES)]

    def side_order(own, other):
        low = [jnp.where(zero_side, a, b) for a, b in zip(own, other)]
        high = [jnp.where(zero_side, b, a) for a, b in zip(own, other)]
        return jnp.concatenate([wide(x, COLS) for x in low + high], axis=0)

    ours, theirs = side_order(mine, side), side_order(core[:HALVES], core[HALVES:])
    for s, x in enumerate((jnp.where(zero_core, ours, theirs), jnp.where(zero_core, theirs, ours))):
        cut = slice(s * LANES, (s + 1) * LANES)
        z_ref[:, cut] = x.T / known_ref[2 * ITERS - 1 : 2 * ITERS, cut]


def q_out_kernel(count, y_ref, known_ref, *refs):
    gots, (q_ref, scale_ref) = refs[:-2], refs[-2:]
    last = 2 * ITERS
    row = slice(last, last + 1)
    total = (known_ref[row, :] + gots[0][row, :]) + (gots[1][row, :] + gots[2][row, :])
    scale = rms(total, count)
    q_ref[...] = y_ref[...] / scale
    scale_ref[:last, :] = known_ref[:last, :]
    scale_ref[last:, :] = scale


def call(kernel, outs, *args, plain=False, scratch=(), cost=None):
    out_spec = pl.BlockSpec() if plain else pl.BlockSpec(memory_space=pltpu.VMEM)
    return pl.pallas_call(
        kernel,
        out_shape=[jax.ShapeDtypeStruct(shape, dtype) for shape, dtype in outs],
        in_specs=[pl.BlockSpec(memory_space=pltpu.VMEM)] * len(args),
        out_specs=[out_spec] * len(outs),
        scratch_shapes=scratch,
        cost_estimate=cost,
        compiler_params=pltpu.CompilerParams(vmem_limit_bytes=16 * 1024 * 1024),
    )(*args)


LONG = pl.CostEstimate(flops=10**11, bytes_accessed=2**28, transcendentals=0)


def general(snapshots, sketch):
    high = lax.Precision.HIGHEST
    all_cells = snapshots.shape[0] * lax.axis_size("cell")
    all_snaps = snapshots.shape[1] * lax.axis_size("snap")
    z, scales = sketch, []
    for section in range(ITERS + 1):
        partial = jnp.dot(snapshots, z, precision=high, preferred_element_type=F32)
        y = lax.psum_scatter(partial, "snap", scatter_dimension=0, tiled=True)
        scale = rms(lax.psum(jnp.sum(y * y, axis=0), ("cell", "snap")), all_cells)
        scales.append(scale)
        q = y / scale
        if section < ITERS:
            whole = lax.all_gather(q, "snap", axis=0, tiled=True)
            partial = jnp.dot(snapshots.T, whole, precision=high, preferred_element_type=F32)
            z = lax.psum(partial, "cell")
            scale = rms(lax.psum(jnp.sum(z * z, axis=0), "snap"), all_snaps)
            scales.append(scale)
            z = z / scale
    return q, z, jnp.stack(scales)


def local(snapshots, sketch):
    groups = lax.axis_size("cell")
    places = lax.axis_size("snap")
    rows, width = snapshots.shape
    rank = sketch.shape[1]
    fits = groups == 4 and places == 8 and rank == 4 * QUARTER and rows == 8 * LANES and width == 2 * LANES
    if not fits:
        return general(snapshots, sketch)
    all_cells = rows * groups
    all_snaps = width * places

    def swap(x, bits):
        return lax.ppermute(x, "snap", [(i, i ^ bits) for i in range(places)])

    swap_core = functools.partial(swap, bits=1)
    swap_side = functools.partial(swap, bits=2)
    swap_pair = functools.partial(swap, bits=4)

    def swap_cell(x, step):
        def target(cell, i):
            return cell ^ (1 if i % 2 == step else 2)

        perm = [(c * places + i, target(c, i) * places + i) for c in range(groups) for i in range(places)]
        return lax.ppermute(x, ("cell", "snap"), perm)

    def cell_pair(x):
        x = x + swap_cell(x, 0)
        return x, swap_cell(x, 1)

    def factor(count):
        return [((rows, count * width), BF16)] * 2

    def sketch_half(index):
        return lax.dynamic_slice_in_dim(sketch, index * LANES, LANES, 1)

    core = lax.rem(lax.axis_index("snap"), 2)
    side_block = swap_side(snapshots)
    packed = ((width, LANES), F32)
    mine, theirs = call(prepare_kernel, [packed, packed], sketch_half(core), swap_core(sketch_half(1 - core)))
    side_sketch = swap_side(theirs)
    quarter_shape = ((rows // LANES * QUARTER, LANES), F32)
    near_y, *near = call(near_kernel, [quarter_shape] + factor(2), snapshots, swap_core(snapshots), mine)
    side_block, near_y = lax.optimization_barrier((side_block, near_y))
    side_y, *side = call(side_kernel, [quarter_shape] + factor(1), side_block, side_sketch, near_y, cost=LONG)
    half_shape = ((rows // LANES * COLS, LANES), F32)
    *own, high, low = call(
        far_kernel, [half_shape] * HALVES + factor(1), swap_core(side_block), side_sketch, side_y
    )
    matrix = (near[0], side[0], high, near[1], side[1], low)

    flat = (COLS * rows // LANES + TILE, LANES)
    sent_shape = ((COLS * 4 * width // LANES + TILE, LANES), F32)
    y_shape = (flat, F32)
    scale_shape = ((TILE, LANES), F32)
    z_shape = ((COLS * 4 * width // LANES, LANES), F32)
    scales = [[] for _ in range(HALVES)]
    sent = [call(first_z_kernel, [sent_shape], y, swap_pair(y), *matrix)[0] for y in own]
    ys, zs = [None] * HALVES, [None] * HALVES
    for section in range(ITERS):
        last = section == ITERS - 1
        for h in range(HALVES):
            ys[h], scale, *z = call(
                functools.partial(y_kernel, all_cells), [y_shape, scale_shape] + [z_shape] * last,
                *cell_pair(sent[h]), *matrix,
            )
            scales[h].append(scale)
            if last:
                zs[h] = z[0]
                continue
            sent[h], scale = call(
                functools.partial(z_kernel, all_snaps), [sent_shape, scale_shape],
                ys[h], swap_pair(ys[h]), *matrix,
            )
            scales[h].append(scale)

    small = (2 * COLS + TILE, LANES)
    carried = HALVES * z_shape[0][0] // 2
    keeps, gots = [], []
    for h in range(HALVES):
        parts = zs if h == 0 else []
        keep, send = call(
            functools.partial(end_kernel, all_snaps, len(parts)),
            [(small, F32), ((small[0] + carried * (h == 0), LANES), F32)],
            ys[h], swap_pair(ys[h]), *parts, *scales[h],
            scratch=[pltpu.VMEM((flat[0] - TILE, LANES), F32)],
        )
        keeps.append(keep)
        gots.append(swap_side(send))
    keep, send = call(
        core_kernel, [((LANES + TILE, LANES), F32), ((LANES + TILE + carried, LANES), F32)],
        *keeps, *gots, *zs,
    )
    core_got = swap_core(send)
    y, known = call(join_kernel, [((LANES, rank), F32), ((TILE, rank), F32)], keep, core_got)
    others = [lax.ppermute(known, "cell", [(c, c ^ d) for c in range(groups)]) for d in (1, 2, 3)]
    (z_out,) = call(z_out_kernel, [((width, rank), F32)], *zs, gots[0], core_got, known, plain=True)
    q_out, scale_out = call(
        functools.partial(q_out_kernel, all_cells),
        [((LANES, rank), F32), ((2 * ITERS + 1, rank), F32)],
        y, known, *others, plain=True,
    )
    return q_out, z_out, scale_out


def solution(mesh):
    return jax.shard_map(
        local,
        mesh=mesh,
        in_specs=(P("cell", "snap"), P("snap", None)),
        out_specs=(P(("cell", "snap"), None), P("snap", None), P()),
        check_vma=False,
    )
```

```python
import functools

import jax
import jax.numpy as jnp
from jax import lax
from jax.experimental import pallas as pl
from jax.experimental.pallas import tpu as pltpu
from jax.sharding import PartitionSpec as P

ITERS = 2
EPS = 1e-05
LANES = 128
TILE = 8
HALVES = 2
QUARTER = 64
COLS = QUARTER // HALVES
BLOCKS = 3
BF16 = jnp.bfloat16
F32 = jnp.float32


def position():
    seat = lax.axis_index("snap")
    core, chip = lax.rem(seat, 2), lax.div(seat, 2)
    return core, lax.rem(chip, 2), chip


def split(x):
    high = x.astype(BF16).astype(F32)
    return high, x - high


def dot(a, b):
    return lax.dot_general(a, b, (((1,), (0,)), ((), ())), preferred_element_type=F32)


def eye(cols):
    shape = (cols, LANES)
    return lax.broadcasted_iota(jnp.int32, shape, 0) == lax.broadcasted_iota(jnp.int32, shape, 1)


def to_column(row, cols):
    return jnp.sum(jnp.where(eye(cols), row, 0.0), axis=1, keepdims=True)


def to_row(column):
    return jnp.sum(jnp.where(eye(column.shape[0]), column, 0.0), axis=0, keepdims=True)


def squares_tile(x):
    row = to_row(jnp.sum(x * x, axis=1, keepdims=True))
    return jnp.broadcast_to(row, (TILE, LANES))


def rms(total, count):
    return jnp.sqrt(total / count + EPS)


def wide(x, cols):
    return jnp.concatenate([x[j * cols : (j + 1) * cols] for j in range(x.shape[0] // cols)], axis=1)


def store_blocks(ref, start, x):
    cols = x.shape[0]
    for j in range(x.shape[1] // LANES):
        ref[start + j * cols : start + (j + 1) * cols, :] = x[:, j * LANES : (j + 1) * LANES]


def turn(x, cols):
    return pltpu.roll(x, cols, 1)


def join_lanes(first, second, cols):
    left = lax.broadcasted_iota(jnp.int32, first.shape, 1) < cols
    return jnp.where(left, first, turn(second, cols))


def unfold(total):
    cols = total.shape[0] // 2
    return total[:cols] + total[cols:]


def sketch_sides(x):
    high, low = split(x)
    own = join_lanes(high, low, QUARTER)
    other = join_lanes(turn(high, QUARTER), turn(low, QUARTER), QUARTER)
    return own.astype(BF16), other.astype(BF16)


def store_factors(high_ref, low_ref, blocks, axis=1):
    start = 0
    for block in blocks:
        size = block.shape[axis]
        cut = [slice(None)] * 2
        cut[axis] = slice(start, start + size)
        high, low = split(block)
        high_ref[tuple(cut)] = high.astype(BF16)
        low_ref[tuple(cut)] = low.astype(BF16)
        start += size


def prepare_kernel(near_ref, got_ref, mine_ref, theirs_ref):
    near, got = near_ref[...], got_ref[...]
    low = join_lanes(near, got, QUARTER)
    high = join_lanes(turn(near, QUARTER), turn(got, QUARTER), QUARTER)
    zero = position()[1] == 0
    mine_ref[...] = jnp.where(zero, low, high)
    theirs_ref[...] = jnp.where(zero, high, low)


def near_kernel(own_ref, core_ref, sketch_ref, y_ref, high_ref, low_ref, high_t_ref, low_t_ref):
    blocks = (own_ref[...], core_ref[...])
    store_factors(high_ref, low_ref, blocks)
    store_factors(high_t_ref, low_t_ref, [block.T for block in blocks], 0)
    rhs = jnp.concatenate(sketch_sides(sketch_ref[...]), axis=0)
    for b in range(own_ref.shape[0] // LANES):
        cut = slice(b * LANES, (b + 1) * LANES)
        total = dot(high_ref[cut, :], rhs) + dot(low_ref[cut, :], rhs)
        y_ref[b * QUARTER : (b + 1) * QUARTER, :] = unfold(total.T)


def side_split_kernel(side_ref, high_ref, low_ref, high_t_ref, low_t_ref):
    store_factors(high_ref, low_ref, (side_ref[...],))
    store_factors(high_t_ref, low_t_ref, (side_ref[...].T,), 0)


def side_kernel(high_ref, low_ref, sketch_ref, near_ref, y_ref):
    rhs = sketch_sides(sketch_ref[...])[0]
    for b in range(high_ref.shape[0] // LANES):
        cut = slice(b * LANES, (b + 1) * LANES)
        total = dot(high_ref[cut, :], rhs) + dot(low_ref[cut, :], rhs)
        out = slice(b * QUARTER, (b + 1) * QUARTER)
        y_ref[out, :] = unfold(total.T) + near_ref[out, :]


def add_far(h, high_ref, low_ref, sketch_ref, near_ref, y_ref):
    rhs = sketch_sides(sketch_ref[...])[1]
    for b in range(high_ref.shape[0] // LANES):
        cut = slice(b * LANES, (b + 1) * LANES)
        total = dot(high_ref[cut, :], rhs) + dot(low_ref[cut, :], rhs)
        y = unfold(total.T)[h * COLS : (h + 1) * COLS]
        at = b * QUARTER + h * COLS
        y_ref[b * COLS : (b + 1) * COLS, :] = y + near_ref[at : at + COLS, :]


def far_kernel(diagonal_ref, sketch_ref, near_ref, y_ref, high_ref, low_ref):
    store_factors(high_ref, low_ref, (diagonal_ref[...],))
    add_far(0, high_ref, low_ref, sketch_ref, near_ref, y_ref)


def second_far_kernel(diagonal_ref, high_ref, low_ref, sketch_ref, near_ref, y_ref, high_t_ref, low_t_ref):
    add_far(1, high_ref, low_ref, sketch_ref, near_ref, y_ref)
    store_factors(high_t_ref, low_t_ref, (diagonal_ref[...].T,), 0)


def send_z(y, high_refs, low_refs, z_ref):
    lhs = jnp.concatenate(split(y), axis=0).astype(BF16)
    at = 0
    for high_ref, low_ref in zip(high_refs, low_refs):
        z = unfold(dot(lhs, high_ref[...]) + dot(lhs, low_ref[...]))
        store_blocks(z_ref, at, z)
        at += z.size // LANES
    z_ref[-TILE:, :] = squares_tile(y)


def factors(refs):
    return refs[:BLOCKS], refs[BLOCKS : 2 * BLOCKS]


def first_z_kernel(a_ref, b_ref, *refs):
    high, low = factors(refs)
    send_z(wide(a_ref[...] + b_ref[...], COLS), high, low, refs[-1])


def scaled(own_ref, got_ref, count):
    total = own_ref[...] + got_ref[...]
    scale = rms(total[-TILE:], count)
    return wide(total[:-TILE], COLS) / to_column(scale[:1], COLS), scale


def z_kernel(count, *refs):
    high, low = factors(refs[2:])
    z_ref, scale_ref = refs[-2:]
    y, scale = scaled(refs[0], refs[1], count)
    scale_ref[...] = scale
    send_z(y, high, low, z_ref)


def y_kernel(count, *refs):
    high_refs, low_refs = factors(refs[2:])
    y_ref, scale_ref, *z_refs = refs[2 + 2 * len(high_refs) :]
    z, scale = scaled(refs[0], refs[1], count)
    scale_ref[...] = scale
    for z_ref in z_refs:
        store_blocks(z_ref, 0, z)
    y_ref[-TILE:, :] = squares_tile(z)
    lhs = jnp.concatenate(split(z), axis=0).astype(BF16)
    total, at = None, 0
    for high_ref, low_ref in zip(high_refs, low_refs):
        part = lhs[:, at : at + high_ref.shape[0]]
        term = dot(part, high_ref[...]) + dot(part, low_ref[...])
        total = term if total is None else total + term
        at += high_ref.shape[0]
    store_blocks(y_ref, 0, unfold(total))


def end_kernel(count, carried, own_ref, got_ref, *refs):
    parts, scales, (keep_ref, send_ref, y_ref) = refs[:carried], refs[carried:-3], refs[-3:]
    y, scale = scaled(own_ref, got_ref, count)
    store_blocks(y_ref, 0, y)
    row = lax.broadcasted_iota(jnp.int32, (TILE, LANES), 0)
    tail = squares_tile(y)
    for i, known in enumerate([ref[...] for ref in scales] + [scale]):
        tail = jnp.where(row == i, known, tail)
    size = 2 * COLS
    chip = position()[2]
    for ref, owner in ((keep_ref, chip), (send_ref, chip ^ 1)):
        start = pl.multiple_of(owner * size, size)
        ref[:size, :] = y_ref[pl.ds(start, size), :]
        ref[size : size + TILE, :] = tail
    at = size + TILE
    for ref in parts:
        middle = ref.shape[0] // 2
        send_ref[at : at + middle, :] = ref[middle:, :]
        at += middle


def core_kernel(*refs):
    keeps, gots, parts = (refs[i * HALVES : (i + 1) * HALVES] for i in range(3))
    keep_ref, send_ref = refs[3 * HALVES :]
    core, side, _ = position()
    zero_side, zero_core = side == 0, core == 0
    tail = None
    for s in range(2):
        for h in range(HALVES):
            a, b = keeps[h][...], gots[h][: keeps[h].shape[0], :]
            x = jnp.where(zero_side, a, b) if s == 0 else jnp.where(zero_side, b, a)
            first, second, known = x[:COLS], x[COLS : 2 * COLS], x[2 * COLS :]
            at = (s * HALVES + h) * COLS
            keep_ref[at : at + COLS, :] = jnp.where(zero_core, first, second)
            send_ref[at : at + COLS, :] = jnp.where(zero_core, second, first)
            tail = known if tail is None else join_lanes(tail, known, at)
    keep_ref[LANES : LANES + TILE, :] = tail
    send_ref[LANES : LANES + TILE, :] = tail
    size = 2 * COLS
    for h, ref in enumerate(parts):
        at = LANES + TILE + h * size
        send_ref[at : at + size, :] = ref[size : 2 * size, :]
        at += HALVES * size
        start = keeps[0].shape[0] + (2 * h + 1) * size
        send_ref[at : at + size, :] = gots[0][start : start + size, :]


def join_kernel(keep_ref, got_ref, y_ref, known_ref):
    zero = position()[0] == 0
    keep, got = keep_ref[...], got_ref[: LANES + TILE, :]
    for s, x in enumerate((jnp.where(zero, keep, got), jnp.where(zero, got, keep))):
        cut = slice(s * LANES, (s + 1) * LANES)
        y_ref[:, cut] = x[:LANES].T
        known_ref[:, cut] = x[LANES:]


def z_out_kernel(*refs):
    parts, (side_ref, core_ref, known_ref, z_ref) = refs[:HALVES], refs[HALVES:]
    zero_core, zero_side = (flag == 0 for flag in position()[:2])
    size = 2 * COLS
    side_at, core_at = size + TILE, LANES + TILE
    mine = [ref[:size, :] for ref in parts]
    side = [side_ref[side_at + 2 * h * size : side_at + (2 * h + 1) * size, :] for h in range(HALVES)]
    core = [core_ref[core_at + h * size : core_at + (h + 1) * size, :] for h in range(2 * HALVES)]

    def side_order(own, other):
        low = [jnp.where(zero_side, a, b) for a, b in zip(own, other)]
        high = [jnp.where(zero_side, b, a) for a, b in zip(own, other)]
        return jnp.concatenate([wide(x, COLS) for x in low + high], axis=0)

    ours, theirs = side_order(mine, side), side_order(core[:HALVES], core[HALVES:])
    for s, x in enumerate((jnp.where(zero_core, ours, theirs), jnp.where(zero_core, theirs, ours))):
        cut = slice(s * LANES, (s + 1) * LANES)
        z_ref[:, cut] = x.T / known_ref[2 * ITERS - 1 : 2 * ITERS, cut]


def q_out_kernel(count, y_ref, known_ref, *refs):
    gots, (q_ref, scale_ref) = refs[:-2], refs[-2:]
    last = 2 * ITERS
    row = slice(last, last + 1)
    total = (known_ref[row, :] + gots[0][row, :]) + (gots[1][row, :] + gots[2][row, :])
    scale = rms(total, count)
    q_ref[...] = y_ref[...] / scale
    scale_ref[:last, :] = known_ref[:last, :]
    scale_ref[last:, :] = scale


def call(kernel, outs, *args, plain=False, scratch=(), cost=None):
    out_spec = pl.BlockSpec() if plain else pl.BlockSpec(memory_space=pltpu.VMEM)
    return pl.pallas_call(
        kernel,
        out_shape=[jax.ShapeDtypeStruct(shape, dtype) for shape, dtype in outs],
        in_specs=[pl.BlockSpec(memory_space=pltpu.VMEM)] * len(args),
        out_specs=[out_spec] * len(outs),
        scratch_shapes=scratch,
        cost_estimate=cost,
        compiler_params=pltpu.CompilerParams(vmem_limit_bytes=16 * 1024 * 1024),
    )(*args)


LONG = pl.CostEstimate(flops=10**11, bytes_accessed=2**28, transcendentals=0)


def general(snapshots, sketch):
    high = lax.Precision.HIGHEST
    all_cells = snapshots.shape[0] * lax.axis_size("cell")
    all_snaps = snapshots.shape[1] * lax.axis_size("snap")
    z, scales = sketch, []
    for section in range(ITERS + 1):
        partial = jnp.dot(snapshots, z, precision=high, preferred_element_type=F32)
        y = lax.psum_scatter(partial, "snap", scatter_dimension=0, tiled=True)
        scale = rms(lax.psum(jnp.sum(y * y, axis=0), ("cell", "snap")), all_cells)
        scales.append(scale)
        q = y / scale
        if section < ITERS:
            whole = lax.all_gather(q, "snap", axis=0, tiled=True)
            partial = jnp.dot(snapshots.T, whole, precision=high, preferred_element_type=F32)
            z = lax.psum(partial, "cell")
            scale = rms(lax.psum(jnp.sum(z * z, axis=0), "snap"), all_snaps)
            scales.append(scale)
            z = z / scale
    return q, z, jnp.stack(scales)


def local(snapshots, sketch):
    groups = lax.axis_size("cell")
    places = lax.axis_size("snap")
    rows, width = snapshots.shape
    rank = sketch.shape[1]
    fits = groups == 4 and places == 8 and rank == 4 * QUARTER and rows == 8 * LANES and width == 2 * LANES
    if not fits:
        return general(snapshots, sketch)
    all_cells = rows * groups
    all_snaps = width * places

    def swap(x, bits):
        return lax.ppermute(x, "snap", [(i, i ^ bits) for i in range(places)])

    swap_core = functools.partial(swap, bits=1)
    swap_side = functools.partial(swap, bits=2)
    swap_pair = functools.partial(swap, bits=4)

    def swap_cell(x, step):
        def target(cell, i):
            return cell ^ (1 if i % 2 == step else 2)

        perm = [(c * places + i, target(c, i) * places + i) for c in range(groups) for i in range(places)]
        return lax.ppermute(x, ("cell", "snap"), perm)

    def cell_pair(x):
        x = x + swap_cell(x, 0)
        return x, swap_cell(x, 1)

    def factor(count):
        return [((rows, count * width), BF16)] * 2

    def factor_t(count):
        return [((count * width, rows), BF16)] * 2

    def sketch_half(index):
        return lax.dynamic_slice_in_dim(sketch, index * LANES, LANES, 1)

    core = lax.rem(lax.axis_index("snap"), 2)
    side_block = swap_side(snapshots)
    packed = ((width, LANES), F32)
    mine, theirs = call(prepare_kernel, [packed, packed], sketch_half(core), swap_core(sketch_half(1 - core)))
    side_sketch = swap_side(theirs)
    quarter_shape = ((rows // LANES * QUARTER, LANES), F32)
    near_y, *near = call(
        near_kernel, [quarter_shape] + factor(2) + factor_t(2), snapshots, swap_core(snapshots), mine
    )
    side_block, near_y = lax.optimization_barrier((side_block, near_y))
    side = call(side_split_kernel, factor(1) + factor_t(1), side_block)
    (side_y,) = call(side_kernel, [quarter_shape], *side[:2], side_sketch, near_y, cost=LONG)
    half_shape = ((rows // LANES * COLS, LANES), F32)
    diagonal = swap_core(side_block)
    own_first, *far = call(far_kernel, [half_shape] + factor(1), diagonal, side_sketch, side_y)
    own_second, *far_t = call(
        second_far_kernel, [half_shape] + factor_t(1), diagonal, *far, side_sketch, side_y
    )
    own = (own_first, own_second)
    matrix = (near[0], side[0], far[0], near[1], side[1], far[1])
    matrix_t = (near[2], side[2], far_t[0], near[3], side[3], far_t[1])

    flat = (COLS * rows // LANES + TILE, LANES)
    sent_shape = ((COLS * 4 * width // LANES + TILE, LANES), F32)
    y_shape = (flat, F32)
    scale_shape = ((TILE, LANES), F32)
    z_shape = ((COLS * 4 * width // LANES, LANES), F32)
    scales = [[] for _ in range(HALVES)]
    sent = [call(first_z_kernel, [sent_shape], y, swap_pair(y), *matrix, cost=LONG)[0] for y in own]
    ys, zs = [None] * HALVES, [None] * HALVES
    for section in range(ITERS):
        last = section == ITERS - 1
        for h in range(HALVES):
            ys[h], scale, *z = call(
                functools.partial(y_kernel, all_cells), [y_shape, scale_shape] + [z_shape] * last,
                *cell_pair(sent[h]), *matrix_t,
            )
            scales[h].append(scale)
            if last:
                zs[h] = z[0]
                continue
            sent[h], scale = call(
                functools.partial(z_kernel, all_snaps), [sent_shape, scale_shape],
                ys[h], swap_pair(ys[h]), *matrix,
            )
            scales[h].append(scale)

    small = (2 * COLS + TILE, LANES)
    carried = HALVES * z_shape[0][0] // 2
    keeps, gots = [], []
    for h in range(HALVES):
        parts = zs if h == 0 else []
        keep, send = call(
            functools.partial(end_kernel, all_snaps, len(parts)),
            [(small, F32), ((small[0] + carried * (h == 0), LANES), F32)],
            ys[h], swap_pair(ys[h]), *parts, *scales[h],
            scratch=[pltpu.VMEM((flat[0] - TILE, LANES), F32)],
        )
        keeps.append(keep)
        gots.append(swap_side(send))
    keep, send = call(
        core_kernel, [((LANES + TILE, LANES), F32), ((LANES + TILE + carried, LANES), F32)],
        *keeps, *gots, *zs,
    )
    core_got = swap_core(send)
    y, known = call(join_kernel, [((LANES, rank), F32), ((TILE, rank), F32)], keep, core_got)
    others = [lax.ppermute(known, "cell", [(c, c ^ d) for c in range(groups)]) for d in (1, 2, 3)]
    (z_out,) = call(z_out_kernel, [((width, rank), F32)], *zs, gots[0], core_got, known, plain=True)
    q_out, scale_out = call(
        functools.partial(q_out_kernel, all_cells),
        [((LANES, rank), F32), ((2 * ITERS + 1, rank), F32)],
        y, known, *others, plain=True,
    )
    return q_out, z_out, scale_out


def solution(mesh):
    return jax.shard_map(
        local,
        mesh=mesh,
        in_specs=(P("cell", "snap"), P("snap", None)),
        out_specs=(P(("cell", "snap"), None), P("snap", None), P()),
        check_vma=False,
    )
```

```python
import functools

import jax
import jax.numpy as jnp
from jax import lax
from jax.experimental import pallas as pl
from jax.experimental.pallas import tpu as pltpu
from jax.sharding import PartitionSpec as P

ITERS = 2
EPS = 1e-05
LANES = 128
TILE = 8
HALVES = 2
QUARTER = 64
COLS = QUARTER // HALVES
BLOCKS = 3
BF16 = jnp.bfloat16
F32 = jnp.float32


def position():
    seat = lax.axis_index("snap")
    core, chip = lax.rem(seat, 2), lax.div(seat, 2)
    inner = jnp.logical_or(chip == 1, chip == 2)
    return core, inner.astype(jnp.int32), chip


def split(x):
    high = x.astype(BF16).astype(F32)
    return high, x - high


def dot(a, b):
    return lax.dot_general(a, b, (((1,), (0,)), ((), ())), preferred_element_type=F32)


def eye(cols):
    shape = (cols, LANES)
    return lax.broadcasted_iota(jnp.int32, shape, 0) == lax.broadcasted_iota(jnp.int32, shape, 1)


def to_column(row, cols):
    return jnp.sum(jnp.where(eye(cols), row, 0.0), axis=1, keepdims=True)


def to_row(column):
    return jnp.sum(jnp.where(eye(column.shape[0]), column, 0.0), axis=0, keepdims=True)


def squares_tile(x):
    row = to_row(jnp.sum(x * x, axis=1, keepdims=True))
    return jnp.broadcast_to(row, (TILE, LANES))


def rms(total, count):
    return jnp.sqrt(total / count + EPS)


def wide(x, cols):
    return jnp.concatenate([x[j * cols : (j + 1) * cols] for j in range(x.shape[0] // cols)], axis=1)


def store_blocks(ref, start, x):
    cols = x.shape[0]
    for j in range(x.shape[1] // LANES):
        ref[start + j * cols : start + (j + 1) * cols, :] = x[:, j * LANES : (j + 1) * LANES]


def turn(x, cols):
    return pltpu.roll(x, cols, 1)


def join_lanes(first, second, cols):
    left = lax.broadcasted_iota(jnp.int32, first.shape, 1) < cols
    return jnp.where(left, first, turn(second, cols))


def unfold(total):
    cols = total.shape[0] // 2
    return total[:cols] + total[cols:]


def sketch_sides(x):
    high, low = split(x)
    own = join_lanes(high, low, QUARTER)
    other = join_lanes(turn(high, QUARTER), turn(low, QUARTER), QUARTER)
    return own.astype(BF16), other.astype(BF16)


def store_factors(high_ref, low_ref, blocks, axis=1):
    start = 0
    for block in blocks:
        size = block.shape[axis]
        cut = [slice(None)] * 2
        cut[axis] = slice(start, start + size)
        high, low = split(block)
        high_ref[tuple(cut)] = high.astype(BF16)
        low_ref[tuple(cut)] = low.astype(BF16)
        start += size


def prepare_kernel(near_ref, got_ref, mine_ref, theirs_ref):
    near, got = near_ref[...], got_ref[...]
    low = join_lanes(near, got, QUARTER)
    high = join_lanes(turn(near, QUARTER), turn(got, QUARTER), QUARTER)
    zero = position()[1] == 0
    mine_ref[...] = jnp.where(zero, low, high)
    theirs_ref[...] = jnp.where(zero, high, low)


def near_kernel(own_ref, core_ref, sketch_ref, y_ref, high_ref, low_ref, high_t_ref, low_t_ref):
    blocks = (own_ref[...], core_ref[...])
    store_factors(high_ref, low_ref, blocks)
    store_factors(high_t_ref, low_t_ref, [block.T for block in blocks], 0)
    rhs = jnp.concatenate(sketch_sides(sketch_ref[...]), axis=0)
    for b in range(own_ref.shape[0] // LANES):
        cut = slice(b * LANES, (b + 1) * LANES)
        total = dot(high_ref[cut, :], rhs) + dot(low_ref[cut, :], rhs)
        y_ref[b * QUARTER : (b + 1) * QUARTER, :] = unfold(total.T)


def side_split_kernel(side_ref, high_ref, low_ref, high_t_ref, low_t_ref):
    store_factors(high_ref, low_ref, (side_ref[...],))
    store_factors(high_t_ref, low_t_ref, (side_ref[...].T,), 0)


def side_kernel(high_ref, low_ref, sketch_ref, near_ref, y_ref):
    rhs = sketch_sides(sketch_ref[...])[0]
    for b in range(high_ref.shape[0] // LANES):
        cut = slice(b * LANES, (b + 1) * LANES)
        total = dot(high_ref[cut, :], rhs) + dot(low_ref[cut, :], rhs)
        out = slice(b * QUARTER, (b + 1) * QUARTER)
        y_ref[out, :] = unfold(total.T) + near_ref[out, :]


def add_far(h, high_ref, low_ref, sketch_ref, near_ref, y_ref):
    rhs = sketch_sides(sketch_ref[...])[1]
    for b in range(high_ref.shape[0] // LANES):
        cut = slice(b * LANES, (b + 1) * LANES)
        total = dot(high_ref[cut, :], rhs) + dot(low_ref[cut, :], rhs)
        y = unfold(total.T)[h * COLS : (h + 1) * COLS]
        at = b * QUARTER + h * COLS
        y_ref[b * COLS : (b + 1) * COLS, :] = y + near_ref[at : at + COLS, :]


def far_kernel(diagonal_ref, sketch_ref, near_ref, y_ref, high_ref, low_ref):
    store_factors(high_ref, low_ref, (diagonal_ref[...],))
    add_far(0, high_ref, low_ref, sketch_ref, near_ref, y_ref)


def second_far_kernel(diagonal_ref, high_ref, low_ref, sketch_ref, near_ref, y_ref, high_t_ref, low_t_ref):
    add_far(1, high_ref, low_ref, sketch_ref, near_ref, y_ref)
    store_factors(high_t_ref, low_t_ref, (diagonal_ref[...].T,), 0)


def send_z(y, high_refs, low_refs, z_ref):
    lhs = jnp.concatenate(split(y), axis=0).astype(BF16)
    at = 0
    for high_ref, low_ref in zip(high_refs, low_refs):
        z = unfold(dot(lhs, high_ref[...]) + dot(lhs, low_ref[...]))
        store_blocks(z_ref, at, z)
        at += z.size // LANES
    z_ref[-TILE:, :] = squares_tile(y)


def factors(refs):
    return refs[:BLOCKS], refs[BLOCKS : 2 * BLOCKS]


def first_z_kernel(a_ref, b_ref, *refs):
    high, low = factors(refs)
    send_z(wide(a_ref[...] + b_ref[...], COLS), high, low, refs[-1])


def scaled(own_ref, got_ref, count):
    total = own_ref[...] + got_ref[...]
    scale = rms(total[-TILE:], count)
    return wide(total[:-TILE], COLS) / to_column(scale[:1], COLS), scale


def z_kernel(count, *refs):
    high, low = factors(refs[2:])
    z_ref, scale_ref = refs[-2:]
    y, scale = scaled(refs[0], refs[1], count)
    scale_ref[...] = scale
    send_z(y, high, low, z_ref)


def y_kernel(count, *refs):
    high_refs, low_refs = factors(refs[2:])
    y_ref, scale_ref, *z_refs = refs[2 + 2 * len(high_refs) :]
    z, scale = scaled(refs[0], refs[1], count)
    scale_ref[...] = scale
    for z_ref in z_refs:
        store_blocks(z_ref, 0, z)
    y_ref[-TILE:, :] = squares_tile(z)
    lhs = jnp.concatenate(split(z), axis=0).astype(BF16)
    total, at = None, 0
    for high_ref, low_ref in zip(high_refs, low_refs):
        part = lhs[:, at : at + high_ref.shape[0]]
        term = dot(part, high_ref[...]) + dot(part, low_ref[...])
        total = term if total is None else total + term
        at += high_ref.shape[0]
    store_blocks(y_ref, 0, unfold(total))


def end_kernel(count, carried, own_ref, got_ref, *refs):
    parts, scales, (keep_ref, send_ref, y_ref) = refs[:carried], refs[carried:-3], refs[-3:]
    y, scale = scaled(own_ref, got_ref, count)
    store_blocks(y_ref, 0, y)
    row = lax.broadcasted_iota(jnp.int32, (TILE, LANES), 0)
    tail = squares_tile(y)
    for i, known in enumerate([ref[...] for ref in scales] + [scale]):
        tail = jnp.where(row == i, known, tail)
    size = 2 * COLS
    chip = position()[2]
    for ref, owner in ((keep_ref, chip), (send_ref, chip ^ 1)):
        start = pl.multiple_of(owner * size, size)
        ref[:size, :] = y_ref[pl.ds(start, size), :]
        ref[size : size + TILE, :] = tail
    at = size + TILE
    for ref in parts:
        middle = ref.shape[0] // 2
        send_ref[at : at + middle, :] = ref[middle:, :]
        at += middle


def core_kernel(*refs):
    keeps, gots, parts = (refs[i * HALVES : (i + 1) * HALVES] for i in range(3))
    keep_ref, send_ref = refs[3 * HALVES :]
    core, side, _ = position()
    zero_side, zero_core = side == 0, core == 0
    tail = None
    for s in range(2):
        for h in range(HALVES):
            a, b = keeps[h][...], gots[h][: keeps[h].shape[0], :]
            x = jnp.where(zero_side, a, b) if s == 0 else jnp.where(zero_side, b, a)
            first, second, known = x[:COLS], x[COLS : 2 * COLS], x[2 * COLS :]
            at = (s * HALVES + h) * COLS
            keep_ref[at : at + COLS, :] = jnp.where(zero_core, first, second)
            send_ref[at : at + COLS, :] = jnp.where(zero_core, second, first)
            tail = known if tail is None else join_lanes(tail, known, at)
    keep_ref[LANES : LANES + TILE, :] = tail
    send_ref[LANES : LANES + TILE, :] = tail
    size = 2 * COLS
    for h, ref in enumerate(parts):
        at = LANES + TILE + h * size
        send_ref[at : at + size, :] = ref[size : 2 * size, :]
        at += HALVES * size
        start = keeps[0].shape[0] + (2 * h + 1) * size
        send_ref[at : at + size, :] = gots[0][start : start + size, :]


def join_kernel(keep_ref, got_ref, y_ref, known_ref):
    zero = position()[0] == 0
    keep, got = keep_ref[...], got_ref[: LANES + TILE, :]
    for s, x in enumerate((jnp.where(zero, keep, got), jnp.where(zero, got, keep))):
        cut = slice(s * LANES, (s + 1) * LANES)
        y_ref[:, cut] = x[:LANES].T
        known_ref[:, cut] = x[LANES:]


def z_out_kernel(*refs):
    parts, (side_ref, core_ref, known_ref, z_ref) = refs[:HALVES], refs[HALVES:]
    zero_core, zero_side = (flag == 0 for flag in position()[:2])
    size = 2 * COLS
    side_at, core_at = size + TILE, LANES + TILE
    mine = [ref[:size, :] for ref in parts]
    side = [side_ref[side_at + 2 * h * size : side_at + (2 * h + 1) * size, :] for h in range(HALVES)]
    core = [core_ref[core_at + h * size : core_at + (h + 1) * size, :] for h in range(2 * HALVES)]

    def side_order(own, other):
        low = [jnp.where(zero_side, a, b) for a, b in zip(own, other)]
        high = [jnp.where(zero_side, b, a) for a, b in zip(own, other)]
        return jnp.concatenate([wide(x, COLS) for x in low + high], axis=0)

    ours, theirs = side_order(mine, side), side_order(core[:HALVES], core[HALVES:])
    for s, x in enumerate((jnp.where(zero_core, ours, theirs), jnp.where(zero_core, theirs, ours))):
        cut = slice(s * LANES, (s + 1) * LANES)
        z_ref[:, cut] = x.T / known_ref[2 * ITERS - 1 : 2 * ITERS, cut]


def q_out_kernel(count, y_ref, known_ref, *refs):
    gots, (q_ref, scale_ref) = refs[:-2], refs[-2:]
    last = 2 * ITERS
    row = slice(last, last + 1)
    total = (known_ref[row, :] + gots[0][row, :]) + (gots[1][row, :] + gots[2][row, :])
    scale = rms(total, count)
    q_ref[...] = y_ref[...] / scale
    scale_ref[:last, :] = known_ref[:last, :]
    scale_ref[last:, :] = scale


def call(kernel, outs, *args, plain=False, scratch=(), cost=None):
    out_spec = pl.BlockSpec() if plain else pl.BlockSpec(memory_space=pltpu.VMEM)
    return pl.pallas_call(
        kernel,
        out_shape=[jax.ShapeDtypeStruct(shape, dtype) for shape, dtype in outs],
        in_specs=[pl.BlockSpec(memory_space=pltpu.VMEM)] * len(args),
        out_specs=[out_spec] * len(outs),
        scratch_shapes=scratch,
        cost_estimate=cost,
        compiler_params=pltpu.CompilerParams(vmem_limit_bytes=16 * 1024 * 1024),
    )(*args)


LONG = pl.CostEstimate(flops=10**11, bytes_accessed=2**28, transcendentals=0)


def general(snapshots, sketch):
    high = lax.Precision.HIGHEST
    all_cells = snapshots.shape[0] * lax.axis_size("cell")
    all_snaps = snapshots.shape[1] * lax.axis_size("snap")
    z, scales = sketch, []
    for section in range(ITERS + 1):
        partial = jnp.dot(snapshots, z, precision=high, preferred_element_type=F32)
        y = lax.psum_scatter(partial, "snap", scatter_dimension=0, tiled=True)
        scale = rms(lax.psum(jnp.sum(y * y, axis=0), ("cell", "snap")), all_cells)
        scales.append(scale)
        q = y / scale
        if section < ITERS:
            whole = lax.all_gather(q, "snap", axis=0, tiled=True)
            partial = jnp.dot(snapshots.T, whole, precision=high, preferred_element_type=F32)
            z = lax.psum(partial, "cell")
            scale = rms(lax.psum(jnp.sum(z * z, axis=0), "snap"), all_snaps)
            scales.append(scale)
            z = z / scale
    return q, z, jnp.stack(scales)


def local(snapshots, sketch):
    groups = lax.axis_size("cell")
    places = lax.axis_size("snap")
    rows, width = snapshots.shape
    rank = sketch.shape[1]
    fits = groups == 4 and places == 8 and rank == 4 * QUARTER and rows == 8 * LANES and width == 2 * LANES
    if not fits:
        return general(snapshots, sketch)
    all_cells = rows * groups
    all_snaps = width * places

    def swap(x, bits):
        return lax.ppermute(x, "snap", [(i, i ^ bits) for i in range(places)])

    swap_core = functools.partial(swap, bits=1)
    swap_side = functools.partial(swap, bits=2)
    swap_pair = functools.partial(swap, bits=6)

    def swap_cell(x, step):
        def target(cell, i):
            return cell ^ (1 if i % 2 == step else 2)

        perm = [(c * places + i, target(c, i) * places + i) for c in range(groups) for i in range(places)]
        return lax.ppermute(x, ("cell", "snap"), perm)

    def cell_pair(x):
        x = x + swap_cell(x, 0)
        return x, swap_cell(x, 1)

    def factor(count):
        return [((rows, count * width), BF16)] * 2

    def factor_t(count):
        return [((count * width, rows), BF16)] * 2

    def sketch_half(index):
        return lax.dynamic_slice_in_dim(sketch, index * LANES, LANES, 1)

    core = lax.rem(lax.axis_index("snap"), 2)
    side_block = swap_side(snapshots)
    packed = ((width, LANES), F32)
    mine, theirs = call(prepare_kernel, [packed, packed], sketch_half(core), swap_core(sketch_half(1 - core)))
    side_sketch = swap_side(theirs)
    quarter_shape = ((rows // LANES * QUARTER, LANES), F32)
    near_y, *near = call(
        near_kernel, [quarter_shape] + factor(2) + factor_t(2), snapshots, swap_core(snapshots), mine
    )
    side_block, near_y = lax.optimization_barrier((side_block, near_y))
    side = call(side_split_kernel, factor(1) + factor_t(1), side_block)
    (side_y,) = call(side_kernel, [quarter_shape], *side[:2], side_sketch, near_y, cost=LONG)
    half_shape = ((rows // LANES * COLS, LANES), F32)
    diagonal = swap_core(side_block)
    own_first, *far = call(far_kernel, [half_shape] + factor(1), diagonal, side_sketch, side_y)
    own_second, *far_t = call(
        second_far_kernel, [half_shape] + factor_t(1), diagonal, *far, side_sketch, side_y
    )
    own = (own_first, own_second)
    matrix = (near[0], side[0], far[0], near[1], side[1], far[1])
    matrix_t = (near[2], side[2], far_t[0], near[3], side[3], far_t[1])

    flat = (COLS * rows // LANES + TILE, LANES)
    sent_shape = ((COLS * 4 * width // LANES + TILE, LANES), F32)
    y_shape = (flat, F32)
    scale_shape = ((TILE, LANES), F32)
    z_shape = ((COLS * 4 * width // LANES, LANES), F32)
    scales = [[] for _ in range(HALVES)]
    sent = [call(first_z_kernel, [sent_shape], y, swap_pair(y), *matrix, cost=LONG)[0] for y in own]
    ys, zs = [None] * HALVES, [None] * HALVES
    for section in range(ITERS):
        last = section == ITERS - 1
        for h in range(HALVES):
            ys[h], scale, *z = call(
                functools.partial(y_kernel, all_cells), [y_shape, scale_shape] + [z_shape] * last,
                *cell_pair(sent[h]), *matrix_t,
            )
            scales[h].append(scale)
            if last:
                zs[h] = z[0]
                continue
            sent[h], scale = call(
                functools.partial(z_kernel, all_snaps), [sent_shape, scale_shape],
                ys[h], swap_pair(ys[h]), *matrix,
            )
            scales[h].append(scale)

    small = (2 * COLS + TILE, LANES)
    carried = HALVES * z_shape[0][0] // 2
    keeps, gots = [], []
    for h in range(HALVES):
        parts = zs if h == 0 else []
        keep, send = call(
            functools.partial(end_kernel, all_snaps, len(parts)),
            [(small, F32), ((small[0] + carried * (h == 0), LANES), F32)],
            ys[h], swap_pair(ys[h]), *parts, *scales[h],
            scratch=[pltpu.VMEM((flat[0] - TILE, LANES), F32)],
        )
        keeps.append(keep)
        gots.append(swap_side(send))
    keep, send = call(
        core_kernel, [((LANES + TILE, LANES), F32), ((LANES + TILE + carried, LANES), F32)],
        *keeps, *gots, *zs,
    )
    core_got = swap_core(send)
    y, known = call(join_kernel, [((LANES, rank), F32), ((TILE, rank), F32)], keep, core_got)
    others = [lax.ppermute(known, "cell", [(c, c ^ d) for c in range(groups)]) for d in (1, 2, 3)]
    (z_out,) = call(z_out_kernel, [((width, rank), F32)], *zs, gots[0], core_got, known, plain=True)
    q_out, scale_out = call(
        functools.partial(q_out_kernel, all_cells),
        [((LANES, rank), F32), ((2 * ITERS + 1, rank), F32)],
        y, known, *others, plain=True,
    )
    return q_out, z_out, scale_out


def solution(mesh):
    return jax.shard_map(
        local,
        mesh=mesh,
        in_specs=(P("cell", "snap"), P("snap", None)),
        out_specs=(P(("cell", "snap"), None), P("snap", None), P()),
        check_vma=False,
    )
```

```python
import functools

import jax
import jax.numpy as jnp
from jax import lax
from jax.experimental import pallas as pl
from jax.experimental.pallas import tpu as pltpu
from jax.sharding import PartitionSpec as P

ITERS = 2
EPS = 1e-05
LANES = 128
TILE = 8
HALVES = 2
QUARTER = 64
COLS = QUARTER // HALVES
BLOCKS = 3
BF16 = jnp.bfloat16
F32 = jnp.float32


def position():
    seat = lax.axis_index("snap")
    core, chip = lax.rem(seat, 2), lax.div(seat, 2)
    inner = jnp.logical_or(chip == 1, chip == 2)
    return core, inner.astype(jnp.int32), chip


def split(x):
    high = x.astype(BF16).astype(F32)
    return high, x - high


def dot(a, b):
    return lax.dot_general(a, b, (((1,), (0,)), ((), ())), preferred_element_type=F32)


def eye(cols):
    shape = (cols, LANES)
    return lax.broadcasted_iota(jnp.int32, shape, 0) == lax.broadcasted_iota(jnp.int32, shape, 1)


def to_column(row, cols):
    return jnp.sum(jnp.where(eye(cols), row, 0.0), axis=1, keepdims=True)


def to_row(column):
    return jnp.sum(jnp.where(eye(column.shape[0]), column, 0.0), axis=0, keepdims=True)


def squares_tile(x):
    row = to_row(jnp.sum(x * x, axis=1, keepdims=True))
    return jnp.broadcast_to(row, (TILE, LANES))


def rms(total, count):
    return jnp.sqrt(total / count + EPS)


def wide(x, cols):
    return jnp.concatenate([x[j * cols : (j + 1) * cols] for j in range(x.shape[0] // cols)], axis=1)


def store_blocks(ref, start, x):
    cols = x.shape[0]
    for j in range(x.shape[1] // LANES):
        ref[start + j * cols : start + (j + 1) * cols, :] = x[:, j * LANES : (j + 1) * LANES]


def turn(x, cols):
    return pltpu.roll(x, cols, 1)


def join_lanes(first, second, cols):
    left = lax.broadcasted_iota(jnp.int32, first.shape, 1) < cols
    return jnp.where(left, first, turn(second, cols))


def unfold(total):
    cols = total.shape[0] // 2
    return total[:cols] + total[cols:]


def store_factors(high_ref, low_ref, blocks, axis=1):
    start = 0
    for block in blocks:
        size = block.shape[axis]
        cut = [slice(None)] * 2
        cut[axis] = slice(start, start + size)
        high, low = split(block)
        high_ref[tuple(cut)] = high.astype(BF16)
        low_ref[tuple(cut)] = low.astype(BF16)
        start += size


def near_kernel(own_ref, core_ref, near_ref, got_ref, y_ref, high_ref, low_ref, high_t_ref, low_t_ref):
    blocks = (own_ref[...], core_ref[...])
    store_factors(high_ref, low_ref, blocks)
    store_factors(high_t_ref, low_t_ref, [block.T for block in blocks], 0)
    sketch = jnp.concatenate([near_ref[...], got_ref[...]], axis=0)
    rhs = jnp.concatenate(split(sketch), axis=1).astype(BF16)
    zero = position()[1] == 0
    size = y_ref.shape[0] // (2 * HALVES)
    for b in range(own_ref.shape[0] // LANES):
        cut = slice(b * LANES, (b + 1) * LANES)
        total = dot(high_ref[cut, :], rhs) + dot(low_ref[cut, :], rhs)
        y = (total[:, :LANES] + total[:, LANES:]).T
        low, high = y[:QUARTER], y[QUARTER:]
        for s, x in enumerate((jnp.where(zero, low, high), jnp.where(zero, high, low))):
            for h in range(HALVES):
                at = (s * HALVES + h) * size + b * COLS
                y_ref[at : at + COLS, :] = x[h * COLS : (h + 1) * COLS]


def cross_kernel(y_ref, got_ref, *refs):
    for i, ref in enumerate(refs):
        cut = slice(i * ref.shape[0], (i + 1) * ref.shape[0])
        ref[...] = y_ref[cut, :] + got_ref[cut, :]


def split_kernel(block_ref, high_ref, low_ref):
    store_factors(high_ref, low_ref, (block_ref[...],))


def turned_kernel(block_ref, high_ref, low_ref):
    store_factors(high_ref, low_ref, (block_ref[...].T,), 0)


def send_z(y, high_refs, low_refs, z_ref):
    lhs = jnp.concatenate(split(y), axis=0).astype(BF16)
    at = 0
    for high_ref, low_ref in zip(high_refs, low_refs):
        z = unfold(dot(lhs, high_ref[...]) + dot(lhs, low_ref[...]))
        store_blocks(z_ref, at, z)
        at += z.size // LANES
    z_ref[-TILE:, :] = squares_tile(y)


def factors(refs):
    return refs[:BLOCKS], refs[BLOCKS : 2 * BLOCKS]


def first_z_kernel(a_ref, b_ref, *refs):
    high, low = factors(refs)
    send_z(wide(a_ref[...] + b_ref[...], COLS), high, low, refs[-1])


def scaled(own_ref, got_ref, count):
    total = own_ref[...] + got_ref[...]
    scale = rms(total[-TILE:], count)
    return wide(total[:-TILE], COLS) / to_column(scale[:1], COLS), scale


def z_kernel(count, *refs):
    high, low = factors(refs[2:])
    z_ref, scale_ref = refs[-2:]
    y, scale = scaled(refs[0], refs[1], count)
    scale_ref[...] = scale
    send_z(y, high, low, z_ref)


def y_kernel(count, *refs):
    high_refs, low_refs = factors(refs[2:])
    y_ref, scale_ref, *z_refs = refs[2 + 2 * len(high_refs) :]
    z, scale = scaled(refs[0], refs[1], count)
    scale_ref[...] = scale
    for z_ref in z_refs:
        store_blocks(z_ref, 0, z)
    y_ref[-TILE:, :] = squares_tile(z)
    lhs = jnp.concatenate(split(z), axis=0).astype(BF16)
    total, at = None, 0
    for high_ref, low_ref in zip(high_refs, low_refs):
        part = lhs[:, at : at + high_ref.shape[0]]
        term = dot(part, high_ref[...]) + dot(part, low_ref[...])
        total = term if total is None else total + term
        at += high_ref.shape[0]
    store_blocks(y_ref, 0, unfold(total))


def end_kernel(count, carried, own_ref, got_ref, *refs):
    parts, scales, (keep_ref, send_ref, y_ref) = refs[:carried], refs[carried:-3], refs[-3:]
    y, scale = scaled(own_ref, got_ref, count)
    store_blocks(y_ref, 0, y)
    row = lax.broadcasted_iota(jnp.int32, (TILE, LANES), 0)
    tail = squares_tile(y)
    for i, known in enumerate([ref[...] for ref in scales] + [scale]):
        tail = jnp.where(row == i, known, tail)
    size = 2 * COLS
    chip = position()[2]
    for ref, owner in ((keep_ref, chip), (send_ref, chip ^ 1)):
        start = pl.multiple_of(owner * size, size)
        ref[:size, :] = y_ref[pl.ds(start, size), :]
        ref[size : size + TILE, :] = tail
    at = size + TILE
    for ref in parts:
        middle = ref.shape[0] // 2
        send_ref[at : at + middle, :] = ref[middle:, :]
        at += middle


def core_kernel(*refs):
    keeps, gots, parts = (refs[i * HALVES : (i + 1) * HALVES] for i in range(3))
    keep_ref, send_ref = refs[3 * HALVES :]
    core, side, _ = position()
    zero_side, zero_core = side == 0, core == 0
    tail = None
    for s in range(2):
        for h in range(HALVES):
            a, b = keeps[h][...], gots[h][: keeps[h].shape[0], :]
            x = jnp.where(zero_side, a, b) if s == 0 else jnp.where(zero_side, b, a)
            first, second, known = x[:COLS], x[COLS : 2 * COLS], x[2 * COLS :]
            at = (s * HALVES + h) * COLS
            keep_ref[at : at + COLS, :] = jnp.where(zero_core, first, second)
            send_ref[at : at + COLS, :] = jnp.where(zero_core, second, first)
            tail = known if tail is None else join_lanes(tail, known, at)
    keep_ref[LANES : LANES + TILE, :] = tail
    send_ref[LANES : LANES + TILE, :] = tail
    size = 2 * COLS
    for h, ref in enumerate(parts):
        at = LANES + TILE + h * size
        send_ref[at : at + size, :] = ref[size : 2 * size, :]
        at += HALVES * size
        start = keeps[0].shape[0] + (2 * h + 1) * size
        send_ref[at : at + size, :] = gots[0][start : start + size, :]


def join_kernel(keep_ref, got_ref, y_ref, known_ref):
    zero = position()[0] == 0
    keep, got = keep_ref[...], got_ref[: LANES + TILE, :]
    for s, x in enumerate((jnp.where(zero, keep, got), jnp.where(zero, got, keep))):
        cut = slice(s * LANES, (s + 1) * LANES)
        y_ref[:, cut] = x[:LANES].T
        known_ref[:, cut] = x[LANES:]


def z_out_kernel(*refs):
    parts, (side_ref, core_ref, known_ref, z_ref) = refs[:HALVES], refs[HALVES:]
    zero_core, zero_side = (flag == 0 for flag in position()[:2])
    size = 2 * COLS
    side_at, core_at = size + TILE, LANES + TILE
    mine = [ref[:size, :] for ref in parts]
    side = [side_ref[side_at + 2 * h * size : side_at + (2 * h + 1) * size, :] for h in range(HALVES)]
    core = [core_ref[core_at + h * size : core_at + (h + 1) * size, :] for h in range(2 * HALVES)]

    def side_order(own, other):
        low = [jnp.where(zero_side, a, b) for a, b in zip(own, other)]
        high = [jnp.where(zero_side, b, a) for a, b in zip(own, other)]
        return jnp.concatenate([wide(x, COLS) for x in low + high], axis=0)

    ours, theirs = side_order(mine, side), side_order(core[:HALVES], core[HALVES:])
    for s, x in enumerate((jnp.where(zero_core, ours, theirs), jnp.where(zero_core, theirs, ours))):
        cut = slice(s * LANES, (s + 1) * LANES)
        z_ref[:, cut] = x.T / known_ref[2 * ITERS - 1 : 2 * ITERS, cut]


def q_out_kernel(count, y_ref, known_ref, *refs):
    gots, (q_ref, scale_ref) = refs[:-2], refs[-2:]
    last = 2 * ITERS
    row = slice(last, last + 1)
    total = (known_ref[row, :] + gots[0][row, :]) + (gots[1][row, :] + gots[2][row, :])
    scale = rms(total, count)
    q_ref[...] = y_ref[...] / scale
    scale_ref[:last, :] = known_ref[:last, :]
    scale_ref[last:, :] = scale


def call(kernel, outs, *args, plain=False, scratch=(), cost=None):
    out_spec = pl.BlockSpec() if plain else pl.BlockSpec(memory_space=pltpu.VMEM)
    return pl.pallas_call(
        kernel,
        out_shape=[jax.ShapeDtypeStruct(shape, dtype) for shape, dtype in outs],
        in_specs=[pl.BlockSpec(memory_space=pltpu.VMEM)] * len(args),
        out_specs=[out_spec] * len(outs),
        scratch_shapes=scratch,
        cost_estimate=cost,
        compiler_params=pltpu.CompilerParams(vmem_limit_bytes=16 * 1024 * 1024),
    )(*args)


LONG = pl.CostEstimate(flops=10**11, bytes_accessed=2**28, transcendentals=0)


def general(snapshots, sketch):
    high = lax.Precision.HIGHEST
    all_cells = snapshots.shape[0] * lax.axis_size("cell")
    all_snaps = snapshots.shape[1] * lax.axis_size("snap")
    z, scales = sketch, []
    for section in range(ITERS + 1):
        partial = jnp.dot(snapshots, z, precision=high, preferred_element_type=F32)
        y = lax.psum_scatter(partial, "snap", scatter_dimension=0, tiled=True)
        scale = rms(lax.psum(jnp.sum(y * y, axis=0), ("cell", "snap")), all_cells)
        scales.append(scale)
        q = y / scale
        if section < ITERS:
            whole = lax.all_gather(q, "snap", axis=0, tiled=True)
            partial = jnp.dot(snapshots.T, whole, precision=high, preferred_element_type=F32)
            z = lax.psum(partial, "cell")
            scale = rms(lax.psum(jnp.sum(z * z, axis=0), "snap"), all_snaps)
            scales.append(scale)
            z = z / scale
    return q, z, jnp.stack(scales)


def local(snapshots, sketch):
    groups = lax.axis_size("cell")
    places = lax.axis_size("snap")
    rows, width = snapshots.shape
    rank = sketch.shape[1]
    fits = groups == 4 and places == 8 and rank == 4 * QUARTER and rows == 8 * LANES and width == 2 * LANES
    if not fits:
        return general(snapshots, sketch)
    all_cells = rows * groups
    all_snaps = width * places

    def swap(x, bits):
        return lax.ppermute(x, "snap", [(i, i ^ bits) for i in range(places)])

    swap_core = functools.partial(swap, bits=1)
    swap_side = functools.partial(swap, bits=2)
    swap_pair = functools.partial(swap, bits=6)

    def swap_cell(x, step):
        def target(cell, i):
            return cell ^ (1 if i % 2 == step else 2)

        perm = [(c * places + i, target(c, i) * places + i) for c in range(groups) for i in range(places)]
        return lax.ppermute(x, ("cell", "snap"), perm)

    def cell_pair(x):
        x = x + swap_cell(x, 0)
        return x, swap_cell(x, 1)

    def factor(count):
        return [((rows, count * width), BF16)] * 2

    def factor_t(count):
        return [((count * width, rows), BF16)] * 2

    def sketch_half(index):
        return lax.dynamic_slice_in_dim(sketch, index * LANES, LANES, 1)

    core = lax.rem(lax.axis_index("snap"), 2)
    side_block = swap_side(snapshots)
    half_rows = rows // LANES * COLS
    y_near, *near = call(
        near_kernel,
        [((2 * HALVES * half_rows, LANES), F32)] + factor(2) + factor_t(2),
        snapshots, swap_core(snapshots), sketch_half(core), swap_core(sketch_half(1 - core)),
    )
    sums = call(cross_kernel, [((half_rows, LANES), F32)] * 2 * HALVES, y_near, swap_pair(y_near))
    own, others = sums[:HALVES], sums[HALVES:]
    got = [swap_side(other) for other in others]
    side_block, *own = lax.optimization_barrier((side_block, *own))
    side = call(split_kernel, factor(1), side_block)
    side_t = call(turned_kernel, factor_t(1), side_block)
    diagonal = swap_core(side_block)
    far = call(split_kernel, factor(1), diagonal, cost=LONG)
    far_t = call(turned_kernel, factor_t(1), diagonal)
    matrix = (near[0], side[0], far[0], near[1], side[1], far[1])
    matrix_t = (near[2], side_t[0], far_t[0], near[3], side_t[1], far_t[1])

    flat = (COLS * rows // LANES + TILE, LANES)
    sent_shape = ((COLS * 4 * width // LANES + TILE, LANES), F32)
    y_shape = (flat, F32)
    scale_shape = ((TILE, LANES), F32)
    z_shape = ((COLS * 4 * width // LANES, LANES), F32)
    scales = [[] for _ in range(HALVES)]
    sent = [call(first_z_kernel, [sent_shape], y, g, *matrix, cost=LONG)[0] for y, g in zip(own, got)]
    ys, zs = [None] * HALVES, [None] * HALVES
    for section in range(ITERS):
        last = section == ITERS - 1
        for h in range(HALVES):
            ys[h], scale, *z = call(
                functools.partial(y_kernel, all_cells), [y_shape, scale_shape] + [z_shape] * last,
                *cell_pair(sent[h]), *matrix_t,
            )
            scales[h].append(scale)
            if last:
                zs[h] = z[0]
                continue
            sent[h], scale = call(
                functools.partial(z_kernel, all_snaps), [sent_shape, scale_shape],
                ys[h], swap_pair(ys[h]), *matrix,
            )
            scales[h].append(scale)

    small = (2 * COLS + TILE, LANES)
    carried = HALVES * z_shape[0][0] // 2
    keeps, gots = [], []
    for h in range(HALVES):
        parts = zs if h == 0 else []
        keep, send = call(
            functools.partial(end_kernel, all_snaps, len(parts)),
            [(small, F32), ((small[0] + carried * (h == 0), LANES), F32)],
            ys[h], swap_pair(ys[h]), *parts, *scales[h],
            scratch=[pltpu.VMEM((flat[0] - TILE, LANES), F32)],
        )
        keeps.append(keep)
        gots.append(swap_side(send))
    keep, send = call(
        core_kernel, [((LANES + TILE, LANES), F32), ((LANES + TILE + carried, LANES), F32)],
        *keeps, *gots, *zs,
    )
    core_got = swap_core(send)
    y, known = call(join_kernel, [((LANES, rank), F32), ((TILE, rank), F32)], keep, core_got)
    others = [lax.ppermute(known, "cell", [(c, c ^ d) for c in range(groups)]) for d in (1, 2, 3)]
    (z_out,) = call(z_out_kernel, [((width, rank), F32)], *zs, gots[0], core_got, known, plain=True)
    q_out, scale_out = call(
        functools.partial(q_out_kernel, all_cells),
        [((LANES, rank), F32), ((2 * ITERS + 1, rank), F32)],
        y, known, *others, plain=True,
    )
    return q_out, z_out, scale_out


def solution(mesh):
    return jax.shard_map(
        local,
        mesh=mesh,
        in_specs=(P("cell", "snap"), P("snap", None)),
        out_specs=(P(("cell", "snap"), None), P("snap", None), P()),
        check_vma=False,
    )
```

```python
import functools

import jax
import jax.numpy as jnp
from jax import lax
from jax.experimental import pallas as pl
from jax.experimental.pallas import tpu as pltpu
from jax.sharding import PartitionSpec as P

ITERS = 2
EPS = 1e-05
LANES = 128
TILE = 8
HALVES = 2
QUARTER = 64
COLS = QUARTER // HALVES
BLOCKS = 3
BF16 = jnp.bfloat16
F32 = jnp.float32


def position():
    seat = lax.axis_index("snap")
    core, chip = lax.rem(seat, 2), lax.div(seat, 2)
    inner = jnp.logical_or(chip == 1, chip == 2)
    return core, inner.astype(jnp.int32), chip


def split(x):
    high = x.astype(BF16).astype(F32)
    return high, x - high


def dot(a, b):
    return lax.dot_general(a, b, (((1,), (0,)), ((), ())), preferred_element_type=F32)


def eye(cols):
    shape = (cols, LANES)
    return lax.broadcasted_iota(jnp.int32, shape, 0) == lax.broadcasted_iota(jnp.int32, shape, 1)


def to_column(row, cols):
    return jnp.sum(jnp.where(eye(cols), row, 0.0), axis=1, keepdims=True)


def to_row(column):
    return jnp.sum(jnp.where(eye(column.shape[0]), column, 0.0), axis=0, keepdims=True)


def squares_tile(x):
    row = to_row(jnp.sum(x * x, axis=1, keepdims=True))
    return jnp.broadcast_to(row, (TILE, LANES))


def rms(total, count):
    return jnp.sqrt(total / count + EPS)


def wide(x, cols):
    return jnp.concatenate([x[j * cols : (j + 1) * cols] for j in range(x.shape[0] // cols)], axis=1)


def store_blocks(ref, start, x):
    cols = x.shape[0]
    for j in range(x.shape[1] // LANES):
        ref[start + j * cols : start + (j + 1) * cols, :] = x[:, j * LANES : (j + 1) * LANES]


def turn(x, cols):
    return pltpu.roll(x, cols, 1)


def join_lanes(first, second, cols):
    left = lax.broadcasted_iota(jnp.int32, first.shape, 1) < cols
    return jnp.where(left, first, turn(second, cols))


def unfold(total):
    cols = total.shape[0] // 2
    return total[:cols] + total[cols:]


def store_factors(high_ref, low_ref, blocks, axis=1):
    start = 0
    for block in blocks:
        size = block.shape[axis]
        cut = [slice(None)] * 2
        cut[axis] = slice(start, start + size)
        high, low = split(block)
        high_ref[tuple(cut)] = high.astype(BF16)
        low_ref[tuple(cut)] = low.astype(BF16)
        start += size


def near_kernel(own_ref, core_ref, near_ref, got_ref, y_ref, *refs):
    high_ref, low_ref, high_t_ref, low_t_ref = refs
    blocks = (own_ref[...], core_ref[...])
    store_factors(high_ref, low_ref, blocks)
    store_factors(high_t_ref, low_t_ref, [block.T for block in blocks], 0)
    sketch = jnp.concatenate([near_ref[...], got_ref[...]], axis=0)
    rhs = jnp.concatenate(split(sketch), axis=1).astype(BF16)
    zero = position()[1] == 0
    size = y_ref.shape[0] // (2 * HALVES)
    for b in range(own_ref.shape[0] // LANES):
        cut = slice(b * LANES, (b + 1) * LANES)
        total = dot(high_ref[cut, :], rhs) + dot(low_ref[cut, :], rhs)
        y = (total[:, :LANES] + total[:, LANES:]).T
        low, high = y[:QUARTER], y[QUARTER:]
        for s, x in enumerate((jnp.where(zero, low, high), jnp.where(zero, high, low))):
            for h in range(HALVES):
                at = (s * HALVES + h) * size + b * COLS
                y_ref[at : at + COLS, :] = x[h * COLS : (h + 1) * COLS]


def pack_kernel(own_ref, y_ref, first_ref, second_ref, rest_ref):
    core = position()[0]
    part = rest_ref.shape[0]
    rest_ref[...] = own_ref[own_ref.shape[0] - part :, :]
    middle = wide_rows(own_ref[part : own_ref.shape[0] - part, :])
    y = y_ref[...]
    first_ref[...] = jnp.where(core == 0, middle, y)
    second_ref[...] = jnp.where(core == 0, y, middle)


def wide_rows(x):
    return jnp.concatenate([x[:, :LANES], x[:, LANES:]], axis=0)


def cross_kernel(y_ref, first_ref, second_ref, side_ref, *refs):
    zero = position()[0] == 0
    middle = jnp.where(zero, first_ref[...], second_ref[...])
    count = side_ref.shape[0]
    side_ref[:, :LANES] = middle[:count]
    side_ref[:, LANES:] = middle[count:]
    total = y_ref[...] + jnp.where(zero, second_ref[...], first_ref[...])
    for i, ref in enumerate(refs):
        ref[...] = total[i * ref.shape[0] : (i + 1) * ref.shape[0]]


def split_kernel(*refs):
    blocks, (high_ref, low_ref, high_t_ref, low_t_ref) = [ref[...] for ref in refs[:-4]], refs[-4:]
    store_factors(high_ref, low_ref, blocks, 0)
    store_factors(high_t_ref, low_t_ref, [block.T for block in blocks], 1)


def send_z(y, high_refs, low_refs, z_ref):
    lhs = jnp.concatenate(split(y), axis=0).astype(BF16)
    at = 0
    for high_ref, low_ref in zip(high_refs, low_refs):
        z = unfold(dot(lhs, high_ref[...]) + dot(lhs, low_ref[...]))
        store_blocks(z_ref, at, z)
        at += z.size // LANES
    z_ref[-TILE:, :] = squares_tile(y)


def factors(refs):
    return refs[:BLOCKS], refs[BLOCKS : 2 * BLOCKS]


def first_z_kernel(a_ref, b_ref, *refs):
    high, low = factors(refs)
    send_z(wide(a_ref[...] + b_ref[...], COLS), high, low, refs[-1])


def scaled(own_ref, got_ref, count):
    total = own_ref[...] + got_ref[...]
    scale = rms(total[-TILE:], count)
    return wide(total[:-TILE], COLS) / to_column(scale[:1], COLS), scale


def z_kernel(count, *refs):
    high, low = factors(refs[2:])
    z_ref, scale_ref = refs[-2:]
    y, scale = scaled(refs[0], refs[1], count)
    scale_ref[...] = scale
    send_z(y, high, low, z_ref)


def y_kernel(count, *refs):
    high_refs, low_refs = factors(refs[2:])
    y_ref, scale_ref, *z_refs = refs[2 + 2 * len(high_refs) :]
    z, scale = scaled(refs[0], refs[1], count)
    scale_ref[...] = scale
    for z_ref in z_refs:
        store_blocks(z_ref, 0, z)
    y_ref[-TILE:, :] = squares_tile(z)
    lhs = jnp.concatenate(split(z), axis=0).astype(BF16)
    total, at = None, 0
    for high_ref, low_ref in zip(high_refs, low_refs):
        part = lhs[:, at : at + high_ref.shape[0]]
        term = dot(part, high_ref[...]) + dot(part, low_ref[...])
        total = term if total is None else total + term
        at += high_ref.shape[0]
    store_blocks(y_ref, 0, unfold(total))


def end_kernel(count, carried, own_ref, got_ref, *refs):
    parts, scales, (keep_ref, send_ref, y_ref) = refs[:carried], refs[carried:-3], refs[-3:]
    y, scale = scaled(own_ref, got_ref, count)
    store_blocks(y_ref, 0, y)
    row = lax.broadcasted_iota(jnp.int32, (TILE, LANES), 0)
    tail = squares_tile(y)
    for i, known in enumerate([ref[...] for ref in scales] + [scale]):
        tail = jnp.where(row == i, known, tail)
    size = 2 * COLS
    chip = position()[2]
    for ref, owner in ((keep_ref, chip), (send_ref, chip ^ 1)):
        start = pl.multiple_of(owner * size, size)
        ref[:size, :] = y_ref[pl.ds(start, size), :]
        ref[size : size + TILE, :] = tail
    at = size + TILE
    for ref in parts:
        middle = ref.shape[0] // 2
        send_ref[at : at + middle, :] = ref[middle:, :]
        at += middle


def core_kernel(*refs):
    keeps, gots, parts = (refs[i * HALVES : (i + 1) * HALVES] for i in range(3))
    keep_ref, send_ref = refs[3 * HALVES :]
    core, side, _ = position()
    zero_side, zero_core = side == 0, core == 0
    tail = None
    for s in range(2):
        for h in range(HALVES):
            a, b = keeps[h][...], gots[h][: keeps[h].shape[0], :]
            x = jnp.where(zero_side, a, b) if s == 0 else jnp.where(zero_side, b, a)
            first, second, known = x[:COLS], x[COLS : 2 * COLS], x[2 * COLS :]
            at = (s * HALVES + h) * COLS
            keep_ref[at : at + COLS, :] = jnp.where(zero_core, first, second)
            send_ref[at : at + COLS, :] = jnp.where(zero_core, second, first)
            tail = known if tail is None else join_lanes(tail, known, at)
    keep_ref[LANES : LANES + TILE, :] = tail
    send_ref[LANES : LANES + TILE, :] = tail
    size = 2 * COLS
    for h, ref in enumerate(parts):
        at = LANES + TILE + h * size
        send_ref[at : at + size, :] = ref[size : 2 * size, :]
        at += HALVES * size
        start = keeps[0].shape[0] + (2 * h + 1) * size
        send_ref[at : at + size, :] = gots[0][start : start + size, :]


def join_kernel(keep_ref, got_ref, y_ref, known_ref):
    zero = position()[0] == 0
    keep, got = keep_ref[...], got_ref[: LANES + TILE, :]
    for s, x in enumerate((jnp.where(zero, keep, got), jnp.where(zero, got, keep))):
        cut = slice(s * LANES, (s + 1) * LANES)
        y_ref[:, cut] = x[:LANES].T
        known_ref[:, cut] = x[LANES:]


def z_out_kernel(*refs):
    parts, (side_ref, core_ref, known_ref, z_ref) = refs[:HALVES], refs[HALVES:]
    zero_core, zero_side = (flag == 0 for flag in position()[:2])
    size = 2 * COLS
    side_at, core_at = size + TILE, LANES + TILE
    mine = [ref[:size, :] for ref in parts]
    side = [side_ref[side_at + 2 * h * size : side_at + (2 * h + 1) * size, :] for h in range(HALVES)]
    core = [core_ref[core_at + h * size : core_at + (h + 1) * size, :] for h in range(2 * HALVES)]

    def side_order(own, other):
        low = [jnp.where(zero_side, a, b) for a, b in zip(own, other)]
        high = [jnp.where(zero_side, b, a) for a, b in zip(own, other)]
        return jnp.concatenate([wide(x, COLS) for x in low + high], axis=0)

    ours, theirs = side_order(mine, side), side_order(core[:HALVES], core[HALVES:])
    for s, x in enumerate((jnp.where(zero_core, ours, theirs), jnp.where(zero_core, theirs, ours))):
        cut = slice(s * LANES, (s + 1) * LANES)
        z_ref[:, cut] = x.T / known_ref[2 * ITERS - 1 : 2 * ITERS, cut]


def q_out_kernel(count, y_ref, known_ref, *refs):
    gots, (q_ref, scale_ref) = refs[:-2], refs[-2:]
    last = 2 * ITERS
    row = slice(last, last + 1)
    total = (known_ref[row, :] + gots[0][row, :]) + (gots[1][row, :] + gots[2][row, :])
    scale = rms(total, count)
    q_ref[...] = y_ref[...] / scale
    scale_ref[:last, :] = known_ref[:last, :]
    scale_ref[last:, :] = scale


def call(kernel, outs, *args, plain=False, scratch=(), cost=None):
    out_spec = pl.BlockSpec() if plain else pl.BlockSpec(memory_space=pltpu.VMEM)
    return pl.pallas_call(
        kernel,
        out_shape=[jax.ShapeDtypeStruct(shape, dtype) for shape, dtype in outs],
        in_specs=[pl.BlockSpec(memory_space=pltpu.VMEM)] * len(args),
        out_specs=[out_spec] * len(outs),
        scratch_shapes=scratch,
        cost_estimate=cost,
        compiler_params=pltpu.CompilerParams(vmem_limit_bytes=10 * 1024 * 1024),
    )(*args)


LONG = pl.CostEstimate(flops=10**11, bytes_accessed=2**28, transcendentals=0)


def general(snapshots, sketch):
    high = lax.Precision.HIGHEST
    all_cells = snapshots.shape[0] * lax.axis_size("cell")
    all_snaps = snapshots.shape[1] * lax.axis_size("snap")
    z, scales = sketch, []
    for section in range(ITERS + 1):
        partial = jnp.dot(snapshots, z, precision=high, preferred_element_type=F32)
        y = lax.psum_scatter(partial, "snap", scatter_dimension=0, tiled=True)
        scale = rms(lax.psum(jnp.sum(y * y, axis=0), ("cell", "snap")), all_cells)
        scales.append(scale)
        q = y / scale
        if section < ITERS:
            whole = lax.all_gather(q, "snap", axis=0, tiled=True)
            partial = jnp.dot(snapshots.T, whole, precision=high, preferred_element_type=F32)
            z = lax.psum(partial, "cell")
            scale = rms(lax.psum(jnp.sum(z * z, axis=0), "snap"), all_snaps)
            scales.append(scale)
            z = z / scale
    return q, z, jnp.stack(scales)


def local(snapshots, sketch):
    groups = lax.axis_size("cell")
    places = lax.axis_size("snap")
    rows, width = snapshots.shape
    rank = sketch.shape[1]
    fits = groups == 4 and places == 8 and rank == 4 * QUARTER and rows == 8 * LANES and width == 2 * LANES
    if not fits:
        return general(snapshots, sketch)
    all_cells = rows * groups
    all_snaps = width * places

    def swap(x, bits):
        return lax.ppermute(x, "snap", [(i, i ^ bits) for i in range(places)])

    swap_core = functools.partial(swap, bits=1)
    swap_side = functools.partial(swap, bits=2)
    swap_pair = functools.partial(swap, bits=6)

    def swap_cell(x, step):
        def target(cell, i):
            return cell ^ (1 if i % 2 == step else 2)

        perm = [(c * places + i, target(c, i) * places + i) for c in range(groups) for i in range(places)]
        return lax.ppermute(x, ("cell", "snap"), perm)

    def cell_pair(x):
        x = x + swap_cell(x, 0)
        return x, swap_cell(x, 1)

    def factor(count):
        return [((rows, count * width), BF16)] * 2

    def factor_t(count):
        return [((count * width, rows), BF16)] * 2

    def sketch_half(index):
        return lax.dynamic_slice_in_dim(sketch, index * LANES, LANES, 1)

    core = lax.rem(lax.axis_index("snap"), 2)
    def mixed(x, first):
        return lax.ppermute(x, "snap", [(i, i ^ (2 if i % 2 == first else 6)) for i in range(places)])

    part = rows // 4
    half_rows = rows // LANES * COLS
    sums_shape = ((2 * HALVES * half_rows, LANES), F32)
    side_first = swap_side(snapshots[:part])
    y_near, *near = call(
        near_kernel,
        [sums_shape] + factor(2) + factor_t(2),
        snapshots, swap_core(snapshots), sketch_half(core), swap_core(sketch_half(1 - core)),
    )
    side_first, y_near = lax.optimization_barrier((side_first, y_near))
    first, second, rest = call(pack_kernel, [sums_shape] * 2 + [((part, width), F32)], snapshots, y_near)
    first, second = mixed(first, 0), mixed(second, 1)
    side_rest = swap_side(rest)
    side_middle, *sums = call(
        cross_kernel,
        [((2 * part, width), F32)] + [((half_rows, LANES), F32)] * 2 * HALVES,
        y_near, first, second,
    )
    own, others = sums[:HALVES], sums[HALVES:]
    got = [swap_side(other) for other in others]
    side_blocks = (side_first, side_middle, side_rest)
    side = call(split_kernel, factor(1) + factor_t(1), *side_blocks)
    diagonals = [swap_core(block) for block in side_blocks]
    far = call(split_kernel, factor(1) + factor_t(1), *diagonals, cost=LONG)
    matrix = (near[0], side[0], far[0], near[1], side[1], far[1])
    matrix_t = (near[2], side[2], far[2], near[3], side[3], far[3])

    flat = (COLS * rows // LANES + TILE, LANES)
    sent_shape = ((COLS * 4 * width // LANES + TILE, LANES), F32)
    y_shape = (flat, F32)
    scale_shape = ((TILE, LANES), F32)
    z_shape = ((COLS * 4 * width // LANES, LANES), F32)
    scales = [[] for _ in range(HALVES)]
    sent = [call(first_z_kernel, [sent_shape], y, g, *matrix, cost=LONG)[0] for y, g in zip(own, got)]
    ys, zs = [None] * HALVES, [None] * HALVES
    for section in range(ITERS):
        last = section == ITERS - 1
        for h in range(HALVES):
            ys[h], scale, *z = call(
                functools.partial(y_kernel, all_cells), [y_shape, scale_shape] + [z_shape] * last,
                *cell_pair(sent[h]), *matrix_t,
            )
            scales[h].append(scale)
            if last:
                zs[h] = z[0]
                continue
            sent[h], scale = call(
                functools.partial(z_kernel, all_snaps), [sent_shape, scale_shape],
                ys[h], swap_pair(ys[h]), *matrix,
            )
            scales[h].append(scale)

    small = (2 * COLS + TILE, LANES)
    carried = HALVES * z_shape[0][0] // 2
    keeps, gots = [], []
    for h in range(HALVES):
        parts = zs if h == 0 else []
        keep, send = call(
            functools.partial(end_kernel, all_snaps, len(parts)),
            [(small, F32), ((small[0] + carried * (h == 0), LANES), F32)],
            ys[h], swap_pair(ys[h]), *parts, *scales[h],
            scratch=[pltpu.VMEM((flat[0] - TILE, LANES), F32)],
        )
        keeps.append(keep)
        gots.append(swap_side(send))
    keep, send = call(
        core_kernel, [((LANES + TILE, LANES), F32), ((LANES + TILE + carried, LANES), F32)],
        *keeps, *gots, *zs,
    )
    core_got = swap_core(send)
    y, known = call(join_kernel, [((LANES, rank), F32), ((TILE, rank), F32)], keep, core_got)
    others = [lax.ppermute(known, "cell", [(c, c ^ d) for c in range(groups)]) for d in (1, 2, 3)]
    (z_out,) = call(z_out_kernel, [((width, rank), F32)], *zs, gots[0], core_got, known, plain=True)
    q_out, scale_out = call(
        functools.partial(q_out_kernel, all_cells),
        [((LANES, rank), F32), ((2 * ITERS + 1, rank), F32)],
        y, known, *others, plain=True,
    )
    return q_out, z_out, scale_out


def solution(mesh):
    return jax.shard_map(
        local,
        mesh=mesh,
        in_specs=(P("cell", "snap"), P("snap", None)),
        out_specs=(P(("cell", "snap"), None), P("snap", None), P()),
        check_vma=False,
    )
```

```python
import functools

import jax
import jax.numpy as jnp
from jax import lax
from jax.experimental import pallas as pl
from jax.experimental.pallas import tpu as pltpu
from jax.sharding import PartitionSpec as P

ITERS = 2
EPS = 1e-05
LANES = 128
TILE = 8
HALVES = 2
QUARTER = 64
COLS = QUARTER // HALVES
BLOCKS = 3
BF16 = jnp.bfloat16
F32 = jnp.float32


def position():
    seat = lax.axis_index("snap")
    core, chip = lax.rem(seat, 2), lax.div(seat, 2)
    inner = jnp.logical_or(chip == 1, chip == 2)
    return core, inner.astype(jnp.int32), chip


def split(x):
    high = x.astype(BF16).astype(F32)
    return high, x - high


def dot(a, b):
    return lax.dot_general(a, b, (((1,), (0,)), ((), ())), preferred_element_type=F32)


def eye(cols):
    shape = (cols, LANES)
    return lax.broadcasted_iota(jnp.int32, shape, 0) == lax.broadcasted_iota(jnp.int32, shape, 1)


def to_column(row, cols):
    return jnp.sum(jnp.where(eye(cols), row, 0.0), axis=1, keepdims=True)


def to_row(column):
    return jnp.sum(jnp.where(eye(column.shape[0]), column, 0.0), axis=0, keepdims=True)


def squares_tile(x):
    row = to_row(jnp.sum(x * x, axis=1, keepdims=True))
    return jnp.broadcast_to(row, (TILE, LANES))


def rms(total, count):
    return jnp.sqrt(total / count + EPS)


def wide(x, cols):
    return jnp.concatenate([x[j * cols : (j + 1) * cols] for j in range(x.shape[0] // cols)], axis=1)


def store_blocks(ref, start, x):
    cols = x.shape[0]
    for j in range(x.shape[1] // LANES):
        ref[start + j * cols : start + (j + 1) * cols, :] = x[:, j * LANES : (j + 1) * LANES]


def turn(x, cols):
    return pltpu.roll(x, cols, 1)


def join_lanes(first, second, cols):
    left = lax.broadcasted_iota(jnp.int32, first.shape, 1) < cols
    return jnp.where(left, first, turn(second, cols))


def unfold(total):
    cols = total.shape[0] // 2
    return total[:cols] + total[cols:]


def sketch_sides(x):
    high, low = split(x)
    own = join_lanes(high, low, QUARTER)
    other = join_lanes(turn(high, QUARTER), turn(low, QUARTER), QUARTER)
    return own.astype(BF16), other.astype(BF16)


def store_factors(high_ref, low_ref, blocks, axis=1):
    start = 0
    for block in blocks:
        size = block.shape[axis]
        cut = [slice(None)] * 2
        cut[axis] = slice(start, start + size)
        high, low = split(block)
        high_ref[tuple(cut)] = high.astype(BF16)
        low_ref[tuple(cut)] = low.astype(BF16)
        start += size


def prepare_kernel(near_ref, got_ref, mine_ref, theirs_ref):
    near, got = near_ref[...], got_ref[...]
    low = join_lanes(near, got, QUARTER)
    high = join_lanes(turn(near, QUARTER), turn(got, QUARTER), QUARTER)
    zero = position()[1] == 0
    mine_ref[...] = jnp.where(zero, low, high)
    theirs_ref[...] = jnp.where(zero, high, low)


def near_kernel(own_ref, core_ref, sketch_ref, y_ref, high_ref, low_ref, high_t_ref, low_t_ref):
    blocks = (own_ref[...], core_ref[...])
    store_factors(high_ref, low_ref, blocks)
    store_factors(high_t_ref, low_t_ref, [block.T for block in blocks], 0)
    rhs = jnp.concatenate(sketch_sides(sketch_ref[...]), axis=0)
    for b in range(own_ref.shape[0] // LANES):
        cut = slice(b * LANES, (b + 1) * LANES)
        total = dot(high_ref[cut, :], rhs) + dot(low_ref[cut, :], rhs)
        y_ref[b * QUARTER : (b + 1) * QUARTER, :] = unfold(total.T)


def side_split_kernel(side_ref, high_ref, low_ref, high_t_ref, low_t_ref):
    store_factors(high_ref, low_ref, (side_ref[...],))
    store_factors(high_t_ref, low_t_ref, (side_ref[...].T,), 0)


def side_kernel(high_ref, low_ref, sketch_ref, near_ref, y_ref):
    rhs = sketch_sides(sketch_ref[...])[0]
    for b in range(high_ref.shape[0] // LANES):
        cut = slice(b * LANES, (b + 1) * LANES)
        total = dot(high_ref[cut, :], rhs) + dot(low_ref[cut, :], rhs)
        out = slice(b * QUARTER, (b + 1) * QUARTER)
        y_ref[out, :] = unfold(total.T) + near_ref[out, :]


def add_far(h, high_ref, low_ref, sketch_ref, near_ref, y_ref):
    rhs = sketch_sides(sketch_ref[...])[1]
    for b in range(high_ref.shape[0] // LANES):
        cut = slice(b * LANES, (b + 1) * LANES)
        total = dot(high_ref[cut, :], rhs) + dot(low_ref[cut, :], rhs)
        y = unfold(total.T)[h * COLS : (h + 1) * COLS]
        at = b * QUARTER + h * COLS
        y_ref[b * COLS : (b + 1) * COLS, :] = y + near_ref[at : at + COLS, :]


def far_kernel(diagonal_ref, sketch_ref, near_ref, y_ref, high_ref, low_ref):
    store_factors(high_ref, low_ref, (diagonal_ref[...],))
    add_far(0, high_ref, low_ref, sketch_ref, near_ref, y_ref)


def second_far_kernel(diagonal_ref, high_ref, low_ref, sketch_ref, near_ref, y_ref, high_t_ref, low_t_ref):
    add_far(1, high_ref, low_ref, sketch_ref, near_ref, y_ref)
    store_factors(high_t_ref, low_t_ref, (diagonal_ref[...].T,), 0)


def send_z(y, high_refs, low_refs, z_ref):
    lhs = jnp.concatenate(split(y), axis=0).astype(BF16)
    at = 0
    for high_ref, low_ref in zip(high_refs, low_refs):
        z = unfold(dot(lhs, high_ref[...]) + dot(lhs, low_ref[...]))
        store_blocks(z_ref, at, z)
        at += z.size // LANES
    z_ref[-TILE:, :] = squares_tile(y)


def factors(refs):
    return refs[:BLOCKS], refs[BLOCKS : 2 * BLOCKS]


def first_z_kernel(a_ref, b_ref, *refs):
    high, low = factors(refs)
    send_z(wide(a_ref[...] + b_ref[...], COLS), high, low, refs[-1])


def scaled(own_ref, got_ref, count):
    total = own_ref[...] + got_ref[...]
    scale = rms(total[-TILE:], count)
    return wide(total[:-TILE], COLS) / to_column(scale[:1], COLS), scale


def z_kernel(count, *refs):
    high, low = factors(refs[2:])
    z_ref, scale_ref = refs[-2:]
    y, scale = scaled(refs[0], refs[1], count)
    scale_ref[...] = scale
    send_z(y, high, low, z_ref)


def y_kernel(count, *refs):
    high_refs, low_refs = factors(refs[2:])
    y_ref, scale_ref, *z_refs = refs[2 + 2 * len(high_refs) :]
    z, scale = scaled(refs[0], refs[1], count)
    scale_ref[...] = scale
    for z_ref in z_refs:
        store_blocks(z_ref, 0, z)
    y_ref[-TILE:, :] = squares_tile(z)
    lhs = jnp.concatenate(split(z), axis=0).astype(BF16)
    total, at = None, 0
    for high_ref, low_ref in zip(high_refs, low_refs):
        part = lhs[:, at : at + high_ref.shape[0]]
        term = dot(part, high_ref[...]) + dot(part, low_ref[...])
        total = term if total is None else total + term
        at += high_ref.shape[0]
    store_blocks(y_ref, 0, unfold(total))


def end_kernel(count, carried, own_ref, got_ref, *refs):
    parts, scales, (keep_ref, send_ref, y_ref) = refs[:carried], refs[carried:-3], refs[-3:]
    y, scale = scaled(own_ref, got_ref, count)
    store_blocks(y_ref, 0, y)
    row = lax.broadcasted_iota(jnp.int32, (TILE, LANES), 0)
    tail = squares_tile(y)
    for i, known in enumerate([ref[...] for ref in scales] + [scale]):
        tail = jnp.where(row == i, known, tail)
    size = 2 * COLS
    chip = position()[2]
    for ref, owner in ((keep_ref, chip), (send_ref, chip ^ 1)):
        start = pl.multiple_of(owner * size, size)
        ref[:size, :] = y_ref[pl.ds(start, size), :]
        ref[size : size + TILE, :] = tail
    at = size + TILE
    for ref in parts:
        middle = ref.shape[0] // 2
        send_ref[at : at + middle, :] = ref[middle:, :]
        at += middle


def core_kernel(*refs):
    keeps, gots, parts = (refs[i * HALVES : (i + 1) * HALVES] for i in range(3))
    keep_ref, send_ref = refs[3 * HALVES :]
    core, side, _ = position()
    zero_side, zero_core = side == 0, core == 0
    tail = None
    for s in range(2):
        for h in range(HALVES):
            a, b = keeps[h][...], gots[h][: keeps[h].shape[0], :]
            x = jnp.where(zero_side, a, b) if s == 0 else jnp.where(zero_side, b, a)
            first, second, known = x[:COLS], x[COLS : 2 * COLS], x[2 * COLS :]
            at = (s * HALVES + h) * COLS
            keep_ref[at : at + COLS, :] = jnp.where(zero_core, first, second)
            send_ref[at : at + COLS, :] = jnp.where(zero_core, second, first)
            tail = known if tail is None else join_lanes(tail, known, at)
    keep_ref[LANES : LANES + TILE, :] = tail
    send_ref[LANES : LANES + TILE, :] = tail
    size = 2 * COLS
    for h, ref in enumerate(parts):
        at = LANES + TILE + h * size
        send_ref[at : at + size, :] = ref[size : 2 * size, :]
        at += HALVES * size
        start = keeps[0].shape[0] + (2 * h + 1) * size
        send_ref[at : at + size, :] = gots[0][start : start + size, :]


def join_kernel(keep_ref, got_ref, y_ref, known_ref):
    zero = position()[0] == 0
    keep, got = keep_ref[...], got_ref[: LANES + TILE, :]
    for s, x in enumerate((jnp.where(zero, keep, got), jnp.where(zero, got, keep))):
        cut = slice(s * LANES, (s + 1) * LANES)
        y_ref[:, cut] = x[:LANES].T
        known_ref[:, cut] = x[LANES:]


def z_out_kernel(*refs):
    parts, (side_ref, core_ref, known_ref, z_ref) = refs[:HALVES], refs[HALVES:]
    zero_core, zero_side = (flag == 0 for flag in position()[:2])
    size = 2 * COLS
    side_at, core_at = size + TILE, LANES + TILE
    mine = [ref[:size, :] for ref in parts]
    side = [side_ref[side_at + 2 * h * size : side_at + (2 * h + 1) * size, :] for h in range(HALVES)]
    core = [core_ref[core_at + h * size : core_at + (h + 1) * size, :] for h in range(2 * HALVES)]

    def side_order(own, other):
        low = [jnp.where(zero_side, a, b) for a, b in zip(own, other)]
        high = [jnp.where(zero_side, b, a) for a, b in zip(own, other)]
        return jnp.concatenate([wide(x, COLS) for x in low + high], axis=0)

    ours, theirs = side_order(mine, side), side_order(core[:HALVES], core[HALVES:])
    for s, x in enumerate((jnp.where(zero_core, ours, theirs), jnp.where(zero_core, theirs, ours))):
        cut = slice(s * LANES, (s + 1) * LANES)
        z_ref[:, cut] = x.T / known_ref[2 * ITERS - 1 : 2 * ITERS, cut]


def q_out_kernel(count, y_ref, known_ref, *refs):
    gots, (q_ref, scale_ref) = refs[:-2], refs[-2:]
    last = 2 * ITERS
    row = slice(last, last + 1)
    total = (known_ref[row, :] + gots[0][row, :]) + (gots[1][row, :] + gots[2][row, :])
    scale = rms(total, count)
    q_ref[...] = y_ref[...] / scale
    scale_ref[:last, :] = known_ref[:last, :]
    scale_ref[last:, :] = scale


def call(kernel, outs, *args, plain=False, scratch=(), cost=None):
    out_spec = pl.BlockSpec() if plain else pl.BlockSpec(memory_space=pltpu.VMEM)
    return pl.pallas_call(
        kernel,
        out_shape=[jax.ShapeDtypeStruct(shape, dtype) for shape, dtype in outs],
        in_specs=[pl.BlockSpec(memory_space=pltpu.VMEM)] * len(args),
        out_specs=[out_spec] * len(outs),
        scratch_shapes=scratch,
        cost_estimate=cost,
        compiler_params=pltpu.CompilerParams(vmem_limit_bytes=16 * 1024 * 1024),
    )(*args)


LONG = pl.CostEstimate(flops=10**11, bytes_accessed=2**28, transcendentals=0)


def general(snapshots, sketch):
    high = lax.Precision.HIGHEST
    all_cells = snapshots.shape[0] * lax.axis_size("cell")
    all_snaps = snapshots.shape[1] * lax.axis_size("snap")
    z, scales = sketch, []
    for section in range(ITERS + 1):
        partial = jnp.dot(snapshots, z, precision=high, preferred_element_type=F32)
        y = lax.psum_scatter(partial, "snap", scatter_dimension=0, tiled=True)
        scale = rms(lax.psum(jnp.sum(y * y, axis=0), ("cell", "snap")), all_cells)
        scales.append(scale)
        q = y / scale
        if section < ITERS:
            whole = lax.all_gather(q, "snap", axis=0, tiled=True)
            partial = jnp.dot(snapshots.T, whole, precision=high, preferred_element_type=F32)
            z = lax.psum(partial, "cell")
            scale = rms(lax.psum(jnp.sum(z * z, axis=0), "snap"), all_snaps)
            scales.append(scale)
            z = z / scale
    return q, z, jnp.stack(scales)


def local(snapshots, sketch):
    groups = lax.axis_size("cell")
    places = lax.axis_size("snap")
    rows, width = snapshots.shape
    rank = sketch.shape[1]
    fits = groups == 4 and places == 8 and rank == 4 * QUARTER and rows == 8 * LANES and width == 2 * LANES
    if not fits:
        return general(snapshots, sketch)
    all_cells = rows * groups
    all_snaps = width * places

    def swap(x, bits):
        return lax.ppermute(x, "snap", [(i, i ^ bits) for i in range(places)])

    swap_core = functools.partial(swap, bits=1)
    swap_side = functools.partial(swap, bits=2)
    swap_pair = functools.partial(swap, bits=6)

    def swap_cell(x, step):
        def target(cell, i):
            return cell ^ (1 if i % 2 == step else 2)

        perm = [(c * places + i, target(c, i) * places + i) for c in range(groups) for i in range(places)]
        return lax.ppermute(x, ("cell", "snap"), perm)

    def cell_pair(x):
        x = x + swap_cell(x, 0)
        return x, swap_cell(x, 1)

    def factor(count):
        return [((rows, count * width), BF16)] * 2

    def factor_t(count):
        return [((count * width, rows), BF16)] * 2

    def sketch_half(index):
        return lax.dynamic_slice_in_dim(sketch, index * LANES, LANES, 1)

    core = lax.rem(lax.axis_index("snap"), 2)
    side_block = swap_side(snapshots)
    packed = ((width, LANES), F32)
    mine, theirs = call(prepare_kernel, [packed, packed], sketch_half(core), swap_core(sketch_half(1 - core)))
    side_sketch = swap_side(theirs)
    quarter_shape = ((rows // LANES * QUARTER, LANES), F32)
    near_y, *near = call(
        near_kernel, [quarter_shape] + factor(2) + factor_t(2), snapshots, swap_core(snapshots), mine
    )
    side_block, near_y = lax.optimization_barrier((side_block, near_y))
    side = call(side_split_kernel, factor(1) + factor_t(1), side_block)
    (side_y,) = call(side_kernel, [quarter_shape], *side[:2], side_sketch, near_y, cost=LONG)
    half_shape = ((rows // LANES * COLS, LANES), F32)
    diagonal = swap_core(side_block)
    own_first, *far = call(far_kernel, [half_shape] + factor(1), diagonal, side_sketch, side_y)
    own_second, *far_t = call(
        second_far_kernel, [half_shape] + factor_t(1), diagonal, *far, side_sketch, side_y
    )
    own = (own_first, own_second)
    matrix = (near[0], side[0], far[0], near[1], side[1], far[1])
    matrix_t = (near[2], side[2], far_t[0], near[3], side[3], far_t[1])

    flat = (COLS * rows // LANES + TILE, LANES)
    sent_shape = ((COLS * 4 * width // LANES + TILE, LANES), F32)
    y_shape = (flat, F32)
    scale_shape = ((TILE, LANES), F32)
    z_shape = ((COLS * 4 * width // LANES, LANES), F32)
    scales = [[] for _ in range(HALVES)]
    first_got = swap_pair(own[0])
    later, first_got = lax.optimization_barrier((own[1], first_got))
    own, got = (own[0], later), (first_got, swap_pair(later))
    sent = [call(first_z_kernel, [sent_shape], y, g, *matrix, cost=LONG)[0] for y, g in zip(own, got)]
    ys, zs = [None] * HALVES, [None] * HALVES
    for section in range(ITERS):
        last = section == ITERS - 1
        for h in range(HALVES):
            ys[h], scale, *z = call(
                functools.partial(y_kernel, all_cells), [y_shape, scale_shape] + [z_shape] * last,
                *cell_pair(sent[h]), *matrix_t,
            )
            scales[h].append(scale)
            if last:
                zs[h] = z[0]
                continue
            sent[h], scale = call(
                functools.partial(z_kernel, all_snaps), [sent_shape, scale_shape],
                ys[h], swap_pair(ys[h]), *matrix,
            )
            scales[h].append(scale)

    small = (2 * COLS + TILE, LANES)
    carried = HALVES * z_shape[0][0] // 2
    keeps, gots = [], []
    for h in range(HALVES):
        parts = zs if h == 0 else []
        keep, send = call(
            functools.partial(end_kernel, all_snaps, len(parts)),
            [(small, F32), ((small[0] + carried * (h == 0), LANES), F32)],
            ys[h], swap_pair(ys[h]), *parts, *scales[h],
            scratch=[pltpu.VMEM((flat[0] - TILE, LANES), F32)],
        )
        keeps.append(keep)
        gots.append(swap_side(send))
    keep, send = call(
        core_kernel, [((LANES + TILE, LANES), F32), ((LANES + TILE + carried, LANES), F32)],
        *keeps, *gots, *zs,
    )
    core_got = swap_core(send)
    y, known = call(join_kernel, [((LANES, rank), F32), ((TILE, rank), F32)], keep, core_got)
    others = [lax.ppermute(known, "cell", [(c, c ^ d) for c in range(groups)]) for d in (1, 2, 3)]
    (z_out,) = call(z_out_kernel, [((width, rank), F32)], *zs, gots[0], core_got, known, plain=True)
    q_out, scale_out = call(
        functools.partial(q_out_kernel, all_cells),
        [((LANES, rank), F32), ((2 * ITERS + 1, rank), F32)],
        y, known, *others, plain=True,
    )
    return q_out, z_out, scale_out


def solution(mesh):
    return jax.shard_map(
        local,
        mesh=mesh,
        in_specs=(P("cell", "snap"), P("snap", None)),
        out_specs=(P(("cell", "snap"), None), P("snap", None), P()),
        check_vma=False,
    )
```

```python
import functools

import jax
import jax.numpy as jnp
from jax import lax
from jax.experimental import pallas as pl
from jax.experimental.pallas import tpu as pltpu
from jax.sharding import PartitionSpec as P

ITERS = 2
EPS = 1e-05
LANES = 128
TILE = 8
HALVES = 2
QUARTER = 64
COLS = QUARTER // HALVES
BLOCKS = 3
BF16 = jnp.bfloat16
F32 = jnp.float32


def position():
    seat = lax.axis_index("snap")
    core, chip = lax.rem(seat, 2), lax.div(seat, 2)
    inner = jnp.logical_or(chip == 1, chip == 2)
    return core, inner.astype(jnp.int32), chip


def split(x):
    high = x.astype(BF16).astype(F32)
    return high, x - high


def dot(a, b):
    return lax.dot_general(a, b, (((1,), (0,)), ((), ())), preferred_element_type=F32)


def eye(cols):
    shape = (cols, LANES)
    return lax.broadcasted_iota(jnp.int32, shape, 0) == lax.broadcasted_iota(jnp.int32, shape, 1)


def to_column(row, cols):
    return jnp.sum(jnp.where(eye(cols), row, 0.0), axis=1, keepdims=True)


def to_row(column):
    return jnp.sum(jnp.where(eye(column.shape[0]), column, 0.0), axis=0, keepdims=True)


def squares_tile(x):
    row = to_row(jnp.sum(x * x, axis=1, keepdims=True))
    return jnp.broadcast_to(row, (TILE, LANES))


def rms(total, count):
    return jnp.sqrt(total / count + EPS)


def wide(x, cols):
    return jnp.concatenate([x[j * cols : (j + 1) * cols] for j in range(x.shape[0] // cols)], axis=1)


def store_blocks(ref, start, x):
    cols = x.shape[0]
    for j in range(x.shape[1] // LANES):
        ref[start + j * cols : start + (j + 1) * cols, :] = x[:, j * LANES : (j + 1) * LANES]


def turn(x, cols):
    return pltpu.roll(x, cols, 1)


def join_lanes(first, second, cols):
    left = lax.broadcasted_iota(jnp.int32, first.shape, 1) < cols
    return jnp.where(left, first, turn(second, cols))


def unfold(total):
    cols = total.shape[0] // 2
    return total[:cols] + total[cols:]


def sketch_sides(x):
    high, low = split(x)
    own = join_lanes(high, low, QUARTER)
    other = join_lanes(turn(high, QUARTER), turn(low, QUARTER), QUARTER)
    return own.astype(BF16), other.astype(BF16)


def store_factors(high_ref, low_ref, blocks, axis=1):
    start = 0
    for block in blocks:
        size = block.shape[axis]
        cut = [slice(None)] * 2
        cut[axis] = slice(start, start + size)
        high, low = split(block)
        high_ref[tuple(cut)] = high.astype(BF16)
        low_ref[tuple(cut)] = low.astype(BF16)
        start += size


def prepare_kernel(near_ref, got_ref, mine_ref, theirs_ref):
    near, got = near_ref[...], got_ref[...]
    low = join_lanes(near, got, QUARTER)
    high = join_lanes(turn(near, QUARTER), turn(got, QUARTER), QUARTER)
    zero = position()[1] == 0
    mine_ref[...] = jnp.where(zero, low, high)
    theirs_ref[...] = jnp.where(zero, high, low)


def near_kernel(own_ref, core_ref, sketch_ref, y_ref, high_ref, low_ref, high_t_ref, low_t_ref):
    blocks = (own_ref[...], core_ref[...])
    store_factors(high_ref, low_ref, blocks)
    store_factors(high_t_ref, low_t_ref, [block.T for block in blocks], 0)
    rhs = jnp.concatenate(sketch_sides(sketch_ref[...]), axis=0)
    for b in range(own_ref.shape[0] // LANES):
        cut = slice(b * LANES, (b + 1) * LANES)
        total = dot(high_ref[cut, :], rhs) + dot(low_ref[cut, :], rhs)
        y_ref[b * QUARTER : (b + 1) * QUARTER, :] = unfold(total.T)


def side_split_kernel(side_ref, high_ref, low_ref, high_t_ref, low_t_ref):
    store_factors(high_ref, low_ref, (side_ref[...],))
    store_factors(high_t_ref, low_t_ref, (side_ref[...].T,), 0)


def side_kernel(high_ref, low_ref, sketch_ref, near_ref, y_ref):
    rhs = sketch_sides(sketch_ref[...])[0]
    for b in range(high_ref.shape[0] // LANES):
        cut = slice(b * LANES, (b + 1) * LANES)
        total = dot(high_ref[cut, :], rhs) + dot(low_ref[cut, :], rhs)
        out = slice(b * QUARTER, (b + 1) * QUARTER)
        y_ref[out, :] = unfold(total.T) + near_ref[out, :]


def add_far(h, high_ref, low_ref, sketch_ref, near_ref, y_ref):
    rhs = sketch_sides(sketch_ref[...])[1]
    for b in range(high_ref.shape[0] // LANES):
        cut = slice(b * LANES, (b + 1) * LANES)
        total = dot(high_ref[cut, :], rhs) + dot(low_ref[cut, :], rhs)
        y = unfold(total.T)[h * COLS : (h + 1) * COLS]
        at = b * QUARTER + h * COLS
        y_ref[b * COLS : (b + 1) * COLS, :] = y + near_ref[at : at + COLS, :]


def far_kernel(diagonal_ref, sketch_ref, near_ref, y_ref, high_ref, low_ref):
    store_factors(high_ref, low_ref, (diagonal_ref[...],))
    add_far(0, high_ref, low_ref, sketch_ref, near_ref, y_ref)


def second_far_kernel(diagonal_ref, high_ref, low_ref, sketch_ref, near_ref, y_ref, high_t_ref, low_t_ref):
    add_far(1, high_ref, low_ref, sketch_ref, near_ref, y_ref)
    store_factors(high_t_ref, low_t_ref, (diagonal_ref[...].T,), 0)


def send_z(y, high_refs, low_refs, z_ref):
    lhs = jnp.concatenate(split(y), axis=0).astype(BF16)
    at = 0
    for high_ref, low_ref in zip(high_refs, low_refs):
        z = unfold(dot(lhs, high_ref[...]) + dot(lhs, low_ref[...]))
        store_blocks(z_ref, at, z)
        at += z.size // LANES
    z_ref[-TILE:, :] = squares_tile(y)


def factors(refs):
    return refs[:BLOCKS], refs[BLOCKS : 2 * BLOCKS]


def first_z_kernel(a_ref, b_ref, *refs):
    high, low = factors(refs)
    send_z(wide(a_ref[...] + b_ref[...], COLS), high, low, refs[-1])


def scaled(own_ref, got_ref, count):
    total = own_ref[...] + got_ref[...]
    scale = rms(total[-TILE:], count)
    return wide(total[:-TILE], COLS) / to_column(scale[:1], COLS), scale


def z_kernel(count, *refs):
    high, low = factors(refs[2:])
    z_ref, scale_ref = refs[-2:]
    y, scale = scaled(refs[0], refs[1], count)
    scale_ref[...] = scale
    send_z(y, high, low, z_ref)


def y_kernel(count, *refs):
    high_refs, low_refs = factors(refs[2:])
    y_ref, scale_ref, *z_refs = refs[2 + 2 * len(high_refs) :]
    z, scale = scaled(refs[0], refs[1], count)
    scale_ref[...] = scale
    for z_ref in z_refs:
        store_blocks(z_ref, 0, z)
    y_ref[-TILE:, :] = squares_tile(z)
    lhs = jnp.concatenate(split(z), axis=0).astype(BF16)
    total, at = None, 0
    for high_ref, low_ref in zip(high_refs, low_refs):
        part = lhs[:, at : at + high_ref.shape[0]]
        term = dot(part, high_ref[...]) + dot(part, low_ref[...])
        total = term if total is None else total + term
        at += high_ref.shape[0]
    store_blocks(y_ref, 0, unfold(total))


def end_kernel(count, carried, own_ref, got_ref, *refs):
    parts, scales, (keep_ref, send_ref, y_ref) = refs[:carried], refs[carried:-3], refs[-3:]
    y, scale = scaled(own_ref, got_ref, count)
    store_blocks(y_ref, 0, y)
    row = lax.broadcasted_iota(jnp.int32, (TILE, LANES), 0)
    tail = squares_tile(y)
    for i, known in enumerate([ref[...] for ref in scales] + [scale]):
        tail = jnp.where(row == i, known, tail)
    size = 2 * COLS
    chip = position()[2]
    for ref, owner in ((keep_ref, chip), (send_ref, chip ^ 1)):
        start = pl.multiple_of(owner * size, size)
        ref[:size, :] = y_ref[pl.ds(start, size), :]
        ref[size : size + TILE, :] = tail
    at = size + TILE
    for ref in parts:
        middle = ref.shape[0] // 2
        send_ref[at : at + middle, :] = ref[middle:, :]
        at += middle


def core_kernel(*refs):
    keeps, gots, parts = (refs[i * HALVES : (i + 1) * HALVES] for i in range(3))
    keep_ref, send_ref = refs[3 * HALVES :]
    core, side, _ = position()
    zero_side, zero_core = side == 0, core == 0
    tail = None
    for s in range(2):
        for h in range(HALVES):
            a, b = keeps[h][...], gots[h][: keeps[h].shape[0], :]
            x = jnp.where(zero_side, a, b) if s == 0 else jnp.where(zero_side, b, a)
            first, second, known = x[:COLS], x[COLS : 2 * COLS], x[2 * COLS :]
            at = (s * HALVES + h) * COLS
            keep_ref[at : at + COLS, :] = jnp.where(zero_core, first, second)
            send_ref[at : at + COLS, :] = jnp.where(zero_core, second, first)
            tail = known if tail is None else join_lanes(tail, known, at)
    keep_ref[LANES : LANES + TILE, :] = tail
    send_ref[LANES : LANES + TILE, :] = tail
    size = 2 * COLS
    for h, ref in enumerate(parts):
        at = LANES + TILE + h * size
        send_ref[at : at + size, :] = ref[size : 2 * size, :]
        at += HALVES * size
        start = keeps[0].shape[0] + (2 * h + 1) * size
        send_ref[at : at + size, :] = gots[0][start : start + size, :]


def join_kernel(keep_ref, got_ref, y_ref, known_ref):
    zero = position()[0] == 0
    keep, got = keep_ref[...], got_ref[: LANES + TILE, :]
    for s, x in enumerate((jnp.where(zero, keep, got), jnp.where(zero, got, keep))):
        cut = slice(s * LANES, (s + 1) * LANES)
        y_ref[:, cut] = x[:LANES].T
        known_ref[:, cut] = x[LANES:]


def z_out_kernel(*refs):
    parts, (side_ref, core_ref, known_ref, z_ref) = refs[:HALVES], refs[HALVES:]
    zero_core, zero_side = (flag == 0 for flag in position()[:2])
    size = 2 * COLS
    side_at, core_at = size + TILE, LANES + TILE
    mine = [ref[:size, :] for ref in parts]
    side = [side_ref[side_at + 2 * h * size : side_at + (2 * h + 1) * size, :] for h in range(HALVES)]
    core = [core_ref[core_at + h * size : core_at + (h + 1) * size, :] for h in range(2 * HALVES)]

    def side_order(own, other):
        low = [jnp.where(zero_side, a, b) for a, b in zip(own, other)]
        high = [jnp.where(zero_side, b, a) for a, b in zip(own, other)]
        return jnp.concatenate([wide(x, COLS) for x in low + high], axis=0)

    ours, theirs = side_order(mine, side), side_order(core[:HALVES], core[HALVES:])
    for s, x in enumerate((jnp.where(zero_core, ours, theirs), jnp.where(zero_core, theirs, ours))):
        cut = slice(s * LANES, (s + 1) * LANES)
        z_ref[:, cut] = x.T / known_ref[2 * ITERS - 1 : 2 * ITERS, cut]


def q_out_kernel(count, y_ref, known_ref, *refs):
    gots, (q_ref, scale_ref) = refs[:-2], refs[-2:]
    last = 2 * ITERS
    row = slice(last, last + 1)
    total = (known_ref[row, :] + gots[0][row, :]) + (gots[1][row, :] + gots[2][row, :])
    scale = rms(total, count)
    q_ref[...] = y_ref[...] / scale
    scale_ref[:last, :] = known_ref[:last, :]
    scale_ref[last:, :] = scale


def call(kernel, outs, *args, plain=False, scratch=(), cost=None):
    out_spec = pl.BlockSpec() if plain else pl.BlockSpec(memory_space=pltpu.VMEM)
    return pl.pallas_call(
        kernel,
        out_shape=[jax.ShapeDtypeStruct(shape, dtype) for shape, dtype in outs],
        in_specs=[pl.BlockSpec(memory_space=pltpu.VMEM)] * len(args),
        out_specs=[out_spec] * len(outs),
        scratch_shapes=scratch,
        cost_estimate=cost,
        compiler_params=pltpu.CompilerParams(vmem_limit_bytes=16 * 1024 * 1024),
    )(*args)


LONG = pl.CostEstimate(flops=10**11, bytes_accessed=2**28, transcendentals=0)


def general(snapshots, sketch):
    high = lax.Precision.HIGHEST
    all_cells = snapshots.shape[0] * lax.axis_size("cell")
    all_snaps = snapshots.shape[1] * lax.axis_size("snap")
    z, scales = sketch, []
    for section in range(ITERS + 1):
        partial = jnp.dot(snapshots, z, precision=high, preferred_element_type=F32)
        y = lax.psum_scatter(partial, "snap", scatter_dimension=0, tiled=True)
        scale = rms(lax.psum(jnp.sum(y * y, axis=0), ("cell", "snap")), all_cells)
        scales.append(scale)
        q = y / scale
        if section < ITERS:
            whole = lax.all_gather(q, "snap", axis=0, tiled=True)
            partial = jnp.dot(snapshots.T, whole, precision=high, preferred_element_type=F32)
            z = lax.psum(partial, "cell")
            scale = rms(lax.psum(jnp.sum(z * z, axis=0), "snap"), all_snaps)
            scales.append(scale)
            z = z / scale
    return q, z, jnp.stack(scales)


def local(snapshots, sketch):
    groups = lax.axis_size("cell")
    places = lax.axis_size("snap")
    rows, width = snapshots.shape
    rank = sketch.shape[1]
    fits = groups == 4 and places == 8 and rank == 4 * QUARTER and rows == 8 * LANES and width == 2 * LANES
    if not fits:
        return general(snapshots, sketch)
    all_cells = rows * groups
    all_snaps = width * places

    def swap(x, bits):
        return lax.ppermute(x, "snap", [(i, i ^ bits) for i in range(places)])

    swap_core = functools.partial(swap, bits=1)
    swap_side = functools.partial(swap, bits=2)

    def swap_pair(x):
        inner = [(i, i ^ 6) for i in range(2, 6)]
        outer = [(i, i ^ 6) for i in (0, 1, 6, 7)]
        return lax.ppermute(x, "snap", inner) + lax.ppermute(x, "snap", outer)


    def swap_cell(x, step):
        def target(cell, i):
            return cell ^ (1 if i % 2 == step else 2)

        perm = [(c * places + i, target(c, i) * places + i) for c in range(groups) for i in range(places)]
        return lax.ppermute(x, ("cell", "snap"), perm)

    def cell_pair(x):
        x = x + swap_cell(x, 0)
        return x, swap_cell(x, 1)

    def factor(count):
        return [((rows, count * width), BF16)] * 2

    def factor_t(count):
        return [((count * width, rows), BF16)] * 2

    def sketch_half(index):
        return lax.dynamic_slice_in_dim(sketch, index * LANES, LANES, 1)

    core = lax.rem(lax.axis_index("snap"), 2)
    side_block = swap_side(snapshots)
    packed = ((width, LANES), F32)
    mine, theirs = call(prepare_kernel, [packed, packed], sketch_half(core), swap_core(sketch_half(1 - core)))
    side_sketch = swap_side(theirs)
    quarter_shape = ((rows // LANES * QUARTER, LANES), F32)
    near_y, *near = call(
        near_kernel, [quarter_shape] + factor(2) + factor_t(2), snapshots, swap_core(snapshots), mine
    )
    side_block, near_y = lax.optimization_barrier((side_block, near_y))
    side = call(side_split_kernel, factor(1) + factor_t(1), side_block)
    (side_y,) = call(side_kernel, [quarter_shape], *side[:2], side_sketch, near_y, cost=LONG)
    half_shape = ((rows // LANES * COLS, LANES), F32)
    diagonal = swap_core(side_block)
    own_first, *far = call(far_kernel, [half_shape] + factor(1), diagonal, side_sketch, side_y)
    own_second, *far_t = call(
        second_far_kernel, [half_shape] + factor_t(1), diagonal, *far, side_sketch, side_y
    )
    own = (own_first, own_second)
    matrix = (near[0], side[0], far[0], near[1], side[1], far[1])
    matrix_t = (near[2], side[2], far_t[0], near[3], side[3], far_t[1])

    flat = (COLS * rows // LANES + TILE, LANES)
    sent_shape = ((COLS * 4 * width // LANES + TILE, LANES), F32)
    y_shape = (flat, F32)
    scale_shape = ((TILE, LANES), F32)
    z_shape = ((COLS * 4 * width // LANES, LANES), F32)
    scales = [[] for _ in range(HALVES)]
    sent = [call(first_z_kernel, [sent_shape], y, swap_pair(y), *matrix, cost=LONG)[0] for y in own]
    ys, zs = [None] * HALVES, [None] * HALVES
    for section in range(ITERS):
        last = section == ITERS - 1
        for h in range(HALVES):
            ys[h], scale, *z = call(
                functools.partial(y_kernel, all_cells), [y_shape, scale_shape] + [z_shape] * last,
                *cell_pair(sent[h]), *matrix_t,
            )
            scales[h].append(scale)
            if last:
                zs[h] = z[0]
                continue
            sent[h], scale = call(
                functools.partial(z_kernel, all_snaps), [sent_shape, scale_shape],
                ys[h], swap_pair(ys[h]), *matrix,
            )
            scales[h].append(scale)

    small = (2 * COLS + TILE, LANES)
    carried = HALVES * z_shape[0][0] // 2
    keeps, gots = [], []
    for h in range(HALVES):
        parts = zs if h == 0 else []
        keep, send = call(
            functools.partial(end_kernel, all_snaps, len(parts)),
            [(small, F32), ((small[0] + carried * (h == 0), LANES), F32)],
            ys[h], swap_pair(ys[h]), *parts, *scales[h],
            scratch=[pltpu.VMEM((flat[0] - TILE, LANES), F32)],
        )
        keeps.append(keep)
        gots.append(swap_side(send))
    keep, send = call(
        core_kernel, [((LANES + TILE, LANES), F32), ((LANES + TILE + carried, LANES), F32)],
        *keeps, *gots, *zs,
    )
    core_got = swap_core(send)
    y, known = call(join_kernel, [((LANES, rank), F32), ((TILE, rank), F32)], keep, core_got)
    others = [lax.ppermute(known, "cell", [(c, c ^ d) for c in range(groups)]) for d in (1, 2, 3)]
    (z_out,) = call(z_out_kernel, [((width, rank), F32)], *zs, gots[0], core_got, known, plain=True)
    q_out, scale_out = call(
        functools.partial(q_out_kernel, all_cells),
        [((LANES, rank), F32), ((2 * ITERS + 1, rank), F32)],
        y, known, *others, plain=True,
    )
    return q_out, z_out, scale_out


def solution(mesh):
    return jax.shard_map(
        local,
        mesh=mesh,
        in_specs=(P("cell", "snap"), P("snap", None)),
        out_specs=(P(("cell", "snap"), None), P("snap", None), P()),
        check_vma=False,
    )
```

```python
import functools

import jax
import jax.numpy as jnp
from jax import lax
from jax.experimental import pallas as pl
from jax.experimental.pallas import tpu as pltpu
from jax.sharding import PartitionSpec as P

ITERS = 2
EPS = 1e-05
LANES = 128
TILE = 8
HALVES = 2
QUARTER = 64
COLS = QUARTER // HALVES
BLOCKS = 3
BF16 = jnp.bfloat16
F32 = jnp.float32


def position():
    seat = lax.axis_index("snap")
    core, chip = lax.rem(seat, 2), lax.div(seat, 2)
    inner = jnp.logical_or(chip == 1, chip == 2)
    return core, inner.astype(jnp.int32), chip


def split(x):
    high = x.astype(BF16).astype(F32)
    return high, x - high


def dot(a, b):
    return lax.dot_general(a, b, (((1,), (0,)), ((), ())), preferred_element_type=F32)


def eye(cols):
    shape = (cols, LANES)
    return lax.broadcasted_iota(jnp.int32, shape, 0) == lax.broadcasted_iota(jnp.int32, shape, 1)


def to_column(row, cols):
    return jnp.sum(jnp.where(eye(cols), row, 0.0), axis=1, keepdims=True)


def to_row(column):
    return jnp.sum(jnp.where(eye(column.shape[0]), column, 0.0), axis=0, keepdims=True)


def squares_tile(x):
    row = to_row(jnp.sum(x * x, axis=1, keepdims=True))
    return jnp.broadcast_to(row, (TILE, LANES))


def rms(total, count):
    return jnp.sqrt(total / count + EPS)


def wide(x, cols):
    return jnp.concatenate([x[j * cols : (j + 1) * cols] for j in range(x.shape[0] // cols)], axis=1)


def store_blocks(ref, start, x):
    cols = x.shape[0]
    for j in range(x.shape[1] // LANES):
        ref[start + j * cols : start + (j + 1) * cols, :] = x[:, j * LANES : (j + 1) * LANES]


def turn(x, cols):
    return pltpu.roll(x, cols, 1)


def join_lanes(first, second, cols):
    left = lax.broadcasted_iota(jnp.int32, first.shape, 1) < cols
    return jnp.where(left, first, turn(second, cols))


def unfold(total):
    cols = total.shape[0] // 2
    return total[:cols] + total[cols:]


def sketch_sides(x):
    high, low = split(x)
    own = join_lanes(high, low, QUARTER)
    other = join_lanes(turn(high, QUARTER), turn(low, QUARTER), QUARTER)
    return own.astype(BF16), other.astype(BF16)


def store_factors(high_ref, low_ref, blocks, axis=1):
    start = 0
    for block in blocks:
        size = block.shape[axis]
        cut = [slice(None)] * 2
        cut[axis] = slice(start, start + size)
        high, low = split(block)
        high_ref[tuple(cut)] = high.astype(BF16)
        low_ref[tuple(cut)] = low.astype(BF16)
        start += size


def prepare_kernel(near_ref, got_ref, mine_ref, theirs_ref):
    near, got = near_ref[...], got_ref[...]
    low = join_lanes(near, got, QUARTER)
    high = join_lanes(turn(near, QUARTER), turn(got, QUARTER), QUARTER)
    zero = position()[1] == 0
    mine_ref[...] = jnp.where(zero, low, high)
    theirs_ref[...] = jnp.where(zero, high, low)


def near_kernel(own_ref, core_ref, sketch_ref, y_ref, high_ref, low_ref, high_t_ref, low_t_ref):
    blocks = (own_ref[...], core_ref[...])
    store_factors(high_ref, low_ref, blocks)
    store_factors(high_t_ref, low_t_ref, [block.T for block in blocks], 0)
    rhs = jnp.concatenate(sketch_sides(sketch_ref[...]), axis=0)
    for b in range(own_ref.shape[0] // LANES):
        cut = slice(b * LANES, (b + 1) * LANES)
        total = dot(high_ref[cut, :], rhs) + dot(low_ref[cut, :], rhs)
        y_ref[b * QUARTER : (b + 1) * QUARTER, :] = unfold(total.T)


def side_split_kernel(side_ref, high_ref, low_ref, high_t_ref, low_t_ref):
    store_factors(high_ref, low_ref, (side_ref[...],))
    store_factors(high_t_ref, low_t_ref, (side_ref[...].T,), 0)


def side_kernel(high_ref, low_ref, sketch_ref, near_ref, y_ref):
    rhs = sketch_sides(sketch_ref[...])[0]
    for b in range(high_ref.shape[0] // LANES):
        cut = slice(b * LANES, (b + 1) * LANES)
        total = dot(high_ref[cut, :], rhs) + dot(low_ref[cut, :], rhs)
        out = slice(b * QUARTER, (b + 1) * QUARTER)
        y_ref[out, :] = unfold(total.T) + near_ref[out, :]


def add_far(h, high_ref, low_ref, sketch_ref, near_ref, y_ref):
    rhs = sketch_sides(sketch_ref[...])[1]
    for b in range(high_ref.shape[0] // LANES):
        cut = slice(b * LANES, (b + 1) * LANES)
        total = dot(high_ref[cut, :], rhs) + dot(low_ref[cut, :], rhs)
        y = unfold(total.T)[h * COLS : (h + 1) * COLS]
        at = b * QUARTER + h * COLS
        y_ref[b * COLS : (b + 1) * COLS, :] = y + near_ref[at : at + COLS, :]


def far_kernel(diagonal_ref, sketch_ref, near_ref, y_ref, high_ref, low_ref):
    store_factors(high_ref, low_ref, (diagonal_ref[...],))
    add_far(0, high_ref, low_ref, sketch_ref, near_ref, y_ref)


def second_far_kernel(diagonal_ref, high_ref, low_ref, sketch_ref, near_ref, y_ref, high_t_ref, low_t_ref):
    add_far(1, high_ref, low_ref, sketch_ref, near_ref, y_ref)
    store_factors(high_t_ref, low_t_ref, (diagonal_ref[...].T,), 0)


def send_z(y, high_refs, low_refs, z_ref):
    lhs = jnp.concatenate(split(y), axis=0).astype(BF16)
    at = 0
    for high_ref, low_ref in zip(high_refs, low_refs):
        z = unfold(dot(lhs, high_ref[...]) + dot(lhs, low_ref[...]))
        store_blocks(z_ref, at, z)
        at += z.size // LANES
    z_ref[-TILE:, :] = squares_tile(y)


def factors(refs):
    return refs[:BLOCKS], refs[BLOCKS : 2 * BLOCKS]


def first_z_kernel(a_ref, b_ref, *refs):
    high, low = factors(refs)
    send_z(wide(a_ref[...] + b_ref[...], COLS), high, low, refs[-1])


def scaled(own_ref, got_ref, count):
    total = own_ref[...] + got_ref[...]
    scale = rms(total[-TILE:], count)
    return wide(total[:-TILE], COLS) / to_column(scale[:1], COLS), scale


def z_kernel(count, *refs):
    high, low = factors(refs[2:])
    z_ref, scale_ref = refs[-2:]
    y, scale = scaled(refs[0], refs[1], count)
    scale_ref[...] = scale
    send_z(y, high, low, z_ref)


def y_kernel(count, *refs):
    high_refs, low_refs = factors(refs[2:])
    y_ref, scale_ref, *z_refs = refs[2 + 2 * len(high_refs) :]
    z, scale = scaled(refs[0], refs[1], count)
    scale_ref[...] = scale
    for z_ref in z_refs:
        store_blocks(z_ref, 0, z)
    y_ref[-TILE:, :] = squares_tile(z)
    lhs = jnp.concatenate(split(z), axis=0).astype(BF16)
    total, at = None, 0
    for high_ref, low_ref in zip(high_refs, low_refs):
        part = lhs[:, at : at + high_ref.shape[0]]
        term = dot(part, high_ref[...]) + dot(part, low_ref[...])
        total = term if total is None else total + term
        at += high_ref.shape[0]
    store_blocks(y_ref, 0, unfold(total))


def end_kernel(count, carried, own_ref, got_ref, *refs):
    parts, scales, (keep_ref, send_ref, y_ref) = refs[:carried], refs[carried:-3], refs[-3:]
    y, scale = scaled(own_ref, got_ref, count)
    store_blocks(y_ref, 0, y)
    row = lax.broadcasted_iota(jnp.int32, (TILE, LANES), 0)
    tail = squares_tile(y)
    for i, known in enumerate([ref[...] for ref in scales] + [scale]):
        tail = jnp.where(row == i, known, tail)
    size = 2 * COLS
    chip = position()[2]
    for ref, owner in ((keep_ref, chip), (send_ref, chip ^ 1)):
        start = pl.multiple_of(owner * size, size)
        ref[:size, :] = y_ref[pl.ds(start, size), :]
        ref[size : size + TILE, :] = tail
    at = size + TILE
    for ref in parts:
        middle = ref.shape[0] // 2
        send_ref[at : at + middle, :] = ref[middle:, :]
        at += middle


def core_kernel(*refs):
    keeps, gots, parts = (refs[i * HALVES : (i + 1) * HALVES] for i in range(3))
    keep_ref, send_ref = refs[3 * HALVES :]
    core, side, _ = position()
    zero_side, zero_core = side == 0, core == 0
    tail = None
    for s in range(2):
        for h in range(HALVES):
            a, b = keeps[h][...], gots[h][: keeps[h].shape[0], :]
            x = jnp.where(zero_side, a, b) if s == 0 else jnp.where(zero_side, b, a)
            first, second, known = x[:COLS], x[COLS : 2 * COLS], x[2 * COLS :]
            at = (s * HALVES + h) * COLS
            keep_ref[at : at + COLS, :] = jnp.where(zero_core, first, second)
            send_ref[at : at + COLS, :] = jnp.where(zero_core, second, first)
            tail = known if tail is None else join_lanes(tail, known, at)
    keep_ref[LANES : LANES + TILE, :] = tail
    send_ref[LANES : LANES + TILE, :] = tail
    size = 2 * COLS
    for h, ref in enumerate(parts):
        at = LANES + TILE + h * size
        send_ref[at : at + size, :] = ref[size : 2 * size, :]
        at += HALVES * size
        start = keeps[0].shape[0] + (2 * h + 1) * size
        send_ref[at : at + size, :] = gots[0][start : start + size, :]


def join_kernel(keep_ref, got_ref, y_ref, known_ref):
    zero = position()[0] == 0
    keep, got = keep_ref[...], got_ref[: LANES + TILE, :]
    for s, x in enumerate((jnp.where(zero, keep, got), jnp.where(zero, got, keep))):
        cut = slice(s * LANES, (s + 1) * LANES)
        y_ref[:, cut] = x[:LANES].T
        known_ref[:, cut] = x[LANES:]


def z_out_kernel(*refs):
    parts, (side_ref, core_ref, known_ref, z_ref) = refs[:HALVES], refs[HALVES:]
    zero_core, zero_side = (flag == 0 for flag in position()[:2])
    size = 2 * COLS
    side_at, core_at = size + TILE, LANES + TILE
    mine = [ref[:size, :] for ref in parts]
    side = [side_ref[side_at + 2 * h * size : side_at + (2 * h + 1) * size, :] for h in range(HALVES)]
    core = [core_ref[core_at + h * size : core_at + (h + 1) * size, :] for h in range(2 * HALVES)]

    def side_order(own, other):
        low = [jnp.where(zero_side, a, b) for a, b in zip(own, other)]
        high = [jnp.where(zero_side, b, a) for a, b in zip(own, other)]
        return jnp.concatenate([wide(x, COLS) for x in low + high], axis=0)

    ours, theirs = side_order(mine, side), side_order(core[:HALVES], core[HALVES:])
    for s, x in enumerate((jnp.where(zero_core, ours, theirs), jnp.where(zero_core, theirs, ours))):
        cut = slice(s * LANES, (s + 1) * LANES)
        z_ref[:, cut] = x.T / known_ref[2 * ITERS - 1 : 2 * ITERS, cut]


def q_out_kernel(count, y_ref, known_ref, *refs):
    gots, (q_ref, scale_ref) = refs[:-2], refs[-2:]
    last = 2 * ITERS
    row = slice(last, last + 1)
    total = (known_ref[row, :] + gots[0][row, :]) + (gots[1][row, :] + gots[2][row, :])
    scale = rms(total, count)
    q_ref[...] = y_ref[...] / scale
    scale_ref[:last, :] = known_ref[:last, :]
    scale_ref[last:, :] = scale


def call(kernel, outs, *args, plain=False, scratch=(), cost=None):
    out_spec = pl.BlockSpec() if plain else pl.BlockSpec(memory_space=pltpu.VMEM)
    return pl.pallas_call(
        kernel,
        out_shape=[jax.ShapeDtypeStruct(shape, dtype) for shape, dtype in outs],
        in_specs=[pl.BlockSpec(memory_space=pltpu.VMEM)] * len(args),
        out_specs=[out_spec] * len(outs),
        scratch_shapes=scratch,
        cost_estimate=cost,
        compiler_params=pltpu.CompilerParams(vmem_limit_bytes=16 * 1024 * 1024),
    )(*args)


LONG = pl.CostEstimate(flops=10**11, bytes_accessed=2**28, transcendentals=0)


def general(snapshots, sketch):
    high = lax.Precision.HIGHEST
    all_cells = snapshots.shape[0] * lax.axis_size("cell")
    all_snaps = snapshots.shape[1] * lax.axis_size("snap")
    z, scales = sketch, []
    for section in range(ITERS + 1):
        partial = jnp.dot(snapshots, z, precision=high, preferred_element_type=F32)
        y = lax.psum_scatter(partial, "snap", scatter_dimension=0, tiled=True)
        scale = rms(lax.psum(jnp.sum(y * y, axis=0), ("cell", "snap")), all_cells)
        scales.append(scale)
        q = y / scale
        if section < ITERS:
            whole = lax.all_gather(q, "snap", axis=0, tiled=True)
            partial = jnp.dot(snapshots.T, whole, precision=high, preferred_element_type=F32)
            z = lax.psum(partial, "cell")
            scale = rms(lax.psum(jnp.sum(z * z, axis=0), "snap"), all_snaps)
            scales.append(scale)
            z = z / scale
    return q, z, jnp.stack(scales)


def local(snapshots, sketch):
    groups = lax.axis_size("cell")
    places = lax.axis_size("snap")
    rows, width = snapshots.shape
    rank = sketch.shape[1]
    fits = groups == 4 and places == 8 and rank == 4 * QUARTER and rows == 8 * LANES and width == 2 * LANES
    if not fits:
        return general(snapshots, sketch)
    all_cells = rows * groups
    all_snaps = width * places

    def swap(x, bits):
        return lax.ppermute(x, "snap", [(i, i ^ bits) for i in range(places)])

    swap_core = functools.partial(swap, bits=1)
    swap_side = functools.partial(swap, bits=2)
    swap_pair = functools.partial(swap, bits=6)

    def swap_cell(x, step):
        def target(cell, i):
            return cell ^ (1 if i % 2 == step else 2)

        perm = [(c * places + i, target(c, i) * places + i) for c in range(groups) for i in range(places)]
        return lax.ppermute(x, ("cell", "snap"), perm)

    def cell_pair(x, h):
        x = x + swap_cell(x, h)
        return x, swap_cell(x, 1 - h)

    def factor(count):
        return [((rows, count * width), BF16)] * 2

    def factor_t(count):
        return [((count * width, rows), BF16)] * 2

    def sketch_half(index):
        return lax.dynamic_slice_in_dim(sketch, index * LANES, LANES, 1)

    core = lax.rem(lax.axis_index("snap"), 2)
    side_block = swap_side(snapshots)
    packed = ((width, LANES), F32)
    mine, theirs = call(prepare_kernel, [packed, packed], sketch_half(core), swap_core(sketch_half(1 - core)))
    side_sketch = swap_side(theirs)
    quarter_shape = ((rows // LANES * QUARTER, LANES), F32)
    near_y, *near = call(
        near_kernel, [quarter_shape] + factor(2) + factor_t(2), snapshots, swap_core(snapshots), mine
    )
    side_block, near_y = lax.optimization_barrier((side_block, near_y))
    side = call(side_split_kernel, factor(1) + factor_t(1), side_block)
    (side_y,) = call(side_kernel, [quarter_shape], *side[:2], side_sketch, near_y, cost=LONG)
    half_shape = ((rows // LANES * COLS, LANES), F32)
    diagonal = swap_core(side_block)
    own_first, *far = call(far_kernel, [half_shape] + factor(1), diagonal, side_sketch, side_y)
    own_second, *far_t = call(
        second_far_kernel, [half_shape] + factor_t(1), diagonal, *far, side_sketch, side_y
    )
    own = (own_first, own_second)
    matrix = (near[0], side[0], far[0], near[1], side[1], far[1])
    matrix_t = (near[2], side[2], far_t[0], near[3], side[3], far_t[1])

    flat = (COLS * rows // LANES + TILE, LANES)
    sent_shape = ((COLS * 4 * width // LANES + TILE, LANES), F32)
    y_shape = (flat, F32)
    scale_shape = ((TILE, LANES), F32)
    z_shape = ((COLS * 4 * width // LANES, LANES), F32)
    scales = [[] for _ in range(HALVES)]
    sent = [call(first_z_kernel, [sent_shape], y, swap_pair(y), *matrix, cost=LONG)[0] for y in own]
    ys, zs = [None] * HALVES, [None] * HALVES
    for section in range(ITERS):
        last = section == ITERS - 1
        for h in range(HALVES):
            ys[h], scale, *z = call(
                functools.partial(y_kernel, all_cells), [y_shape, scale_shape] + [z_shape] * last,
                *cell_pair(sent[h], h), *matrix_t,
            )
            scales[h].append(scale)
            if last:
                zs[h] = z[0]
                continue
            sent[h], scale = call(
                functools.partial(z_kernel, all_snaps), [sent_shape, scale_shape],
                ys[h], swap_pair(ys[h]), *matrix,
            )
            scales[h].append(scale)

    small = (2 * COLS + TILE, LANES)
    carried = HALVES * z_shape[0][0] // 2
    keeps, gots = [], []
    for h in range(HALVES):
        parts = zs if h == 0 else []
        keep, send = call(
            functools.partial(end_kernel, all_snaps, len(parts)),
            [(small, F32), ((small[0] + carried * (h == 0), LANES), F32)],
            ys[h], swap_pair(ys[h]), *parts, *scales[h],
            scratch=[pltpu.VMEM((flat[0] - TILE, LANES), F32)],
        )
        keeps.append(keep)
        gots.append(swap_side(send))
    keep, send = call(
        core_kernel, [((LANES + TILE, LANES), F32), ((LANES + TILE + carried, LANES), F32)],
        *keeps, *gots, *zs,
    )
    core_got = swap_core(send)
    y, known = call(join_kernel, [((LANES, rank), F32), ((TILE, rank), F32)], keep, core_got)
    others = [lax.ppermute(known, "cell", [(c, c ^ d) for c in range(groups)]) for d in (1, 2, 3)]
    (z_out,) = call(z_out_kernel, [((width, rank), F32)], *zs, gots[0], core_got, known, plain=True)
    q_out, scale_out = call(
        functools.partial(q_out_kernel, all_cells),
        [((LANES, rank), F32), ((2 * ITERS + 1, rank), F32)],
        y, known, *others, plain=True,
    )
    return q_out, z_out, scale_out


def solution(mesh):
    return jax.shard_map(
        local,
        mesh=mesh,
        in_specs=(P("cell", "snap"), P("snap", None)),
        out_specs=(P(("cell", "snap"), None), P("snap", None), P()),
        check_vma=False,
    )
```

```python
import functools

import jax
import jax.numpy as jnp
from jax import lax
from jax.experimental import pallas as pl
from jax.experimental.pallas import tpu as pltpu
from jax.sharding import PartitionSpec as P

ITERS = 2
EPS = 1e-05
LANES = 128
TILE = 8
HALVES = 2
QUARTER = 64
COLS = QUARTER // HALVES
BLOCKS = 3
BF16 = jnp.bfloat16
F32 = jnp.float32


def sides():
    seat = lax.axis_index("snap")
    core, chip = lax.rem(seat, 2), lax.div(seat, 2)
    inner = jnp.logical_or(chip == 1, chip == 2).astype(jnp.int32)
    odd = lax.rem(chip, 2)
    return jnp.where(core == 0, inner, odd), jnp.where(core == 0, odd, inner)


def position():
    seat = lax.axis_index("snap")
    return lax.rem(seat, 2), sides()[0], lax.div(seat, 2)


def split(x):
    high = x.astype(BF16).astype(F32)
    return high, x - high


def dot(a, b):
    return lax.dot_general(a, b, (((1,), (0,)), ((), ())), preferred_element_type=F32)


def eye(cols):
    shape = (cols, LANES)
    return lax.broadcasted_iota(jnp.int32, shape, 0) == lax.broadcasted_iota(jnp.int32, shape, 1)


def to_column(row, cols):
    return jnp.sum(jnp.where(eye(cols), row, 0.0), axis=1, keepdims=True)


def to_row(column):
    return jnp.sum(jnp.where(eye(column.shape[0]), column, 0.0), axis=0, keepdims=True)


def squares_tile(x):
    row = to_row(jnp.sum(x * x, axis=1, keepdims=True))
    return jnp.broadcast_to(row, (TILE, LANES))


def rms(total, count):
    return jnp.sqrt(total / count + EPS)


def wide(x, cols):
    return jnp.concatenate([x[j * cols : (j + 1) * cols] for j in range(x.shape[0] // cols)], axis=1)


def store_blocks(ref, start, x):
    cols = x.shape[0]
    for j in range(x.shape[1] // LANES):
        ref[start + j * cols : start + (j + 1) * cols, :] = x[:, j * LANES : (j + 1) * LANES]


def turn(x, cols):
    return pltpu.roll(x, cols, 1)


def join_lanes(first, second, cols):
    left = lax.broadcasted_iota(jnp.int32, first.shape, 1) < cols
    return jnp.where(left, first, turn(second, cols))


def unfold(total):
    cols = total.shape[0] // 2
    return total[:cols] + total[cols:]


def sketch_sides(x):
    high, low = split(x)
    own = join_lanes(high, low, QUARTER)
    other = join_lanes(turn(high, QUARTER), turn(low, QUARTER), QUARTER)
    return own.astype(BF16), other.astype(BF16)


def store_factors(high_ref, low_ref, blocks, axis=1):
    start = 0
    for block in blocks:
        size = block.shape[axis]
        cut = [slice(None)] * 2
        cut[axis] = slice(start, start + size)
        high, low = split(block)
        high_ref[tuple(cut)] = high.astype(BF16)
        low_ref[tuple(cut)] = low.astype(BF16)
        start += size


def prepare_kernel(near_ref, got_ref, mine_ref, theirs_ref):
    near, got = near_ref[...], got_ref[...]
    low = join_lanes(near, got, QUARTER)
    high = join_lanes(turn(near, QUARTER), turn(got, QUARTER), QUARTER)
    zero = position()[1] == 0
    mine_ref[...] = jnp.where(zero, low, high)
    theirs_ref[...] = jnp.where(zero, high, low)


def near_kernel(own_ref, core_ref, sketch_ref, y_ref, high_ref, low_ref, high_t_ref, low_t_ref):
    blocks = (own_ref[...], core_ref[...])
    store_factors(high_ref, low_ref, blocks)
    store_factors(high_t_ref, low_t_ref, [block.T for block in blocks], 0)
    rhs = jnp.concatenate(sketch_sides(sketch_ref[...]), axis=0)
    for b in range(own_ref.shape[0] // LANES):
        cut = slice(b * LANES, (b + 1) * LANES)
        total = dot(high_ref[cut, :], rhs) + dot(low_ref[cut, :], rhs)
        y_ref[b * QUARTER : (b + 1) * QUARTER, :] = unfold(total.T)


def side_split_kernel(side_ref, high_ref, low_ref, high_t_ref, low_t_ref):
    store_factors(high_ref, low_ref, (side_ref[...],))
    store_factors(high_t_ref, low_t_ref, (side_ref[...].T,), 0)


def side_kernel(high_ref, low_ref, sketch_ref, near_ref, y_ref):
    rhs = sketch_sides(sketch_ref[...])[0]
    for b in range(high_ref.shape[0] // LANES):
        cut = slice(b * LANES, (b + 1) * LANES)
        total = dot(high_ref[cut, :], rhs) + dot(low_ref[cut, :], rhs)
        out = slice(b * QUARTER, (b + 1) * QUARTER)
        y_ref[out, :] = unfold(total.T) + near_ref[out, :]


def add_far(h, high_ref, low_ref, sketch_ref, near_ref, y_ref):
    rhs = sketch_sides(sketch_ref[...])[1]
    for b in range(high_ref.shape[0] // LANES):
        cut = slice(b * LANES, (b + 1) * LANES)
        total = dot(high_ref[cut, :], rhs) + dot(low_ref[cut, :], rhs)
        y = unfold(total.T)[h * COLS : (h + 1) * COLS]
        at = b * QUARTER + h * COLS
        y_ref[b * COLS : (b + 1) * COLS, :] = y + near_ref[at : at + COLS, :]


def far_kernel(diagonal_ref, sketch_ref, near_ref, y_ref, high_ref, low_ref):
    store_factors(high_ref, low_ref, (diagonal_ref[...],))
    add_far(0, high_ref, low_ref, sketch_ref, near_ref, y_ref)


def second_far_kernel(diagonal_ref, high_ref, low_ref, sketch_ref, near_ref, y_ref, high_t_ref, low_t_ref):
    add_far(1, high_ref, low_ref, sketch_ref, near_ref, y_ref)
    store_factors(high_t_ref, low_t_ref, (diagonal_ref[...].T,), 0)


def send_z(y, high_refs, low_refs, z_ref):
    lhs = jnp.concatenate(split(y), axis=0).astype(BF16)
    at = 0
    for high_ref, low_ref in zip(high_refs, low_refs):
        z = unfold(dot(lhs, high_ref[...]) + dot(lhs, low_ref[...]))
        store_blocks(z_ref, at, z)
        at += z.size // LANES
    z_ref[-TILE:, :] = squares_tile(y)


def factors(refs):
    return refs[:BLOCKS], refs[BLOCKS : 2 * BLOCKS]


def first_z_kernel(a_ref, b_ref, *refs):
    high, low = factors(refs)
    send_z(wide(a_ref[...] + b_ref[...], COLS), high, low, refs[-1])


def scaled(own_ref, got_ref, count):
    total = own_ref[...] + got_ref[...]
    scale = rms(total[-TILE:], count)
    return wide(total[:-TILE], COLS) / to_column(scale[:1], COLS), scale


def z_kernel(count, *refs):
    high, low = factors(refs[2:])
    z_ref, scale_ref = refs[-2:]
    y, scale = scaled(refs[0], refs[1], count)
    scale_ref[...] = scale
    send_z(y, high, low, z_ref)


def y_kernel(count, *refs):
    high_refs, low_refs = factors(refs[2:])
    y_ref, scale_ref, *z_refs = refs[2 + 2 * len(high_refs) :]
    z, scale = scaled(refs[0], refs[1], count)
    scale_ref[...] = scale
    for z_ref in z_refs:
        store_blocks(z_ref, 0, z)
    y_ref[-TILE:, :] = squares_tile(z)
    lhs = jnp.concatenate(split(z), axis=0).astype(BF16)
    total, at = None, 0
    for high_ref, low_ref in zip(high_refs, low_refs):
        part = lhs[:, at : at + high_ref.shape[0]]
        term = dot(part, high_ref[...]) + dot(part, low_ref[...])
        total = term if total is None else total + term
        at += high_ref.shape[0]
    store_blocks(y_ref, 0, unfold(total))


def end_kernel(count, carried, own_ref, got_ref, *refs):
    parts, scales, (keep_ref, send_ref, y_ref) = refs[:carried], refs[carried:-3], refs[-3:]
    y, scale = scaled(own_ref, got_ref, count)
    store_blocks(y_ref, 0, y)
    row = lax.broadcasted_iota(jnp.int32, (TILE, LANES), 0)
    tail = squares_tile(y)
    for i, known in enumerate([ref[...] for ref in scales] + [scale]):
        tail = jnp.where(row == i, known, tail)
    size = 2 * COLS
    chip = position()[2]
    for ref, owner in ((keep_ref, chip), (send_ref, chip ^ 1)):
        start = pl.multiple_of(owner * size, size)
        ref[:size, :] = y_ref[pl.ds(start, size), :]
        ref[size : size + TILE, :] = tail
    at = size + TILE
    for ref in parts:
        middle = ref.shape[0] // 2
        send_ref[at : at + middle, :] = ref[middle:, :]
        at += middle


def core_kernel(*refs):
    keeps, gots, parts = (refs[i * HALVES : (i + 1) * HALVES] for i in range(3))
    keep_ref, send_ref = refs[3 * HALVES :]
    core, side, _ = position()
    zero_side, zero_core = side == 0, core == 0
    tail = None
    for s in range(2):
        for h in range(HALVES):
            a, b = keeps[h][...], gots[h][: keeps[h].shape[0], :]
            x = jnp.where(zero_side, a, b) if s == 0 else jnp.where(zero_side, b, a)
            first, second, known = x[:COLS], x[COLS : 2 * COLS], x[2 * COLS :]
            at = (s * HALVES + h) * COLS
            keep_ref[at : at + COLS, :] = jnp.where(zero_core, first, second)
            send_ref[at : at + COLS, :] = jnp.where(zero_core, second, first)
            tail = known if tail is None else join_lanes(tail, known, at)
    keep_ref[LANES : LANES + TILE, :] = tail
    send_ref[LANES : LANES + TILE, :] = tail
    size = 2 * COLS
    for h, ref in enumerate(parts):
        at = LANES + TILE + h * size
        send_ref[at : at + size, :] = ref[size : 2 * size, :]
        at += HALVES * size
        start = keeps[0].shape[0] + (2 * h + 1) * size
        send_ref[at : at + size, :] = gots[0][start : start + size, :]


def join_kernel(keep_ref, got_ref, y_ref, known_ref):
    zero = position()[0] == 0
    keep, got = keep_ref[...], got_ref[: LANES + TILE, :]
    for s, x in enumerate((jnp.where(zero, keep, got), jnp.where(zero, got, keep))):
        cut = slice(s * LANES, (s + 1) * LANES)
        y_ref[:, cut] = x[:LANES].T
        known_ref[:, cut] = x[LANES:]


def z_out_kernel(*refs):
    parts, (side_ref, core_ref, known_ref, z_ref) = refs[:HALVES], refs[HALVES:]
    zero_core, zero_side = (flag == 0 for flag in position()[:2])
    size = 2 * COLS
    side_at, core_at = size + TILE, LANES + TILE
    mine = [ref[:size, :] for ref in parts]
    side = [side_ref[side_at + 2 * h * size : side_at + (2 * h + 1) * size, :] for h in range(HALVES)]
    core = [core_ref[core_at + h * size : core_at + (h + 1) * size, :] for h in range(2 * HALVES)]

    def side_order(own, other, zero):
        low = [jnp.where(zero, a, b) for a, b in zip(own, other)]
        high = [jnp.where(zero, b, a) for a, b in zip(own, other)]
        return jnp.concatenate([wide(x, COLS) for x in low + high], axis=0)

    ours = side_order(mine, side, zero_side)
    theirs = side_order(core[:HALVES], core[HALVES:], sides()[1] == 0)
    for s, x in enumerate((jnp.where(zero_core, ours, theirs), jnp.where(zero_core, theirs, ours))):
        cut = slice(s * LANES, (s + 1) * LANES)
        z_ref[:, cut] = x.T / known_ref[2 * ITERS - 1 : 2 * ITERS, cut]


def q_out_kernel(count, y_ref, known_ref, *refs):
    gots, (q_ref, scale_ref) = refs[:-2], refs[-2:]
    last = 2 * ITERS
    row = slice(last, last + 1)
    total = (known_ref[row, :] + gots[0][row, :]) + (gots[1][row, :] + gots[2][row, :])
    scale = rms(total, count)
    q_ref[...] = y_ref[...] / scale
    scale_ref[:last, :] = known_ref[:last, :]
    scale_ref[last:, :] = scale


def call(kernel, outs, *args, plain=False, scratch=(), cost=None):
    out_spec = pl.BlockSpec() if plain else pl.BlockSpec(memory_space=pltpu.VMEM)
    return pl.pallas_call(
        kernel,
        out_shape=[jax.ShapeDtypeStruct(shape, dtype) for shape, dtype in outs],
        in_specs=[pl.BlockSpec(memory_space=pltpu.VMEM)] * len(args),
        out_specs=[out_spec] * len(outs),
        scratch_shapes=scratch,
        cost_estimate=cost,
        compiler_params=pltpu.CompilerParams(vmem_limit_bytes=16 * 1024 * 1024),
    )(*args)


LONG = pl.CostEstimate(flops=10**11, bytes_accessed=2**28, transcendentals=0)


def general(snapshots, sketch):
    high = lax.Precision.HIGHEST
    all_cells = snapshots.shape[0] * lax.axis_size("cell")
    all_snaps = snapshots.shape[1] * lax.axis_size("snap")
    z, scales = sketch, []
    for section in range(ITERS + 1):
        partial = jnp.dot(snapshots, z, precision=high, preferred_element_type=F32)
        y = lax.psum_scatter(partial, "snap", scatter_dimension=0, tiled=True)
        scale = rms(lax.psum(jnp.sum(y * y, axis=0), ("cell", "snap")), all_cells)
        scales.append(scale)
        q = y / scale
        if section < ITERS:
            whole = lax.all_gather(q, "snap", axis=0, tiled=True)
            partial = jnp.dot(snapshots.T, whole, precision=high, preferred_element_type=F32)
            z = lax.psum(partial, "cell")
            scale = rms(lax.psum(jnp.sum(z * z, axis=0), "snap"), all_snaps)
            scales.append(scale)
            z = z / scale
    return q, z, jnp.stack(scales)


def local(snapshots, sketch):
    groups = lax.axis_size("cell")
    places = lax.axis_size("snap")
    rows, width = snapshots.shape
    rank = sketch.shape[1]
    fits = groups == 4 and places == 8 and rank == 4 * QUARTER and rows == 8 * LANES and width == 2 * LANES
    if not fits:
        return general(snapshots, sketch)
    all_cells = rows * groups
    all_snaps = width * places

    def swap(x, bits):
        return lax.ppermute(x, "snap", [(i, i ^ bits) for i in range(places)])

    swap_core = functools.partial(swap, bits=1)
    swap_side = functools.partial(swap, bits=2)

    def swap_pair(x):
        return lax.ppermute(x, "snap", [(i, i ^ (4 if i % 2 else 6)) for i in range(places)])


    def swap_cell(x, step):
        def target(cell, i):
            return cell ^ (1 if i % 2 == step else 2)

        perm = [(c * places + i, target(c, i) * places + i) for c in range(groups) for i in range(places)]
        return lax.ppermute(x, ("cell", "snap"), perm)

    def cell_pair(x):
        x = x + swap_cell(x, 0)
        return x, swap_cell(x, 1)

    def factor(count):
        return [((rows, count * width), BF16)] * 2

    def factor_t(count):
        return [((count * width, rows), BF16)] * 2

    def sketch_half(index):
        return lax.dynamic_slice_in_dim(sketch, index * LANES, LANES, 1)

    core = lax.rem(lax.axis_index("snap"), 2)
    side_block = swap_side(snapshots)
    packed = ((width, LANES), F32)
    mine, theirs = call(prepare_kernel, [packed, packed], sketch_half(core), swap_core(sketch_half(1 - core)))
    side_sketch = swap_side(theirs)
    quarter_shape = ((rows // LANES * QUARTER, LANES), F32)
    near_y, *near = call(
        near_kernel, [quarter_shape] + factor(2) + factor_t(2), snapshots, swap_core(snapshots), mine
    )
    side_block, near_y = lax.optimization_barrier((side_block, near_y))
    side = call(side_split_kernel, factor(1) + factor_t(1), side_block)
    (side_y,) = call(side_kernel, [quarter_shape], *side[:2], side_sketch, near_y, cost=LONG)
    half_shape = ((rows // LANES * COLS, LANES), F32)
    diagonal = swap_core(side_block)
    own_first, *far = call(far_kernel, [half_shape] + factor(1), diagonal, side_sketch, side_y)
    own_second, *far_t = call(
        second_far_kernel, [half_shape] + factor_t(1), diagonal, *far, side_sketch, side_y
    )
    own = (own_first, own_second)
    matrix = (near[0], side[0], far[0], near[1], side[1], far[1])
    matrix_t = (near[2], side[2], far_t[0], near[3], side[3], far_t[1])

    flat = (COLS * rows // LANES + TILE, LANES)
    sent_shape = ((COLS * 4 * width // LANES + TILE, LANES), F32)
    y_shape = (flat, F32)
    scale_shape = ((TILE, LANES), F32)
    z_shape = ((COLS * 4 * width // LANES, LANES), F32)
    scales = [[] for _ in range(HALVES)]
    sent = [call(first_z_kernel, [sent_shape], y, swap_pair(y), *matrix, cost=LONG)[0] for y in own]
    ys, zs = [None] * HALVES, [None] * HALVES
    for section in range(ITERS):
        last = section == ITERS - 1
        for h in range(HALVES):
            ys[h], scale, *z = call(
                functools.partial(y_kernel, all_cells), [y_shape, scale_shape] + [z_shape] * last,
                *cell_pair(sent[h]), *matrix_t,
            )
            scales[h].append(scale)
            if last:
                zs[h] = z[0]
                continue
            sent[h], scale = call(
                functools.partial(z_kernel, all_snaps), [sent_shape, scale_shape],
                ys[h], swap_pair(ys[h]), *matrix,
            )
            scales[h].append(scale)

    small = (2 * COLS + TILE, LANES)
    carried = HALVES * z_shape[0][0] // 2
    keeps, gots = [], []
    for h in range(HALVES):
        parts = zs if h == 0 else []
        keep, send = call(
            functools.partial(end_kernel, all_snaps, len(parts)),
            [(small, F32), ((small[0] + carried * (h == 0), LANES), F32)],
            ys[h], swap_pair(ys[h]), *parts, *scales[h],
            scratch=[pltpu.VMEM((flat[0] - TILE, LANES), F32)],
        )
        keeps.append(keep)
        gots.append(swap_side(send))
    keep, send = call(
        core_kernel, [((LANES + TILE, LANES), F32), ((LANES + TILE + carried, LANES), F32)],
        *keeps, *gots, *zs,
    )
    core_got = swap_core(send)
    y, known = call(join_kernel, [((LANES, rank), F32), ((TILE, rank), F32)], keep, core_got)
    others = [lax.ppermute(known, "cell", [(c, c ^ d) for c in range(groups)]) for d in (1, 2, 3)]
    (z_out,) = call(z_out_kernel, [((width, rank), F32)], *zs, gots[0], core_got, known, plain=True)
    q_out, scale_out = call(
        functools.partial(q_out_kernel, all_cells),
        [((LANES, rank), F32), ((2 * ITERS + 1, rank), F32)],
        y, known, *others, plain=True,
    )
    return q_out, z_out, scale_out


def solution(mesh):
    return jax.shard_map(
        local,
        mesh=mesh,
        in_specs=(P("cell", "snap"), P("snap", None)),
        out_specs=(P(("cell", "snap"), None), P("snap", None), P()),
        check_vma=False,
    )
```

```python
import functools

import jax
import jax.numpy as jnp
from jax import lax
from jax.experimental import pallas as pl
from jax.experimental.pallas import tpu as pltpu
from jax.sharding import PartitionSpec as P

ITERS = 2
EPS = 1e-05
LANES = 128
TILE = 8
HALVES = 2
QUARTER = 64
COLS = QUARTER // HALVES
BLOCKS = 3
BF16 = jnp.bfloat16
F32 = jnp.float32


def position():
    seat = lax.axis_index("snap")
    core, chip = lax.rem(seat, 2), lax.div(seat, 2)
    inner = jnp.logical_or(chip == 1, chip == 2)
    return core, inner.astype(jnp.int32), chip


def split(x):
    high = x.astype(BF16).astype(F32)
    return high, x - high


def dot(a, b):
    return lax.dot_general(a, b, (((1,), (0,)), ((), ())), preferred_element_type=F32)


def eye(cols):
    shape = (cols, LANES)
    return lax.broadcasted_iota(jnp.int32, shape, 0) == lax.broadcasted_iota(jnp.int32, shape, 1)


def to_column(row, cols):
    return jnp.sum(jnp.where(eye(cols), row, 0.0), axis=1, keepdims=True)


def to_row(column):
    return jnp.sum(jnp.where(eye(column.shape[0]), column, 0.0), axis=0, keepdims=True)


def squares_tile(x):
    row = to_row(jnp.sum(x * x, axis=1, keepdims=True))
    return jnp.broadcast_to(row, (TILE, LANES))


def rms(total, count):
    return jnp.sqrt(total / count + EPS)


def wide(x, cols):
    return jnp.concatenate([x[j * cols : (j + 1) * cols] for j in range(x.shape[0] // cols)], axis=1)


def store_blocks(ref, start, x):
    cols = x.shape[0]
    for j in range(x.shape[1] // LANES):
        ref[start + j * cols : start + (j + 1) * cols, :] = x[:, j * LANES : (j + 1) * LANES]


def turn(x, cols):
    return pltpu.roll(x, cols, 1)


def join_lanes(first, second, cols):
    left = lax.broadcasted_iota(jnp.int32, first.shape, 1) < cols
    return jnp.where(left, first, turn(second, cols))


def unfold(total):
    cols = total.shape[0] // 2
    return total[:cols] + total[cols:]


def sketch_sides(x):
    high, low = split(x)
    own = join_lanes(high, low, QUARTER)
    other = join_lanes(turn(high, QUARTER), turn(low, QUARTER), QUARTER)
    return own.astype(BF16), other.astype(BF16)


def store_factors(high_ref, low_ref, blocks, axis=1):
    start = 0
    for block in blocks:
        size = block.shape[axis]
        cut = [slice(None)] * 2
        cut[axis] = slice(start, start + size)
        high, low = split(block)
        high_ref[tuple(cut)] = high.astype(BF16)
        low_ref[tuple(cut)] = low.astype(BF16)
        start += size


def prepare_kernel(near_ref, got_ref, mine_ref, theirs_ref):
    near, got = near_ref[...], got_ref[...]
    low = join_lanes(near, got, QUARTER)
    high = join_lanes(turn(near, QUARTER), turn(got, QUARTER), QUARTER)
    zero = position()[1] == 0
    mine_ref[...] = jnp.where(zero, low, high)
    theirs_ref[...] = jnp.where(zero, high, low)


def near_kernel(own_ref, core_ref, sketch_ref, y_ref, high_ref, low_ref, high_t_ref, low_t_ref):
    blocks = (own_ref[...], core_ref[...])
    store_factors(high_ref, low_ref, blocks)
    store_factors(high_t_ref, low_t_ref, [block.T for block in blocks], 0)
    rhs = jnp.concatenate(sketch_sides(sketch_ref[...]), axis=0)
    for b in range(own_ref.shape[0] // LANES):
        cut = slice(b * LANES, (b + 1) * LANES)
        total = dot(high_ref[cut, :], rhs) + dot(low_ref[cut, :], rhs)
        y_ref[b * QUARTER : (b + 1) * QUARTER, :] = unfold(total.T)


def side_split_kernel(side_ref, high_ref, low_ref, high_t_ref, low_t_ref):
    store_factors(high_ref, low_ref, (side_ref[...],))
    store_factors(high_t_ref, low_t_ref, (side_ref[...].T,), 0)


def side_kernel(high_ref, low_ref, sketch_ref, near_ref, y_ref):
    rhs = sketch_sides(sketch_ref[...])[0]
    for b in range(high_ref.shape[0] // LANES):
        cut = slice(b * LANES, (b + 1) * LANES)
        total = dot(high_ref[cut, :], rhs) + dot(low_ref[cut, :], rhs)
        out = slice(b * QUARTER, (b + 1) * QUARTER)
        y_ref[out, :] = unfold(total.T) + near_ref[out, :]


def add_far(high_ref, low_ref, sketch_ref, near_ref, halves):
    rhs = sketch_sides(sketch_ref[...])[1]
    for b in range(high_ref.shape[0] // LANES):
        cut = slice(b * LANES, (b + 1) * LANES)
        total = dot(high_ref[cut, :], rhs) + dot(low_ref[cut, :], rhs)
        y = unfold(total.T) + near_ref[b * QUARTER : (b + 1) * QUARTER, :]
        for h, ref in enumerate(halves):
            ref[b * COLS : (b + 1) * COLS, :] = y[h * COLS : (h + 1) * COLS]


def far_kernel(diagonal_ref, sketch_ref, near_ref, *refs):
    *halves, high_ref, low_ref = refs
    store_factors(high_ref, low_ref, (diagonal_ref[...],))
    add_far(high_ref, low_ref, sketch_ref, near_ref, halves)


def turned_kernel(diagonal_ref, high_ref, low_ref):
    store_factors(high_ref, low_ref, (diagonal_ref[...].T,), 0)


def send_z(y, high_refs, low_refs, z_ref):
    lhs = jnp.concatenate(split(y), axis=0).astype(BF16)
    at = 0
    for high_ref, low_ref in zip(high_refs, low_refs):
        z = unfold(dot(lhs, high_ref[...]) + dot(lhs, low_ref[...]))
        store_blocks(z_ref, at, z)
        at += z.size // LANES
    z_ref[-TILE:, :] = squares_tile(y)


def factors(refs):
    return refs[:BLOCKS], refs[BLOCKS : 2 * BLOCKS]


def first_z_kernel(a_ref, b_ref, *refs):
    high, low = factors(refs)
    send_z(wide(a_ref[...] + b_ref[...], COLS), high, low, refs[-1])


def scaled(own_ref, got_ref, count):
    total = own_ref[...] + got_ref[...]
    scale = rms(total[-TILE:], count)
    return wide(total[:-TILE], COLS) / to_column(scale[:1], COLS), scale


def z_kernel(count, *refs):
    high, low = factors(refs[2:])
    z_ref, scale_ref = refs[-2:]
    y, scale = scaled(refs[0], refs[1], count)
    scale_ref[...] = scale
    send_z(y, high, low, z_ref)


def y_kernel(count, *refs):
    high_refs, low_refs = factors(refs[2:])
    y_ref, scale_ref, *z_refs = refs[2 + 2 * len(high_refs) :]
    z, scale = scaled(refs[0], refs[1], count)
    scale_ref[...] = scale
    for z_ref in z_refs:
        store_blocks(z_ref, 0, z)
    y_ref[-TILE:, :] = squares_tile(z)
    lhs = jnp.concatenate(split(z), axis=0).astype(BF16)
    total, at = None, 0
    for high_ref, low_ref in zip(high_refs, low_refs):
        part = lhs[:, at : at + high_ref.shape[0]]
        term = dot(part, high_ref[...]) + dot(part, low_ref[...])
        total = term if total is None else total + term
        at += high_ref.shape[0]
    store_blocks(y_ref, 0, unfold(total))


def end_kernel(count, carried, own_ref, got_ref, *refs):
    parts, scales, (keep_ref, send_ref, y_ref) = refs[:carried], refs[carried:-3], refs[-3:]
    y, scale = scaled(own_ref, got_ref, count)
    store_blocks(y_ref, 0, y)
    row = lax.broadcasted_iota(jnp.int32, (TILE, LANES), 0)
    tail = squares_tile(y)
    for i, known in enumerate([ref[...] for ref in scales] + [scale]):
        tail = jnp.where(row == i, known, tail)
    size = 2 * COLS
    chip = position()[2]
    for ref, owner in ((keep_ref, chip), (send_ref, chip ^ 1)):
        start = pl.multiple_of(owner * size, size)
        ref[:size, :] = y_ref[pl.ds(start, size), :]
        ref[size : size + TILE, :] = tail
    at = size + TILE
    for ref in parts:
        middle = ref.shape[0] // 2
        send_ref[at : at + middle, :] = ref[middle:, :]
        at += middle


def core_kernel(*refs):
    keeps, gots, parts = (refs[i * HALVES : (i + 1) * HALVES] for i in range(3))
    keep_ref, send_ref = refs[3 * HALVES :]
    core, side, _ = position()
    zero_side, zero_core = side == 0, core == 0
    tail = None
    for s in range(2):
        for h in range(HALVES):
            a, b = keeps[h][...], gots[h][: keeps[h].shape[0], :]
            x = jnp.where(zero_side, a, b) if s == 0 else jnp.where(zero_side, b, a)
            first, second, known = x[:COLS], x[COLS : 2 * COLS], x[2 * COLS :]
            at = (s * HALVES + h) * COLS
            keep_ref[at : at + COLS, :] = jnp.where(zero_core, first, second)
            send_ref[at : at + COLS, :] = jnp.where(zero_core, second, first)
            tail = known if tail is None else join_lanes(tail, known, at)
    keep_ref[LANES : LANES + TILE, :] = tail
    send_ref[LANES : LANES + TILE, :] = tail
    size = 2 * COLS
    for h, ref in enumerate(parts):
        at = LANES + TILE + h * size
        send_ref[at : at + size, :] = ref[size : 2 * size, :]
        at += HALVES * size
        start = keeps[0].shape[0] + (2 * h + 1) * size
        send_ref[at : at + size, :] = gots[0][start : start + size, :]


def join_kernel(keep_ref, got_ref, y_ref, known_ref):
    zero = position()[0] == 0
    keep, got = keep_ref[...], got_ref[: LANES + TILE, :]
    for s, x in enumerate((jnp.where(zero, keep, got), jnp.where(zero, got, keep))):
        cut = slice(s * LANES, (s + 1) * LANES)
        y_ref[:, cut] = x[:LANES].T
        known_ref[:, cut] = x[LANES:]


def z_out_kernel(*refs):
    parts, (side_ref, core_ref, known_ref, z_ref) = refs[:HALVES], refs[HALVES:]
    zero_core, zero_side = (flag == 0 for flag in position()[:2])
    size = 2 * COLS
    side_at, core_at = size + TILE, LANES + TILE
    mine = [ref[:size, :] for ref in parts]
    side = [side_ref[side_at + 2 * h * size : side_at + (2 * h + 1) * size, :] for h in range(HALVES)]
    core = [core_ref[core_at + h * size : core_at + (h + 1) * size, :] for h in range(2 * HALVES)]

    def side_order(own, other):
        low = [jnp.where(zero_side, a, b) for a, b in zip(own, other)]
        high = [jnp.where(zero_side, b, a) for a, b in zip(own, other)]
        return jnp.concatenate([wide(x, COLS) for x in low + high], axis=0)

    ours, theirs = side_order(mine, side), side_order(core[:HALVES], core[HALVES:])
    for s, x in enumerate((jnp.where(zero_core, ours, theirs), jnp.where(zero_core, theirs, ours))):
        cut = slice(s * LANES, (s + 1) * LANES)
        z_ref[:, cut] = x.T / known_ref[2 * ITERS - 1 : 2 * ITERS, cut]


def q_out_kernel(count, y_ref, known_ref, *refs):
    gots, (q_ref, scale_ref) = refs[:-2], refs[-2:]
    last = 2 * ITERS
    row = slice(last, last + 1)
    total = (known_ref[row, :] + gots[0][row, :]) + (gots[1][row, :] + gots[2][row, :])
    scale = rms(total, count)
    q_ref[...] = y_ref[...] / scale
    scale_ref[:last, :] = known_ref[:last, :]
    scale_ref[last:, :] = scale


def call(kernel, outs, *args, plain=False, scratch=(), cost=None):
    out_spec = pl.BlockSpec() if plain else pl.BlockSpec(memory_space=pltpu.VMEM)
    return pl.pallas_call(
        kernel,
        out_shape=[jax.ShapeDtypeStruct(shape, dtype) for shape, dtype in outs],
        in_specs=[pl.BlockSpec(memory_space=pltpu.VMEM)] * len(args),
        out_specs=[out_spec] * len(outs),
        scratch_shapes=scratch,
        cost_estimate=cost,
        compiler_params=pltpu.CompilerParams(vmem_limit_bytes=16 * 1024 * 1024),
    )(*args)


LONG = pl.CostEstimate(flops=10**11, bytes_accessed=2**28, transcendentals=0)


def general(snapshots, sketch):
    high = lax.Precision.HIGHEST
    all_cells = snapshots.shape[0] * lax.axis_size("cell")
    all_snaps = snapshots.shape[1] * lax.axis_size("snap")
    z, scales = sketch, []
    for section in range(ITERS + 1):
        partial = jnp.dot(snapshots, z, precision=high, preferred_element_type=F32)
        y = lax.psum_scatter(partial, "snap", scatter_dimension=0, tiled=True)
        scale = rms(lax.psum(jnp.sum(y * y, axis=0), ("cell", "snap")), all_cells)
        scales.append(scale)
        q = y / scale
        if section < ITERS:
            whole = lax.all_gather(q, "snap", axis=0, tiled=True)
            partial = jnp.dot(snapshots.T, whole, precision=high, preferred_element_type=F32)
            z = lax.psum(partial, "cell")
            scale = rms(lax.psum(jnp.sum(z * z, axis=0), "snap"), all_snaps)
            scales.append(scale)
            z = z / scale
    return q, z, jnp.stack(scales)


def local(snapshots, sketch):
    groups = lax.axis_size("cell")
    places = lax.axis_size("snap")
    rows, width = snapshots.shape
    rank = sketch.shape[1]
    fits = groups == 4 and places == 8 and rank == 4 * QUARTER and rows == 8 * LANES and width == 2 * LANES
    if not fits:
        return general(snapshots, sketch)
    all_cells = rows * groups
    all_snaps = width * places

    def swap(x, bits):
        return lax.ppermute(x, "snap", [(i, i ^ bits) for i in range(places)])

    swap_core = functools.partial(swap, bits=1)
    swap_side = functools.partial(swap, bits=2)
    swap_pair = functools.partial(swap, bits=6)

    def swap_cell(x, step):
        def target(cell, i):
            return cell ^ (1 if i % 2 == step else 2)

        perm = [(c * places + i, target(c, i) * places + i) for c in range(groups) for i in range(places)]
        return lax.ppermute(x, ("cell", "snap"), perm)

    def cell_pair(x):
        x = x + swap_cell(x, 0)
        return x, swap_cell(x, 1)

    def factor(count):
        return [((rows, count * width), BF16)] * 2

    def factor_t(count):
        return [((count * width, rows), BF16)] * 2

    def sketch_half(index):
        return lax.dynamic_slice_in_dim(sketch, index * LANES, LANES, 1)

    core = lax.rem(lax.axis_index("snap"), 2)
    side_block = swap_side(snapshots)
    packed = ((width, LANES), F32)
    mine, theirs = call(prepare_kernel, [packed, packed], sketch_half(core), swap_core(sketch_half(1 - core)))
    side_sketch = swap_side(theirs)
    quarter_shape = ((rows // LANES * QUARTER, LANES), F32)
    near_y, *near = call(
        near_kernel, [quarter_shape] + factor(2) + factor_t(2), snapshots, swap_core(snapshots), mine
    )
    side_block, near_y = lax.optimization_barrier((side_block, near_y))
    side = call(side_split_kernel, factor(1) + factor_t(1), side_block)
    (side_y,) = call(side_kernel, [quarter_shape], *side[:2], side_sketch, near_y, cost=LONG)
    half_shape = ((rows // LANES * COLS, LANES), F32)
    diagonal = swap_core(side_block)
    *own, high, low = call(far_kernel, [half_shape] * HALVES + factor(1), diagonal, side_sketch, side_y)
    far, far_t = (high, low), call(turned_kernel, factor_t(1), diagonal)
    matrix = (near[0], side[0], far[0], near[1], side[1], far[1])
    matrix_t = (near[2], side[2], far_t[0], near[3], side[3], far_t[1])

    flat = (COLS * rows // LANES + TILE, LANES)
    sent_shape = ((COLS * 4 * width // LANES + TILE, LANES), F32)
    y_shape = (flat, F32)
    scale_shape = ((TILE, LANES), F32)
    z_shape = ((COLS * 4 * width // LANES, LANES), F32)
    scales = [[] for _ in range(HALVES)]
    sent = [call(first_z_kernel, [sent_shape], y, swap_pair(y), *matrix, cost=LONG)[0] for y in own]
    ys, zs = [None] * HALVES, [None] * HALVES
    for section in range(ITERS):
        last = section == ITERS - 1
        for h in range(HALVES):
            ys[h], scale, *z = call(
                functools.partial(y_kernel, all_cells), [y_shape, scale_shape] + [z_shape] * last,
                *cell_pair(sent[h]), *matrix_t,
            )
            scales[h].append(scale)
            if last:
                zs[h] = z[0]
                continue
            sent[h], scale = call(
                functools.partial(z_kernel, all_snaps), [sent_shape, scale_shape],
                ys[h], swap_pair(ys[h]), *matrix,
            )
            scales[h].append(scale)

    small = (2 * COLS + TILE, LANES)
    carried = HALVES * z_shape[0][0] // 2
    keeps, gots = [], []
    for h in range(HALVES):
        parts = zs if h == 0 else []
        keep, send = call(
            functools.partial(end_kernel, all_snaps, len(parts)),
            [(small, F32), ((small[0] + carried * (h == 0), LANES), F32)],
            ys[h], swap_pair(ys[h]), *parts, *scales[h],
            scratch=[pltpu.VMEM((flat[0] - TILE, LANES), F32)],
        )
        keeps.append(keep)
        gots.append(swap_side(send))
    keep, send = call(
        core_kernel, [((LANES + TILE, LANES), F32), ((LANES + TILE + carried, LANES), F32)],
        *keeps, *gots, *zs,
    )
    core_got = swap_core(send)
    y, known = call(join_kernel, [((LANES, rank), F32), ((TILE, rank), F32)], keep, core_got)
    others = [lax.ppermute(known, "cell", [(c, c ^ d) for c in range(groups)]) for d in (1, 2, 3)]
    (z_out,) = call(z_out_kernel, [((width, rank), F32)], *zs, gots[0], core_got, known, plain=True)
    q_out, scale_out = call(
        functools.partial(q_out_kernel, all_cells),
        [((LANES, rank), F32), ((2 * ITERS + 1, rank), F32)],
        y, known, *others, plain=True,
    )
    return q_out, z_out, scale_out


def solution(mesh):
    return jax.shard_map(
        local,
        mesh=mesh,
        in_specs=(P("cell", "snap"), P("snap", None)),
        out_specs=(P(("cell", "snap"), None), P("snap", None), P()),
        check_vma=False,
    )
```
